32 devices in a mesh: dp: 2 (over x), rows: 4 (over z), cols: 4 (over y, core).
Axes of the slice: x: 2, y: 2, z: 4, core: 2. Of those that a mesh axis runs over, the one named last changes fastest.
Arguments:
- block_input: bfloat16 [768, 32768], P('cols', ('dp', 'rows')), may hold values from -6 to 6
- norm_gain_one: float32 [768], P('cols'), may hold values from 0.1 to 1.9
- w_query: bfloat16 [768, 768], P('cols', 'rows'), may hold values from -0.21875 to 0.21875
- w_key: bfloat16 [768, 768], P('cols', 'rows'), may hold values from -0.21875 to 0.21875
- w_value: bfloat16 [768, 768], P('cols', 'rows'), may hold values from -0.21875 to 0.21875
- w_out: bfloat16 [768, 768], P('rows', 'cols'), may hold values from -4 to 4
- norm_gain_two: float32 [768], P('cols'), may hold values from 0.1 to 1.9
- w_up: bfloat16 [768, 3072], P('cols', 'rows'), may hold values from -0.21875 to 0.21875
- w_down: bfloat16 [768, 3072], P('cols', 'rows'), may hold values from -0.15625 to 0.15625
- piece_start: int32 [8, 8], P(('dp', 'cols')), may hold values from 0 to 4032, as said below
- piece_len: int32 [8, 8], P(('dp', 'cols')), may hold values from 64 to 256, as said below
- grad_y: bfloat16 [768, 32768], P('cols', ('dp', 'rows')), may hold values from -6 to 6
Outputs:
- block_output: bfloat16 [768, 32768], P('cols', ('dp', 'rows'))
- grad_x: float32 [768, 32768], P('cols', ('dp', 'rows'))
- grad_gain_one: float32 [768], P('cols')
- grad_query: float32 [768, 768], P('cols', 'rows')
- grad_key: float32 [768, 768], P('cols', 'rows')
- grad_value: float32 [768, 768], P('cols', 'rows')
- grad_out: float32 [768, 768], P('rows', 'cols')
- grad_gain_two: float32 [768], P('cols')
- grad_up: float32 [768, 3072], P('cols', 'rows')
- grad_down: float32 [768, 3072], P('cols', 'rows')
The draws below stay inside these ranges and needn't reach their ends.
Inputs may be any that keep to these rules, and one draw needn't show every extreme that they name: `piece_start`: piece k of a sequence lies inside positions k * 512 to (k + 1) * 512 - 1, so pieces are in order and never meet. `piece_len`: every sequence has a piece of exactly 256 positions.
All inputs are finite; a program needn't handle non-finite values.
Results may differ from the reference program's by a relative error of at most 0.019.
Values may be sent and summed in bfloat16 or wider, within the bound.
No kernel may reach another device: no remote copies, remote signals or barrier semaphores. Data moves between devices by JAX's collectives and lax.ppermute only.
A program may use at most 320 MiB of HBM per device.

```python
import jax
import jax.numpy as jnp
from jax import lax

D = 768
HEADS = 12
HD = 64
FF = 3072
WIN = 1536
PIECE = 256
NPIECE = 8
LEN = 4096
QBLK = 512
SEQS = 8
TOKENS = 32768


def piece_layout(key):
    base_key = jax.random.fold_in(key, 11)
    key_lengths, key_chosen, key_offsets = jax.random.split(base_key, 3)
    slot_size = LEN // NPIECE
    seq_first = (jnp.arange(SEQS) == 0)[:, None]
    piece_index = jnp.arange(NPIECE)[None, :]
    lengths = jax.random.randint(key_lengths, (SEQS, NPIECE), PIECE // 4, PIECE + 1)
    chosen = jax.random.randint(key_chosen, (SEQS, 1), 0, NPIECE)
    chosen = jnp.where(seq_first, 0, chosen)
    lengths = jnp.where(piece_index == chosen, PIECE, lengths)
    last_first = seq_first & (piece_index == NPIECE - 1)
    lengths = jnp.where(last_first, PIECE // 4, lengths)
    room_left = slot_size - lengths + 1
    offsets = jax.random.randint(key_offsets, (SEQS, NPIECE), 0, 1 << 20) % room_left
    offsets = jnp.where(seq_first & (piece_index == 0), 0, offsets)
    offsets = jnp.where(last_first, room_left - 1, offsets)
    starts = piece_index * slot_size + offsets
    return (starts.astype(jnp.int32), lengths.astype(jnp.int32))


def draw_piece_start(key, part):
    return piece_layout(key)[0]


def draw_piece_len(key, part):
    return piece_layout(key)[1]


def level_of(key, shape, cuts, low, top_value):
    level, own = 1.0, jax.random.fold_in(key, 6)
    for position, blocks in cuts:
        draws = jnp.exp(jax.random.uniform(jax.random.fold_in(own, position), (blocks,), jnp.float32, low / len(cuts), top_value / len(cuts)))
        level = level * jnp.repeat(draws, shape[position] // blocks).reshape([-1 if axis == position else 1 for axis in range(len(shape))])
    return level


def bell_draw(stream_key, shape, deviation, bound, cuts=(), held_as=jnp.bfloat16):
    entries = jax.random.normal(stream_key, shape, jnp.float32) * deviation
    if len(cuts) > 0:
        entries = level_of(stream_key, shape, cuts, -0.22, 0.18) * entries
    return jnp.clip(entries, min=-bound, max=bound).astype(held_as)


def setup_inputs(seed: int = 0) -> dict:
    splits = jax.random.split(jax.random.key(seed), 13)
    block_input = bell_draw(splits[0], (D, TOKENS), 1.0, 6.0, ((0, 4), (1, 8)))
    norm_gain_one = jnp.clip(1.0 + 0.18 * jax.random.normal(splits[1], (D,), jnp.float32), 0.1, 1.9)
    w_query = bell_draw(splits[2], (D, D), D ** -0.5, 0.21875, ((0, 4), (1, 4)))
    w_key = bell_draw(splits[3], (D, D), D ** -0.5, 0.21875, ((0, 4), (1, 4)))
    w_value = bell_draw(splits[4], (D, D), D ** -0.5, 0.21875, ((0, 4), (1, 4)))
    w_out = bell_draw(splits[5], (D, D), (max(4 * D // WIN, 1)) ** -0.5, 4.0, ((0, 4), (1, 4)))
    norm_gain_two = jnp.clip(1.0 + 0.18 * jax.random.normal(splits[6], (D,), jnp.float32), 0.1, 1.9)
    w_up = bell_draw(splits[7], (D, FF), D ** -0.5, 0.21875, ((0, 4), (1, 4)))
    w_down = bell_draw(splits[8], (D, FF), (FF // 2) ** -0.5, 0.15625, ((0, 4), (1, 4)))
    piece_start = draw_piece_start(jax.random.fold_in(splits[12], 71), 0)
    piece_len = draw_piece_len(jax.random.fold_in(splits[12], 71), 0)
    grad_y = bell_draw(splits[11], (D, TOKENS), 1.0, 6.0, ((0, 4), (1, 8)))
    return dict(block_input=block_input, norm_gain_one=norm_gain_one, w_query=w_query, w_key=w_key, w_value=w_value, w_out=w_out, norm_gain_two=norm_gain_two, w_up=w_up, w_down=w_down, piece_start=piece_start, piece_len=piece_len, grad_y=grad_y)


EPSILON = 1e-06
MASKED = -1e+30
HIGH = lax.Precision.HIGHEST

@jax.custom_vjp
def low(v):
    return lax.optimization_barrier(v.astype(jnp.bfloat16)).astype(jnp.float32)

@jax.custom_vjp
def low_back(v):
    return v

def low_keep(v):
    return (low(v), None)

def low_pass(kept, grad):
    return (grad,)

def back_keep(v):
    return (v, None)

def back_low(kept, grad):
    return (low(grad),)
low.defvjp(low_keep, low_pass)
low_back.defvjp(back_keep, back_low)

def rounded_both(value):
    return low(low_back(value))

def matmul(left, right):
    return jnp.dot(left, right, precision=HIGH, preferred_element_type=jnp.float32)

def rms_norm(value, gain):
    factor = lax.rsqrt(lax.optimization_barrier(jnp.mean(value * value, axis=-1, keepdims=True)) + EPSILON)
    return value * factor * gain[None, :]

def piece_labels(starts, lengths):
    places = jnp.arange(LEN, dtype=jnp.int32)[:, None]
    inside = (places >= starts[None, :]) & (places < (starts + lengths)[None, :])
    numbers = jnp.arange(1, NPIECE + 1, dtype=jnp.int32)[None, :]
    return lax.optimization_barrier(jnp.sum(jnp.where(inside, numbers, 0), axis=1)).astype(jnp.int32) - 1

def attend_sequence(seq_items):
    queries, key_rows, value_rows, labels = seq_items
    positions = jnp.arange(LEN, dtype=jnp.int32)

    def one_block(block_items):
        query_block, query_pos, query_lab = block_items
        raw_scores = jnp.einsum('qhd,khd->hqk', query_block, key_rows, precision=HIGH, preferred_element_type=jnp.float32) * HD ** (-0.5)
        scores = low_back(raw_scores)
        near = (positions[None, :] <= query_pos[:, None]) & (query_pos[:, None] - positions[None, :] < WIN)
        same = (query_lab[:, None] == labels[None, :]) & (query_lab[:, None] >= 0)
        logits = jnp.where((near | same)[None], scores, MASKED)
        prob_low = low(jax.nn.softmax(logits, axis=-1))
        return jnp.einsum('hqk,khd->qhd', prob_low, value_rows, precision=HIGH, preferred_element_type=jnp.float32)
    block_count = LEN // QBLK
    outputs = lax.map(jax.checkpoint(one_block), (queries.reshape(block_count, QBLK, HEADS, HD), positions.reshape(block_count, QBLK), labels.reshape(block_count, QBLK)))
    return outputs.reshape(LEN, D)

def forward(residual, gain_one, w_query, w_key, w_value, w_out, gain_two, w_up, w_down, labels):
    normed_one = low(rms_norm(residual, gain_one))
    queries = rounded_both(matmul(normed_one, w_query))
    key_rows = rounded_both(matmul(normed_one, w_key))
    value_rows = rounded_both(matmul(normed_one, w_value))
    shape_four = (SEQS, LEN, HEADS, HD)
    attended = lax.map(attend_sequence, (queries.reshape(shape_four), key_rows.reshape(shape_four), value_rows.reshape(shape_four), labels))
    attended = rounded_both(attended.reshape(SEQS * LEN, D))
    middle = residual + low_back(matmul(attended, w_out))
    normed_two = low(rms_norm(middle, gain_two))
    up_value = low_back(matmul(normed_two, w_up))
    gate_act = low(jax.nn.gelu(up_value, approximate=True))
    return middle + low_back(matmul(gate_act, w_down.T))

def reference(block_input, norm_gain_one, w_query, w_key, w_value, w_out, norm_gain_two, w_up, w_down, piece_start, piece_len, grad_y):
    labels = jax.vmap(piece_labels)(piece_start, piece_len)
    floats = tuple((item.astype(jnp.float32) for item in (block_input, norm_gain_one, w_query, w_key, w_value, w_out, norm_gain_two, w_up, w_down)))
    floats = (floats[0].T,) + floats[1:]

    def closed(*items):
        return forward(*items, labels)
    output, pull = jax.vjp(closed, *floats)
    grads = pull(grad_y.astype(jnp.float32).T)
    return (output.T.astype(jnp.bfloat16), grads[0].T, grads[1], grads[2], grads[3], grads[4], grads[5], grads[6], grads[7], grads[8])
```

```python
import functools
import math

import jax
import jax.numpy as jnp
from jax import lax
from jax.experimental import pallas as pl
from jax.experimental.pallas import tpu as pltpu
from jax.sharding import PartitionSpec as P


D = 768
HD = 64
LEN = 4096
HALF = 2048
B = 512
FB = 192
FF = 3072
PACK = 1792
EPSILON = 1e-06
MASKED = -1e30
SCALE = HD**-0.5
LOG2E = math.log2(math.e)
BF = jnp.bfloat16
F32 = jnp.float32
MIB = 1 << 20


def contract(left, right, dims):
    return lax.dot_general(left, right, (dims, ((), ())), preferred_element_type=F32)


def nn(left, right):
    return contract(left, right, ((1,), (0,)))


def nt(left, right):
    return contract(left, right, ((1,), (1,)))


def cols_swap(value, distance):
    return lax.ppermute(value, "cols", [(i, i ^ distance) for i in range(lax.axis_size("cols"))])


def rows_shift(value, step):
    count = lax.axis_size("rows")
    return lax.ppermute(value, "rows", [(i, (i + step) % count) for i in range(count)])


def dp_swap(value):
    return lax.ppermute(value, "dp", [(i, i ^ 1) for i in range(lax.axis_size("dp"))])


def qkv_kernel(tab, x0, x1, x23, gain, w, *refs):
    normed, scale, q_t, k, k_t, v, v_t = refs[-7:]
    i = pl.program_id(0)
    x = jnp.concatenate([x0[...], x1[...], x23[...]], axis=0).astype(F32)
    r1 = lax.rsqrt(jnp.sum(x * x, axis=0, keepdims=True) * (1.0 / D) + EPSILON)
    n_t = (x * r1 * gain[...]).astype(BF)
    normed[...] = n_t
    scale[...] = r1
    n = n_t.T
    k_val = nn(n, w[:, 384:768])
    k[...] = k_val.astype(BF)
    k_t[...] = k_val.T.astype(BF)
    v_val = nn(n, w[:, 768:1152])
    v[...] = v_val.astype(BF)
    v_t[...] = v_val.T.astype(BF)

    @pl.when(i < 2)
    def _():
        q_t[...] = (nn(n, w[:, 0:384]) * (SCALE * LOG2E)).T.astype(BF)


def project_half(order, x0, x1, x23, gain, w, half, old):
    base = half * (HALF // B)

    def cols_of(rows):
        return pl.BlockSpec((rows, B), lambda i, t: (0, t[i]))

    whole = lambda shape: pl.BlockSpec(shape, lambda i, t: (0, 0))
    major = pl.BlockSpec((B, 384), lambda i, t: (base + t[i], 0))
    minor = pl.BlockSpec((384, B), lambda i, t: (0, base + t[i]))
    kv = [jax.ShapeDtypeStruct(s, BF) for s in ((LEN, 384), (384, LEN)) * 2]
    return pl.pallas_call(
        qkv_kernel,
        grid_spec=pltpu.PrefetchScalarGridSpec(
            num_scalar_prefetch=1,
            grid=(HALF // B,),
            in_specs=[cols_of(FB), cols_of(FB), cols_of(2 * FB), whole((D, 1)), whole((D, 1152))]
            + [pl.BlockSpec(memory_space=pl.ANY)] * len(old),
            out_specs=[
                cols_of(D),
                cols_of(1),
                pl.BlockSpec((384, B), lambda i, t: (0, jnp.minimum(i, 1))),
                major,
                minor,
                major,
                minor,
            ],
        ),
        out_shape=[
            jax.ShapeDtypeStruct((D, HALF), BF),
            jax.ShapeDtypeStruct((1, HALF), F32),
            jax.ShapeDtypeStruct((384, HALF // 2), BF),
        ]
        + kv,
        input_output_aliases={6 + n: 3 + n for n in range(len(old))},
        compiler_params=pltpu.CompilerParams(vmem_limit_bytes=48 * MIB),
        cost_estimate=pl.CostEstimate(flops=6_000_000_000, bytes_accessed=20_000_000, transcendentals=0),
    )(order, x0, x1, x23, gain, w, *old)


def block_masks(first, last):
    key = lax.broadcasted_iota(jnp.int32, (B, B), 0)
    query = lax.broadcasted_iota(jnp.int32, (B, B), 1)
    piece = (key >= first) & (key < last) & (query >= first) & (query < last)
    return (key > query, (key <= query) | piece)


def masked(scores, masks, step, count):
    if step == count - 1:
        scores = jnp.where(masks[1], scores, MASKED)
    if count == 4 and step == 0:
        scores = jnp.where(masks[0], scores, MASKED)
    return scores


def head_rows(pair_t):
    row = lax.broadcasted_iota(jnp.int32, pair_t.shape, 0)
    zero = jnp.zeros((), pair_t.dtype)
    return [jnp.where((row // HD) == h, pair_t, zero) for h in range(2)]


def head_cols(pair):
    col = lax.broadcasted_iota(jnp.int32, pair.shape, 1)
    zero = jnp.zeros((), pair.dtype)
    return [jnp.where((col // HD) == h, pair, zero) for h in range(2)]


def for_counts(block, counts, body):
    if len(counts) == 1:
        body(counts[0])
        return
    visible = jnp.minimum(block, 3) + 1
    for count in counts:
        pl.when(visible == count)(functools.partial(body, count))


def attend_kernel(tab, q_t, k, v_t, o_t, log_total, *, counts):
    i = pl.program_id(1)
    block, first, last = tab[i], tab[2 + i], tab[4 + i]

    def body(count):
        masks = block_masks(first, last)
        starts = [pl.multiple_of((block - (count - 1) + t) * B, B) for t in range(count)]
        for h, q_head in enumerate(head_rows(q_t[...])):
            scores = [masked(nn(k[pl.ds(s, B), :], q_head), masks, t, count) for t, s in enumerate(starts)]
            peak = functools.reduce(jnp.maximum, [jnp.max(s, axis=0, keepdims=True) for s in scores])
            total, mixed = 0.0, 0.0
            for score, s in zip(scores, starts):
                part = jnp.exp2(score - peak)
                total = total + jnp.sum(part, axis=0, keepdims=True)
                mixed = mixed + nn(v_t[h * HD : (h + 1) * HD, pl.ds(s, B)], part.astype(BF))
            o_t[h * HD : (h + 1) * HD, :] = (mixed * (1.0 / total)).astype(BF)
            log_total[0, h : h + 1, :] = peak + jnp.log2(total)

    for_counts(block, counts, body)


def attend_specs(span):
    return (
        pl.BlockSpec((128, B), lambda p, i, t: (p, i)),
        pl.BlockSpec((1, 2, B), lambda p, i, t: (p, 0, i)),
        pl.BlockSpec((span, 128), lambda p, i, t: (0, p)),
        pl.BlockSpec((128, span), lambda p, i, t: (p, 0)),
    )


def attend_half(tab, q_t, k, v_t, half):
    query, stat, major, minor = attend_specs(LEN if half else HALF)
    units = 8 if half else 5
    return pl.pallas_call(
        functools.partial(attend_kernel, counts=(4,) if half else (1, 2, 3, 4)),
        grid_spec=pltpu.PrefetchScalarGridSpec(
            num_scalar_prefetch=1,
            grid=(3, 2),
            in_specs=[query, major, minor],
            out_specs=[query, stat],
        ),
        out_shape=[jax.ShapeDtypeStruct(q_t.shape, BF), jax.ShapeDtypeStruct((3, 2, 2 * B), F32)],
        compiler_params=pltpu.CompilerParams(vmem_limit_bytes=48 * MIB),
        cost_estimate=pl.CostEstimate(
            flops=units * 6 * 2 * 512 * B * B, bytes_accessed=10_000_000, transcendentals=units * 6 * B * B
        ),
    )(tab, q_t, k, v_t)


def attend_back_kernel(tab, q_t, do_t, o_t, log_total, k, v, k_t, *refs, counts, half):
    if half:
        dq_t, dk_high, dv_high, dk_low, dv_low, dk, dv = refs
    else:
        dk_start, dv_start, dq_t, dk_out, dv_out, dk, dv = refs
    i = pl.program_id(1)
    block, first, last = tab[i], tab[2 + i], tab[4 + i]

    @pl.when(i == 0)
    def _():
        dk[...] = jnp.zeros_like(dk) if half else dk_start[...]
        dv[...] = jnp.zeros_like(dv) if half else dv_start[...]

    def body(count):
        masks = block_masks(first, last)
        queries, grads = q_t[...], do_t[...]
        q_rows, g_rows = head_rows(queries), head_rows(grads)
        q_cols, g_cols = head_cols(queries.T), head_cols(grads.T)
        product = grads.astype(F32) * o_t[...].astype(F32)
        inner = [jnp.sum(product[h * HD : (h + 1) * HD], axis=0, keepdims=True) for h in range(2)]
        dq = [0.0, 0.0]
        for t in range(count):
            rows = pl.ds(pl.multiple_of((block - (count - 1) + t) * B, B), B)
            key_rows, value_rows = k[rows, :], v[rows, :]
            dk_part = dv_part = 0.0
            for h in range(2):
                score = masked(nn(key_rows, q_rows[h]), masks, t, count)
                probs = jnp.exp2(score - log_total[0, h : h + 1, :])
                grad_probs = nn(value_rows, g_rows[h])
                grad_scores = (probs * (grad_probs - inner[h])).astype(BF)
                dv_part = dv_part + nn(probs.astype(BF), g_cols[h])
                dk_part = dk_part + nn(grad_scores, q_cols[h])
                dq[h] = dq[h] + nn(k_t[h * HD : (h + 1) * HD, rows], grad_scores)
            dv[rows, :] += dv_part
            dk[rows, :] += dk_part
        for h in range(2):
            dq_t[h * HD : (h + 1) * HD, :] = (dq[h] * SCALE).astype(BF)

    for_counts(block, counts, body)

    @pl.when(i == 1)
    def _():
        unscale = 1.0 / LOG2E
        if half:
            dk_high[...] = (dk[HALF:, :] * unscale).astype(BF)
            dv_high[...] = dv[HALF:, :].astype(BF)
            dk_low[...] = dk[:HALF, :]
            dv_low[...] = dv[:HALF, :]
        else:
            dk_out[...] = (dk[...] * unscale).astype(BF)
            dv_out[...] = dv[...].astype(BF)


def attend_back_half(tab, q_t, do_t, o_t, log_total, k, v, k_t, half, start):
    span = LEN if half else HALF
    query, stat, major, minor = attend_specs(span)
    grad = pl.BlockSpec((HALF, 128), lambda p, i, t: (0, p))
    low = jax.ShapeDtypeStruct((HALF, 384), BF)
    wide = jax.ShapeDtypeStruct((HALF, 384), F32)
    units = 8 if half else 5
    return pl.pallas_call(
        functools.partial(attend_back_kernel, counts=(4,) if half else (1, 2, 3, 4), half=half),
        grid_spec=pltpu.PrefetchScalarGridSpec(
            num_scalar_prefetch=1,
            grid=(3, 2),
            in_specs=[query, query, query, stat, major, major, minor] + [grad] * len(start),
            out_specs=[query] + [grad] * (4 if half else 2),
            scratch_shapes=[pltpu.VMEM((span, 128), F32)] * 2,
        ),
        out_shape=[jax.ShapeDtypeStruct(q_t.shape, BF), low, low] + ([wide, wide] if half else []),
        compiler_params=pltpu.CompilerParams(vmem_limit_bytes=56 * MIB),
        cost_estimate=pl.CostEstimate(
            flops=units * 6 * 5 * 512 * B * B, bytes_accessed=20_000_000, transcendentals=units * 6 * B * B
        ),
    )(tab, q_t, do_t, o_t, log_total, k, v, k_t, *start)


def feed_kernel(sel, x_t, a_t, dy_t, wo_t, gain, *refs):
    pieces = refs[:16]
    out_t, gm_t, ga_t, gain_sum, g_near, g_far = refs[16:22]
    w_up, w_down, n_t, n, dy, mid, mlp, gn, stage, stage_out, in_sems, out_sems = refs[22:]
    parity, core = sel[0], sel[1]

    def loads(slot):
        copies = []
        for rel in range(4):
            place = rel if slot == 0 else (rel // 2) * 2 + lax.rem(parity + rel, 2)
            rows = pl.ds(place * FB, FB) if slot == 0 else pl.ds(pl.multiple_of(place * FB, FB), FB)
            for which, target in enumerate((w_up, w_down)):
                copies.append(
                    pltpu.make_async_copy(
                        pieces[slot * 4 + rel].at[:, which * D : (which + 1) * D],
                        target.at[slot, rows, :],
                        in_sems.at[slot, rel * 2 + which],
                    )
                )
        return copies

    for slot in range(4):
        for copy in loads(slot):
            copy.start()

    mid[...] = x_t[...].astype(F32) + nn(wo_t[...], a_t[...])
    r2 = lax.rsqrt(jnp.sum(mid[...] * mid[...], axis=0, keepdims=True) * (1.0 / D) + EPSILON)
    n_t[...] = (mid[...] * r2 * gain[...]).astype(BF)
    n[...] = n_t[...].T
    dy[...] = dy_t[...].T
    mlp[...] = mid[...]
    gn[...] = jnp.zeros_like(gn)
    for slot in range(4):
        for copy in loads(slot):
            copy.wait()

    def stores(slot, buffer):
        copies = []
        for side, target in enumerate((g_near, g_far)):
            for which in range(2):
                copies.append(
                    pltpu.make_async_copy(
                        stage.at[buffer, which, pl.ds(side * 384, 384), :],
                        target.at[slot, :, which * D : (which + 1) * D],
                        out_sems.at[buffer, side * 2 + which],
                    )
                )
        return copies

    root = math.sqrt(2.0 / math.pi)

    def chunk(slot, carry):
        buffer = lax.rem(slot, 2)

        @pl.when(slot >= 2)
        def _():
            for copy in stores(slot - 2, buffer):
                copy.wait()

        up = nn(n[...], w_up[slot])
        square = up * up
        half = 0.5 + 0.5 * jnp.tanh(up * (root + (root * 0.044715) * square))
        act = (up * half).astype(BF)
        slope = half + (2.0 * up) * (half - half * half) * (root + (3.0 * root * 0.044715) * square)
        stage[buffer, 1] = nn(dy_t[...], act).astype(BF)
        mlp[...] += nt(w_down[slot], act)
        grad_up = (nn(dy[...], w_down[slot]) * slope).astype(BF)
        stage[buffer, 0] = nn(n_t[...], grad_up).astype(BF)
        gn[...] += nt(w_up[slot], grad_up)
        for copy in stores(slot, buffer):
            copy.start()
        return carry

    lax.fori_loop(0, 4, chunk, 0)
    out_t[...] = mlp[...].astype(BF)
    weighted = gn[...] * gain[...]
    inner = jnp.sum(mid[...] * weighted, axis=0, keepdims=True)
    cubed = r2 * r2 * r2 * inner * (1.0 / D)
    gm_t[...] = (dy_t[...].astype(F32) + r2 * weighted - mid[...] * cubed).astype(BF)
    gain_sum[...] = jnp.sum(gn[...] * mid[...] * r2, axis=1, keepdims=True)
    ga_t[...] = contract(wo_t[...], gm_t[...], ((0,), (0,))).astype(BF)
    copies = []
    for slot in range(4):
        place = lax.rem(slot + 2 * core, 4)
        part = nt(gm_t[...], a_t[pl.ds(pl.multiple_of(place * FB, FB), FB), :])
        stage_out[slot] = jnp.concatenate([part, jnp.zeros((D, PACK - 2 * D - FB), F32)], axis=1).astype(BF)
        for side, target in enumerate((g_near, g_far)):
            copies.append(
                pltpu.make_async_copy(
                    stage_out.at[slot, pl.ds(side * 384, 384), :],
                    target.at[slot, :, 2 * D : PACK],
                    out_sems.at[2 + side, slot],
                )
            )
            copies[-1].start()
    for slot in (2, 3):
        for copy in stores(slot, slot % 2):
            copy.wait()
    for copy in copies:
        copy.wait()


def feed_forward(sel, x_t, a_t, dy_t, wo_t, gain, pieces):
    count = x_t.shape[1]
    vmem = pl.BlockSpec(memory_space=pltpu.VMEM)
    hbm = pl.BlockSpec(memory_space=pl.ANY)
    token = jax.ShapeDtypeStruct((D, count), BF)
    grads = jax.ShapeDtypeStruct((4, 384, PACK), BF)
    return pl.pallas_call(
        feed_kernel,
        in_specs=[pl.BlockSpec(memory_space=pltpu.SMEM)] + [vmem] * 5 + [hbm] * 16,
        out_specs=[vmem] * 4 + [hbm] * 2,
        out_shape=[token, token, token, jax.ShapeDtypeStruct((D, 1), F32), grads, grads],
        scratch_shapes=[
            pltpu.VMEM((4, D, D), BF),
            pltpu.VMEM((4, D, D), BF),
            pltpu.VMEM((D, count), BF),
            pltpu.VMEM((count, D), BF),
            pltpu.VMEM((count, D), BF),
            pltpu.VMEM((D, count), F32),
            pltpu.VMEM((D, count), F32),
            pltpu.VMEM((D, count), F32),
            pltpu.VMEM((2, 2, D, D), BF),
            pltpu.VMEM((4, D, PACK - 2 * D), BF),
            pltpu.SemaphoreType.DMA((4, 8)),
            pltpu.SemaphoreType.DMA((4, 4)),
        ],
        compiler_params=pltpu.CompilerParams(vmem_limit_bytes=62 * MIB),
        cost_estimate=pl.CostEstimate(
            flops=6 * count * (2 * D * FF + D * D), bytes_accessed=34_000_000, transcendentals=count * FF
        ),
    )(sel, x_t, a_t, dy_t, wo_t, gain, *pieces)


def qkv_back_kernel(tab, w, n_t, dq_t, dk, dv, *refs):
    start, (near, far, inner, gain_out, grad_w, acc, gain_acc) = refs[:-7], refs[-7:]
    i = pl.program_id(0)

    @pl.when(i == 0)
    def _():
        acc[...] = start[0][...] if start else jnp.zeros_like(acc)
        gain_acc[...] = start[1][...] if start else jnp.zeros_like(gain_acc)

    normed = n_t[...]
    acc[:, 384:768] += nn(normed, dk[...])
    acc[:, 768:1152] += nn(normed, dv[...])

    def finish(grad):
        near[...] = grad[:384].astype(BF)
        far[...] = grad[384:].astype(BF)
        product = grad * normed.astype(F32)
        inner[...] = jnp.sum(product, axis=0, keepdims=True)
        gain_acc[...] += jnp.sum(product, axis=1, keepdims=True)

    def key_part():
        return nt(w[:, 384:768], dk[...]) + nt(w[:, 768:1152], dv[...])

    @pl.when(i < 2)
    def _():
        acc[:, 0:384] += nt(normed, dq_t[...])
        finish(key_part() + nn(w[:, 0:384], dq_t[...]))

    @pl.when(i >= 2)
    def _():
        finish(key_part())

    @pl.when(i == pl.num_programs(0) - 1)
    def _():
        grad_w[...] = acc[...].astype(grad_w.dtype)
        gain_out[...] = gain_acc[...]


def project_back_half(order, w, n_t, dq_t, dk, dv, start):
    whole = lambda shape: pl.BlockSpec(shape, lambda i, t: (0, 0))

    def cols_of(rows):
        return pl.BlockSpec((rows, B), lambda i, t: (0, t[i]))

    major = pl.BlockSpec((B, 384), lambda i, t: (t[i], 0))
    low = jax.ShapeDtypeStruct((384, HALF), BF)
    return pl.pallas_call(
        qkv_back_kernel,
        grid_spec=pltpu.PrefetchScalarGridSpec(
            num_scalar_prefetch=1,
            grid=(HALF // B,),
            in_specs=[
                whole((D, 1152)),
                cols_of(D),
                pl.BlockSpec((384, B), lambda i, t: (0, jnp.minimum(i, 1))),
                major,
                major,
            ]
            + [whole((D, 1152)), whole((D, 1))][: len(start)],
            out_specs=[cols_of(384), cols_of(384), cols_of(1), whole((D, 1)), whole((D, 1152))],
            scratch_shapes=[pltpu.VMEM((D, 1152), F32), pltpu.VMEM((D, 1), F32)],
        ),
        out_shape=[
            low,
            low,
            jax.ShapeDtypeStruct((1, HALF), F32),
            jax.ShapeDtypeStruct((D, 1), F32),
            jax.ShapeDtypeStruct((D, 1152), BF if start else F32),
        ],
        compiler_params=pltpu.CompilerParams(vmem_limit_bytes=56 * MIB),
        cost_estimate=pl.CostEstimate(flops=12_000_000_000, bytes_accessed=20_000_000, transcendentals=0),
    )(order, w, n_t, dq_t, dk, dv, *start)


def per_device(
    block_input,
    norm_gain_one,
    w_query,
    w_key,
    w_value,
    w_out,
    norm_gain_two,
    w_up,
    w_down,
    piece_start,
    piece_len,
    grad_y,
):
    c = lax.axis_index("cols")
    r = lax.axis_index("rows")
    y, core = c // 2, c % 2
    parity = lax.axis_index("dp") % 2

    def by_pair(zero, one):
        return jnp.where(y == 0, jnp.array(zero, jnp.int32), jnp.array(one, jnp.int32))

    low_order = by_pair([0, 3, 1, 2], [1, 2, 0, 3])
    high_order = by_pair([0, 1, 2, 3], [2, 3, 0, 1])

    def take(array, block):
        return lax.dynamic_slice_in_dim(array, block * B, B, 1)

    small = jnp.concatenate(
        [norm_gain_one, norm_gain_two, piece_start[0].astype(F32), piece_len[0].astype(F32)]
    )
    small = jnp.stack([small, cols_swap(small, 2)])
    small = jnp.concatenate([small, cols_swap(small, 1)])
    gain_one = small[:, :FB].reshape(D, 1)
    gain_two = small[:, FB : 2 * FB].reshape(D, 1)
    apart = jnp.bitwise_xor(c, r)
    mine = jnp.where(apart == 0, 0, jnp.where(apart == 2, 1, jnp.where(apart == 1, 2, 3)))
    pieces = lax.dynamic_index_in_dim(small, mine, 0, keepdims=False)[2 * FB :].astype(jnp.int32)
    firsts = pieces[:8] - jnp.arange(8, dtype=jnp.int32) * B
    lasts = firsts + pieces[8:]

    def table(order, half):
        blocks = order[:2] + half * 4
        return jnp.concatenate([blocks, firsts[blocks], lasts[blocks]])

    tables = (table(low_order, 0), table(high_order, 1))
    orders = (low_order, high_order)

    def gather_half(half):
        own = block_input[:, half * HALF : (half + 1) * HALF]
        pair = cols_swap(own, 2)
        return own, pair, cols_swap(jnp.concatenate([own, pair]), 1)

    x_low = gather_half(0)

    ring = [jnp.concatenate([w_query, w_key, w_value], axis=1)]
    for _ in range(3):
        ring.append(rows_shift(ring[-1], 1))
    ring = jnp.stack(ring)
    ring = jnp.stack([ring, cols_swap(ring, 2)], axis=1)
    kept = lax.dynamic_slice_in_dim(ring, 2 * core, 2, 0)
    sent = lax.dynamic_slice_in_dim(ring, 2 - 2 * core, 2, 0)
    w_all = jnp.concatenate([kept, cols_swap(sent, 1)], axis=1)
    w_qkv = w_all.reshape(2, D, 3, FB).transpose(1, 2, 0, 3).reshape(D, 1152)

    x_high = gather_half(1)

    def blocks_of(which):
        low = jnp.where(which == 0, jnp.array([0, 3], jnp.int32), jnp.array([1, 2], jnp.int32))
        high = jnp.where(which == 0, jnp.array([4, 5], jnp.int32), jnp.array([6, 7], jnp.int32))
        return low, high

    def tokens_of(which, device):
        low, high = blocks_of(which)
        return jnp.concatenate([take(grad_y, low[device]), take(grad_y, high[device])], axis=1)

    own_core, other_core = tokens_of(y, core), tokens_of(y, 1 - core)
    away = jnp.stack([tokens_of(1 - y, core), tokens_of(1 - y, 1 - core)])
    arrived = cols_swap(away, 2)
    dy_far = cols_swap(jnp.concatenate([other_core, arrived[1]]), 1)
    dy_t = jnp.concatenate([own_core, arrived[0], dy_far])

    pad = jnp.zeros((FB, PACK - 2 * D - FB), BF)
    own_pack = jnp.concatenate([w_up, w_down, w_out.T, pad], axis=1)
    pair_pack = cols_swap(own_pack, 2)
    feed = [own_pack, pair_pack, cols_swap(own_pack, 1), cols_swap(pair_pack, 1)]
    moving = jnp.where(parity == 0, own_pack, pair_pack)
    for _ in range(3):
        moving = rows_shift(moving, 1)
        crossed = dp_swap(moving)
        feed += [moving, crossed, cols_swap(moving, 1), cols_swap(crossed, 1)]
    out_rows = []
    for slot in range(4):
        parts = [piece[:, 2 * D : 2 * D + FB] for piece in feed[slot * 4 : slot * 4 + 4]]
        if slot:
            even = parity == 0
            parts = [
                jnp.where(even, parts[0], parts[1]),
                jnp.where(even, parts[1], parts[0]),
                jnp.where(even, parts[2], parts[3]),
                jnp.where(even, parts[3], parts[2]),
            ]
        out_rows.append(jnp.concatenate(parts))
    wo_t = jnp.stack(out_rows)
    wo_t = jnp.concatenate([lax.dynamic_slice_in_dim(wo_t, 2 * core, 2, 0), lax.dynamic_slice_in_dim(wo_t, 2 - 2 * core, 2, 0)])
    wo_t = wo_t.transpose(1, 0, 2).reshape(D, D)

    normed_low, scale_low, q_low, *kv = project_half(low_order, *x_low, gain_one, w_qkv, 0, ())
    o_low, log_low = attend_half(tables[0], q_low, kv[0], kv[3], 0)
    *kv, o_low, log_low = lax.optimization_barrier((*kv, o_low, log_low))
    normed_high, scale_high, q_high, *kv = project_half(high_order, *x_high, gain_one, w_qkv, 1, tuple(kv))
    k, k_t, v, v_t = kv
    o_high, log_high = attend_half(tables[1], q_high, k, v_t, 1)

    def core_block(array, which):
        return lax.dynamic_slice_in_dim(array, which * B, B, 1)

    def both(low, high, which):
        return jnp.concatenate([core_block(low, which), core_block(high, which)], axis=1)

    a_t = jnp.concatenate([both(o_low, o_high, core), cols_swap(both(o_low, o_high, 1 - core), 1)])
    x_own = jnp.concatenate(
        [
            jnp.concatenate([take(piece, order[core]) for piece in halves])
            for order, halves in ((low_order, x_low), (high_order, x_high))
        ],
        axis=1,
    )
    sel = jnp.stack([parity, core])
    out_t, gm_t, ga_t, gain_two_sum, g_near, g_far = feed_forward(sel, x_own, a_t, dy_t, wo_t, gain_two, feed)

    ga_far = cols_swap(ga_t[384:], 1)
    ga_own = ga_t[:384]

    def tokens(half):
        own, other = core_block(ga_own, half), core_block(ga_far, half)
        first = jnp.where(core == 0, own, other)
        second = jnp.where(core == 0, other, own)
        return jnp.concatenate([first, second], axis=1)

    dq_high, dk_high, dv_high, dk_low, dv_low = attend_back_half(
        tables[1], q_high, tokens(1), o_high, log_high, k, v, k_t, 1, ()
    )
    near_high, far_high, inner_high, gain_part, w_part = project_back_half(
        high_order, w_qkv, normed_high, dq_high, dk_high, dv_high, ()
    )
    dq_low, dk_low, dv_low = attend_back_half(
        tables[0], q_low, tokens(0), o_low, log_low, k, v, k_t, 0, (dk_low, dv_low)
    )
    near_low, far_low, inner_low, gain_part, w_part = project_back_half(
        low_order, w_qkv, normed_low, dq_low, dk_low, dv_low, (w_part, gain_part)
    )

    both_t = jnp.stack([out_t, gm_t])
    rows_near, rows_far = both_t[:, :384], cols_swap(both_t[:, 384:], 1)
    here = [rows_near[:, :FB], rows_far[:, :FB]]
    there = cols_swap(jnp.concatenate([rows_near[:, FB:], rows_far[:, FB:]]), 2)
    there = [there[:2], there[2:]]

    def block_at(pair, device, half):
        parts = [part[:, :, half * B : (half + 1) * B] for part in here + there]
        same = device == core
        return jnp.where(
            pair == y, jnp.where(same, parts[0], parts[1]), jnp.where(same, parts[2], parts[3])
        )

    places = ((0, 0, 0), (1, 0, 0), (1, 1, 0), (0, 1, 0), (0, 0, 1), (0, 1, 1), (1, 0, 1), (1, 1, 1))
    joined = jnp.concatenate([block_at(*place) for place in places], axis=2)
    output, grad_middle = joined[0], joined[1]

    def grad_half(near, far, inner, scale, half):
        total = near.astype(F32) + cols_swap(far, 1).astype(F32)
        own = total[:FB] + cols_swap(total[FB:].astype(BF), 2).astype(F32)
        inner = inner + cols_swap(inner, 1)
        inner = inner + cols_swap(inner, 2)
        x = block_input[:, half * HALF : (half + 1) * HALF].astype(F32)
        gm = grad_middle[:, half * HALF : (half + 1) * HALF].astype(F32)
        return gm + scale * norm_gain_one[:, None] * own - x * (scale * scale * inner * (1.0 / D))

    grad_high = grad_half(near_high, far_high, inner_high, scale_high, 1)
    grad_low = grad_half(near_low, far_low, inner_low, scale_low, 0)
    grad_x = jnp.concatenate([grad_low, grad_high], axis=1)

    gains = jnp.stack([gain_part[:, 0] / gain_one[:, 0], gain_two_sum[:, 0]])
    gains = lax.psum(gains, ("dp", "rows")).reshape(2, 4, FB)
    gains = gains[:, :2] + cols_swap(gains[:, 2:], 1)
    gains = gains[:, 0] + cols_swap(gains[:, 1], 2)

    def dp_sum(part):
        if lax.axis_size("dp") == 2:
            return part.astype(F32) + dp_swap(part).astype(F32)
        return lax.psum(part.astype(F32), "dp")

    def ring_sum(parts):
        total = parts[3]
        for slot in (2, 1, 0):
            total = (rows_shift(total, -1).astype(F32) + parts[slot].astype(F32)).astype(BF)
        return total

    near = g_near.astype(F32) + cols_swap(g_far, 1).astype(F32)
    even = parity == 0
    keep = jnp.where(even, near[:, :FB], near[:, FB:])
    give = jnp.where(even, near[:, FB:], near[:, :FB]).astype(BF)
    keep = (keep + dp_swap(give).astype(F32)).astype(BF)
    total = ring_sum([keep[slot] for slot in range(4)])
    total = dp_sum(jnp.where(even, total, cols_swap(total, 2)))
    grad_up, grad_down, grad_out = total[:, :D], total[:, D : 2 * D], total[:, 2 * D : 2 * D + FB].T

    w_near, w_far = w_part[:384], cols_swap(w_part[384:], 1)
    first, second = jnp.where(core == 0, w_near, w_far), jnp.where(core == 0, w_far, w_near)
    stacked = jnp.stack([first, second]).reshape(2, 2, FB, 3, 2, FB).transpose(1, 0, 4, 2, 3, 5)
    stacked = stacked.reshape(2, 4, FB, 3 * FB)
    stacked = (stacked[0].astype(F32) + cols_swap(stacked[1], 2).astype(F32)).astype(BF)
    joined_grad = dp_sum(ring_sum([stacked[slot] for slot in range(4)]))
    return (
        output,
        grad_x,
        gains[0],
        joined_grad[:, :FB],
        joined_grad[:, FB : 2 * FB],
        joined_grad[:, 2 * FB :],
        grad_out,
        gains[1],
        grad_up,
        grad_down,
    )


def solution(mesh):
    return jax.shard_map(
        per_device,
        mesh=mesh,
        in_specs=(
            P("cols", ("dp", "rows")),
            P("cols"),
            P("cols", "rows"),
            P("cols", "rows"),
            P("cols", "rows"),
            P("rows", "cols"),
            P("cols"),
            P("cols", "rows"),
            P("cols", "rows"),
            P(("dp", "cols"), None),
            P(("dp", "cols"), None),
            P("cols", ("dp", "rows")),
        ),
        out_specs=(
            P("cols", ("dp", "rows")),
            P("cols", ("dp", "rows")),
            P("cols"),
            P("cols", "rows"),
            P("cols", "rows"),
            P("cols", "rows"),
            P("rows", "cols"),
            P("cols"),
            P("cols", "rows"),
            P("cols", "rows"),
        ),
        check_vma=False,
    )
```

```python
import functools
import math

import jax
import jax.numpy as jnp
from jax import lax
from jax.experimental import pallas as pl
from jax.experimental.pallas import tpu as pltpu
from jax.sharding import PartitionSpec as P


D = 768
HD = 64
LEN = 4096
HALF = 2048
B = 512
FB = 192
FF = 3072
EPSILON = 1e-06
MASKED = -1e30
SCALE = HD**-0.5
LOG2E = math.log2(math.e)
BF = jnp.bfloat16
F32 = jnp.float32
MIB = 1 << 20


def cost(us):
    return pl.CostEstimate(flops=int(us * 1_150_000_000), bytes_accessed=0, transcendentals=0)


def contract(left, right, dims):
    return lax.dot_general(left, right, (dims, ((), ())), preferred_element_type=F32)


def nn(left, right):
    return contract(left, right, ((1,), (0,)))


def nt(left, right):
    return contract(left, right, ((1,), (1,)))


def cols_swap(value, distance):
    return lax.ppermute(value, "cols", [(i, i ^ distance) for i in range(lax.axis_size("cols"))])


def rows_shift(value, step):
    count = lax.axis_size("rows")
    return lax.ppermute(value, "rows", [(i, (i + step) % count) for i in range(count)])


def dp_swap(value):
    return lax.ppermute(value, "dp", [(i, i ^ 1) for i in range(lax.axis_size("dp"))])


ANY = pl.BlockSpec(memory_space=pl.ANY)


def hold_kernel(tab, source, *refs):
    refs[-1][0] = source[...]


def hold(blocks, source, width, *deps):
    count = blocks.shape[0]
    return pl.pallas_call(
        hold_kernel,
        grid_spec=pltpu.PrefetchScalarGridSpec(
            num_scalar_prefetch=1,
            grid=(count,),
            in_specs=[pl.BlockSpec((FB, width), lambda i, t: (0, t[i]))] + [ANY] * len(deps),
            out_specs=pl.BlockSpec((1, FB, width), lambda i, t: (i // 2, 0, i % 2)),
        ),
        out_shape=jax.ShapeDtypeStruct((count // 2, FB, 2 * width), source.dtype),
        cost_estimate=cost(3),
    )(blocks, source, *deps)


def join_kernel(first, second, *refs):
    refs[-1][:, :D] = first[...]
    refs[-1][:, D:] = second[...]


def join(first, second, *deps):
    vmem = pl.BlockSpec(memory_space=pltpu.VMEM)
    return pl.pallas_call(
        join_kernel,
        in_specs=[vmem, vmem] + [ANY] * len(deps),
        out_specs=vmem,
        out_shape=jax.ShapeDtypeStruct((FB, 2 * D), BF),
        cost_estimate=cost(2),
    )(first, second, *deps)


def tie(value, *deps):
    return pl.pallas_call(
        lambda *refs: None,
        in_specs=[ANY] * (1 + len(deps)),
        out_specs=ANY,
        out_shape=jax.ShapeDtypeStruct(value.shape, value.dtype),
        input_output_aliases={0: 0},
        cost_estimate=cost(0),
    )(value, *deps)


def qkv_kernel(tab, *refs, first, extra):
    x0, x1, x23, gain = refs[:4]
    normed, scale, q_t, k, k_t, v, v_t = refs[4 + extra : 11 + extra]
    i = pl.program_id(0)
    if first:
        w = refs[11 + extra]

        @pl.when(i == 0)
        def _():
            w[0:FB, :] = refs[4][0]
            w[FB : 2 * FB, :] = refs[5][0]
            w[2 * FB : 3 * FB, :] = refs[6][0]
            w[3 * FB :, :] = refs[6][1]
    else:
        w = refs[4]
    x = jnp.concatenate([x0[...], x1[...], x23[0], x23[1]], axis=0).astype(F32)
    r1 = lax.rsqrt(jnp.sum(x * x, axis=0, keepdims=True) * (1.0 / D) + EPSILON)
    n_t = (x * r1 * gain[...]).astype(BF)
    normed[...] = n_t
    scale[...] = r1
    n = n_t.T
    for p in range(3):
        first_col = p * 384
        kv = nn(n, w[:, first_col + 128 : first_col + 384])
        cols = slice(p * 128, (p + 1) * 128)
        k[:, cols] = kv[:, :128].astype(BF)
        v[:, cols] = kv[:, 128:].astype(BF)
        kv_t = kv.T.astype(BF)
        k_t[cols, :] = kv_t[:128]
        v_t[cols, :] = kv_t[128:]

    @pl.when(i < 2)
    def _():
        for p in range(3):
            q = nn(n, w[:, p * 384 : p * 384 + 128]) * (SCALE * LOG2E)
            q_t[p * 128 : (p + 1) * 128, :] = q.T.astype(BF)


def project_half(order, x, gain, weights, half, old, deps):
    base = half * (HALF // B)
    first = half == 0

    def cols_of(rows, offset=0):
        return pl.BlockSpec((rows, B), lambda i, t: (0, offset + t[i]))

    whole = lambda shape: pl.BlockSpec(shape, lambda i, t: (0, 0))
    slots = pl.BlockSpec((1, FB, 1152), lambda i, t: (t[4], 0, 0))
    major = pl.BlockSpec((B, 384), lambda i, t: (base + t[i], 0))
    minor = pl.BlockSpec((384, B), lambda i, t: (0, base + t[i]))
    kv = [jax.ShapeDtypeStruct(s, BF) for s in ((LEN, 384), (384, LEN)) * 2]
    cross = pl.BlockSpec((2, FB, 1152), lambda i, t: (0, 0, 0))
    w_specs = [slots, slots, cross] if first else [whole((D, 1152))]
    extra = len(w_specs) + len(old) + len(deps)
    return pl.pallas_call(
        functools.partial(qkv_kernel, first=first, extra=extra),
        grid_spec=pltpu.PrefetchScalarGridSpec(
            num_scalar_prefetch=1,
            grid=(HALF // B,),
            in_specs=[cols_of(FB, base), cols_of(FB), pl.BlockSpec((2, FB, B), lambda i, t: (0, 0, t[i])), whole((D, 1))]
            + w_specs
            + [ANY] * (len(old) + len(deps)),
            out_specs=[
                cols_of(D),
                cols_of(1),
                pl.BlockSpec((384, B), lambda i, t: (0, jnp.minimum(i, 1))),
                major,
                minor,
                major,
                minor,
            ]
            + [whole((D, 1152))] * first,
        ),
        out_shape=[
            jax.ShapeDtypeStruct((D, HALF), BF),
            jax.ShapeDtypeStruct((1, HALF), F32),
            jax.ShapeDtypeStruct((384, HALF // 2), BF),
        ]
        + kv
        + [jax.ShapeDtypeStruct((D, 1152), BF)] * first,
        input_output_aliases={5 + len(w_specs) + n: 3 + n for n in range(len(old))},
        compiler_params=pltpu.CompilerParams(vmem_limit_bytes=48 * MIB),
        cost_estimate=cost(12),
    )(order, *x, gain, *weights, *old, *deps)


def block_masks(first, last):
    key = lax.broadcasted_iota(jnp.int32, (B, B), 0)
    query = lax.broadcasted_iota(jnp.int32, (B, B), 1)
    piece = (key >= first) & (key < last) & (query >= first) & (query < last)
    return (key > query, (key <= query) | piece)


def masked(scores, masks, step, count):
    if step == count - 1:
        scores = jnp.where(masks[1], scores, MASKED)
    if count == 4 and step == 0:
        scores = jnp.where(masks[0], scores, MASKED)
    return scores


def head_rows(pair_t):
    row = lax.broadcasted_iota(jnp.int32, pair_t.shape, 0)
    zero = jnp.zeros((), pair_t.dtype)
    return [jnp.where((row // HD) == h, pair_t, zero) for h in range(2)]


def head_cols(pair):
    col = lax.broadcasted_iota(jnp.int32, pair.shape, 1)
    zero = jnp.zeros((), pair.dtype)
    return [jnp.where((col // HD) == h, pair, zero) for h in range(2)]


def for_counts(block, counts, body):
    if len(counts) == 1:
        body(counts[0])
        return
    visible = jnp.minimum(block, 3) + 1
    for count in counts:
        pl.when(visible == count)(functools.partial(body, count))


def attend_kernel(tab, q_t, k, v_t, *refs, counts):
    o_own, o_other, log_total = refs[-3:]
    i = pl.program_id(1)
    block, first, last = tab[i], tab[2 + i], tab[4 + i]

    def body(count):
        masks = block_masks(first, last)
        starts = [pl.multiple_of((block - (count - 1) + t) * B, B) for t in range(count)]
        for h, q_head in enumerate(head_rows(q_t[...])):
            scores = [masked(nn(k[pl.ds(s, B), :], q_head), masks, t, count) for t, s in enumerate(starts)]
            peak = functools.reduce(jnp.maximum, [jnp.max(s, axis=0, keepdims=True) for s in scores])
            total, mixed = 0.0, 0.0
            for score, s in zip(scores, starts):
                part = jnp.exp2(score - peak)
                total = total + jnp.sum(part, axis=0, keepdims=True)
                mixed = mixed + nn(v_t[h * HD : (h + 1) * HD, pl.ds(s, B)], part.astype(BF))
            out = (mixed * (1.0 / total)).astype(BF)

            @pl.when(i == 0)
            def _():
                o_own[h * HD : (h + 1) * HD, :] = out

            @pl.when(i == 1)
            def _():
                o_other[h * HD : (h + 1) * HD, :] = out

            log_total[0, h : h + 1, :] = peak + jnp.log2(total)

    for_counts(block, counts, body)


def attend(tab, q_t, k, v_t, half, pairs, *deps):
    base, count = pairs
    span = LEN if half else HALF
    one = pl.BlockSpec((128, B), lambda p, i, t: (p, 0))
    block = jax.ShapeDtypeStruct((count * 128, B), BF)
    return pl.pallas_call(
        functools.partial(attend_kernel, counts=(4,) if half else (1, 2, 3, 4)),
        grid_spec=pltpu.PrefetchScalarGridSpec(
            num_scalar_prefetch=1,
            grid=(count, 2),
            in_specs=[
                pl.BlockSpec((128, B), lambda p, i, t: (base + p, i)),
                pl.BlockSpec((span, 128), lambda p, i, t: (0, base + p)),
                pl.BlockSpec((128, span), lambda p, i, t: (base + p, 0)),
            ]
            + [ANY] * len(deps),
            out_specs=[one, one, pl.BlockSpec((1, 2, B), lambda p, i, t: (p, 0, i))],
        ),
        out_shape=[block, block, jax.ShapeDtypeStruct((count, 2, 2 * B), F32)],
        compiler_params=pltpu.CompilerParams(vmem_limit_bytes=48 * MIB),
        cost_estimate=cost((8 if half else 6) * count),
    )(tab, q_t, k, v_t, *deps)


def attend_back_kernel(tab, q_t, do_own, do_other, o_own, o_other, log_total, k, v, k_t, *refs, counts, half):
    if half:
        dq_t, high, low, dkv = refs[-4:]
    else:
        start = refs[0]
        dq_t, low, dkv = refs[-3:]
    i = pl.program_id(1)
    block, first, last = tab[i], tab[2 + i], tab[4 + i]

    @pl.when(i == 0)
    def _():
        dkv[...] = jnp.zeros_like(dkv) if half else start[0]

    def body(count):
        masks = block_masks(first, last)
        queries, grads = q_t[...], jnp.where(i == 0, do_own[...], do_other[...])
        mixed = jnp.where(i == 0, o_own[...], o_other[...])
        q_rows, g_rows = head_rows(queries), head_rows(grads)
        q_cols, g_cols = head_cols(queries.T), head_cols(grads.T)
        product = grads.astype(F32) * mixed.astype(F32)
        inner = [jnp.sum(product[h * HD : (h + 1) * HD], axis=0, keepdims=True) for h in range(2)]
        dq = [0.0, 0.0]
        for t in range(count):
            rows = pl.ds(pl.multiple_of((block - (count - 1) + t) * B, B), B)
            key_rows, value_rows = k[rows, :], v[rows, :]
            dk_part = dv_part = 0.0
            for h in range(2):
                score = masked(nn(key_rows, q_rows[h]), masks, t, count)
                probs = jnp.exp2(score - log_total[0, h : h + 1, :])
                grad_probs = nn(value_rows, g_rows[h])
                grad_scores = (probs * (grad_probs - inner[h])).astype(BF)
                dv_part = dv_part + nn(probs.astype(BF), g_cols[h])
                dk_part = dk_part + nn(grad_scores, q_cols[h])
                dq[h] = dq[h] + nn(k_t[h * HD : (h + 1) * HD, rows], grad_scores)
            dkv[rows, :128] += dk_part
            dkv[rows, 128:] += dv_part
        for h in range(2):
            dq_t[h * HD : (h + 1) * HD, :] = (dq[h] * SCALE).astype(BF)

    for_counts(block, counts, body)

    @pl.when(i == 1)
    def _():
        target, rows = (high, slice(HALF, LEN)) if half else (low, slice(0, HALF))
        target[0, :, :128] = (dkv[rows, :128] * (1.0 / LOG2E)).astype(BF)
        target[0, :, 128:] = dkv[rows, 128:].astype(BF)
        if half:
            low[0] = dkv[:HALF, :]


def attend_back(tab, q_t, grads, outs, log_total, k, v, k_t, half, pairs, start, *deps):
    base, count = pairs
    one = pl.BlockSpec((128, B), lambda p, i, t: (base + p, 0))
    one_of = pl.BlockSpec((128, B), lambda p, i, t: (base + p, half))
    span = LEN if half else HALF
    query = pl.BlockSpec((128, B), lambda p, i, t: (base + p, i))
    stat = pl.BlockSpec((1, 2, B), lambda p, i, t: (base + p, 0, i))
    major = pl.BlockSpec((span, 128), lambda p, i, t: (0, base + p))
    minor = pl.BlockSpec((128, span), lambda p, i, t: (base + p, 0))
    grad = pl.BlockSpec((1, HALF, 256), lambda p, i, t: (p, 0, 0))
    grad_in = pl.BlockSpec((1, HALF, 256), lambda p, i, t: (base + p, 0, 0))
    return pl.pallas_call(
        functools.partial(attend_back_kernel, counts=(4,) if half else (1, 2, 3, 4), half=half),
        grid_spec=pltpu.PrefetchScalarGridSpec(
            num_scalar_prefetch=1,
            grid=(count, 2),
            in_specs=[query, one_of, one_of, one, one, stat, major, major, minor]
            + [grad_in] * len(start)
            + [ANY] * len(deps),
            out_specs=[pl.BlockSpec((128, B), lambda p, i, t: (p, i)), grad] + [grad] * half,
            scratch_shapes=[pltpu.VMEM((span, 256), F32)],
        ),
        out_shape=[
            jax.ShapeDtypeStruct((count * 128, 2 * B), BF),
            jax.ShapeDtypeStruct((count, HALF, 256), BF),
        ]
        + [jax.ShapeDtypeStruct((count, HALF, 256), F32)] * half,
        compiler_params=pltpu.CompilerParams(vmem_limit_bytes=56 * MIB),
        cost_estimate=cost((16 if half else 12) * count),
    )(tab, q_t, *grads, *outs, log_total, k, v, k_t, *start, *deps)


HEAD_ROWS = ((0, 0, 128), (128, 192, 128), (256, 128, 64), (320, 320, 64))
ROOT = math.sqrt(2.0 / math.pi)


def feed_chunk(up):
    square = up * up
    half = 0.5 + 0.5 * jnp.tanh(up * (ROOT + (ROOT * 0.044715) * square))
    act = (up * half).astype(BF)
    slope = half + (2.0 * up) * (half - half * half) * (ROOT + (3.0 * ROOT * 0.044715) * square)
    return act, slope


def feed_kernel(sel, gain, *refs):
    nears, pairs, crosses = refs[:4], refs[4:8], refs[8:11]
    a_parts, dy_parts, x_parts = refs[11:17], refs[17:20], refs[20:25]
    outs = refs[-26:]
    both_near, both_far, ga_own, ga_other, gain_sum = outs[:5]
    g_near, g_one, g_rest = outs[5:8]
    w_up, w_down, w_out, a_t, dy_t, x_t, n, dy, mid, mlp, gn, stage, stage_out = outs[8:21]
    w_sems, a_sems, in_sems, out_sems, last_sems = outs[21:26]
    core, parity = sel[0], sel[3]

    def start(copies):
        for copy in copies:
            copy.start()

    def wait(copies):
        for copy in copies:
            copy.wait()

    halves = (((0, 768, 0, 0), (768, 896, 1, 0)), ((0, 128, 1, 128), (128, 896, 2, 0)))
    targets = (w_up, w_out, w_down)

    def loads(slot, swapped):
        copies = []

        def add(source, offset, which_half, rel):
            for first, last, which, at in halves[which_half]:
                copies.append(
                    pltpu.make_async_copy(
                        source.at[:, offset + first : offset + last],
                        targets[which].at[slot, rel * FB : (rel + 1) * FB, at : at + last - first],
                        w_sems.at[slot, len(copies)],
                    )
                )

        for half in range(2):
            add(nears[slot], half * 896, half, 0)
            if slot < 2:
                add(pairs[half ^ swapped].at[slot], 0, half, 1)
                add(crosses[0].at[slot], half * 896, half, 2)
                add(crosses[0].at[slot], 1792 + (half ^ swapped) * 896, half, 3)
            else:
                add(pairs[slot], half * 896, half, 1)
                add(crosses[slot - 1].at[0], half * 896, half, 2)
                add(crosses[slot - 1].at[1], half * 896, half, 3)
        return copies

    def a_loads():
        copies = []
        for half in range(2):
            cols = slice(half * B, (half + 1) * B)
            for side in range(2):
                for source, target, size in HEAD_ROWS:
                    if side == 1:
                        part, at = a_parts[4 + half], source
                    elif source < 128:
                        part, at = a_parts[2 * half], source
                    else:
                        part, at = a_parts[2 * half + 1], source - 128
                    copies.append(
                        pltpu.make_async_copy(
                            part.at[at : at + size, :],
                            a_t.at[side * 384 + target : side * 384 + target + size, cols],
                            a_sems.at[len(copies)],
                        )
                    )
        return copies

    def token_loads():
        copies = []

        def add(source, target):
            copies.append(pltpu.make_async_copy(source, target, in_sems.at[len(copies)]))

        for half in range(2):
            cols = slice(half * B, (half + 1) * B)
            place = pl.ds(pl.multiple_of(sel[1 + half] * B, B), B)
            at_whole = pl.ds(pl.multiple_of((sel[1 + half] + 4 * half) * B, B), B)
            add(dy_parts[0].at[:, at_whole], dy_t.at[0:FB, cols])
            add(x_parts[0].at[:, at_whole], x_t.at[0:FB, cols])
            pair, cross = x_parts[1 + 2 * half : 3 + 2 * half]
            add(pair.at[:, place], x_t.at[FB : 2 * FB, cols])
            add(cross.at[0, :, place], x_t.at[2 * FB : 3 * FB, cols])
            add(cross.at[1, :, place], x_t.at[3 * FB :, cols])
        add(dy_parts[1].at[0], dy_t.at[FB : 2 * FB, :])
        add(dy_parts[2].at[0], dy_t.at[2 * FB : 3 * FB, :])
        add(dy_parts[2].at[1], dy_t.at[3 * FB :, :])
        return copies

    def stores(slot):
        far = g_one if slot == 1 else g_rest.at[(0, 0, 1, 2)[slot]]
        copies = []
        for side, target in enumerate((g_near.at[slot], far)):
            for which in range(2):
                copies.append(
                    pltpu.make_async_copy(
                        stage.at[slot % 2, which, pl.ds(side * 384, 384), :],
                        target.at[:, which * 1024 : which * 1024 + D],
                        out_sems.at[slot % 2, side * 2 + which],
                    )
                )
        return copies

    def last_stores(slot):
        far = g_one if slot == 1 else g_rest.at[(0, 0, 1, 2)[slot]]
        return [
            pltpu.make_async_copy(
                stage_out.at[slot, pl.ds(side * 384, 384), :],
                target.at[:, D : D + 256],
                last_sems.at[slot, side],
            )
            for side, target in enumerate((g_near.at[slot], far))
        ]

    start(a_loads())
    start(token_loads())

    @pl.when(parity == 0)
    def _():
        for slot in range(4):
            start(loads(slot, 0))

    @pl.when(parity == 1)
    def _():
        for slot in range(4):
            start(loads(slot, 1))

    a_t[D:, :] = jnp.zeros((64, a_t.shape[1]), BF)

    def a_rows(slot, count):
        place = lax.rem(slot + 2 * core, 4) * FB
        return pl.ds(pl.multiple_of(place, FB), count)

    wait(token_loads())
    dy[...] = dy_t[...].T
    wait(a_loads())
    for slot in range(4):
        wait(loads(slot, 0))
    mixed = nn(w_out[0], a_t[a_rows(0, 256), :])
    for slot in range(1, 4):
        mixed = mixed + nn(w_out[slot], a_t[a_rows(slot, 256), :])
    mid[...] = x_t[...].astype(F32) + mixed
    mlp[...] = mid[...]
    gn[...] = jnp.zeros_like(gn)
    r2 = lax.rsqrt(jnp.sum(mid[...] * mid[...], axis=0, keepdims=True) * (1.0 / D) + EPSILON)
    n_t = x_t
    n_t[...] = (mid[...] * r2 * gain[...]).astype(BF)
    n[...] = n_t[...].T

    def chunk(slot, carry):
        buffer = lax.rem(slot, 2)
        for before in range(2):

            @pl.when(slot == before + 2)
            def _():
                wait(stores(before))

        up = nn(n[...], w_up[slot])
        act, slope = feed_chunk(up)
        stage[buffer, 1] = nn(dy_t[...], act).astype(BF)
        mlp[...] += nt(w_down[slot], act)
        grad_up = (nn(dy[...], w_down[slot]) * slope).astype(BF)
        stage[buffer, 0] = nn(n_t[...], grad_up).astype(BF)
        gn[...] += nt(w_up[slot], grad_up)
        for now in range(4):

            @pl.when(slot == now)
            def _():
                start(stores(now))

        return carry

    lax.fori_loop(0, 4, chunk, 0)
    both_near[0] = mlp[:384].astype(BF)
    both_far[0] = mlp[384:].astype(BF)
    weighted = gn[...] * gain[...]
    inner = jnp.sum(mid[...] * weighted, axis=0, keepdims=True)
    cubed = r2 * r2 * r2 * inner * (1.0 / D)
    gm = (dy_t[...].astype(F32) + r2 * weighted - mid[...] * cubed).astype(BF)
    x_t[...] = gm
    both_near[1] = gm[:384]
    both_far[1] = gm[384:]
    gain_sum[...] = jnp.sum(gn[...] * mid[...] * r2, axis=1, keepdims=True)
    for slot in range(4):
        grad_a = contract(w_out[slot], x_t[...], ((0,), (0,)))[:FB].astype(BF)

        def place(target):
            for to, source, size in HEAD_ROWS:
                if source // FB == slot % 2:
                    target[to : to + size, :] = grad_a[source % FB : source % FB + size]

        pl.when((slot // 2) == core)(functools.partial(place, ga_own))
        pl.when((slot // 2) != core)(functools.partial(place, ga_other))
        part = nt(x_t[...], a_t[a_rows(slot, FB), :])
        stage_out[slot] = jnp.concatenate([part, jnp.zeros((D, 64), F32)], axis=1).astype(BF)
        start(last_stores(slot))
    wait(stores(2))
    wait(stores(3))
    for slot in range(4):
        wait(last_stores(slot))


def feed_forward(sel, gain, nears, pairs, crosses, a_parts, dy_parts, x_parts, *deps):
    count = 2 * B
    vmem = pl.BlockSpec(memory_space=pltpu.VMEM)
    both = jax.ShapeDtypeStruct((2, 384, count), BF)
    heads = jax.ShapeDtypeStruct((384, count), BF)
    inputs = (*nears, *pairs, *crosses, *a_parts, *dy_parts, *x_parts, *deps)
    return pl.pallas_call(
        feed_kernel,
        in_specs=[pl.BlockSpec(memory_space=pltpu.SMEM), vmem] + [ANY] * len(inputs),
        out_specs=[vmem] * 5 + [ANY] * 3,
        out_shape=[both, both, heads, heads, jax.ShapeDtypeStruct((D, 1), F32)]
        + [jax.ShapeDtypeStruct(shape, BF) for shape in ((4, 384, 1792), (384, 1792), (3, 384, 1792))],
        scratch_shapes=[
            pltpu.VMEM((4, D, D), BF),
            pltpu.VMEM((4, D, D), BF),
            pltpu.VMEM((4, D, 256), BF),
            pltpu.VMEM((D + 64, count), BF),
            pltpu.VMEM((D, count), BF),
            pltpu.VMEM((D, count), BF),
            pltpu.VMEM((count, D), BF),
            pltpu.VMEM((count, D), BF),
            pltpu.VMEM((D, count), F32),
            pltpu.VMEM((D, count), F32),
            pltpu.VMEM((D, count), F32),
            pltpu.VMEM((2, 2, D, D), BF),
            pltpu.VMEM((4, D, 256), BF),
            pltpu.SemaphoreType.DMA((4, 16)),
            pltpu.SemaphoreType.DMA((16,)),
            pltpu.SemaphoreType.DMA((13,)),
            pltpu.SemaphoreType.DMA((2, 4)),
            pltpu.SemaphoreType.DMA((4, 2)),
        ],
        compiler_params=pltpu.CompilerParams(vmem_limit_bytes=62 * MIB),
        cost_estimate=cost(50),
    )(sel, gain, *inputs)


def qkv_back_kernel(tab, w, n_t, *refs, half):
    if half:
        dq, dkv, start = refs[:3]
        dq, dkv = [dq[p * 128 : (p + 1) * 128, :] for p in range(3)], [dkv[p] for p in range(3)]
    else:
        first_dq, last_dq, first_dkv, last_dkv, start = refs[:5]
        dq = [first_dq[:128, :], first_dq[128:, :], last_dq[...]]
        dkv = [first_dkv[0], first_dkv[1], last_dkv[0]]
    near, far, inner, gain_out, *grads = refs[-5:] if half else refs[-4:]
    i = pl.program_id(0)
    grad_w = grads[0] if half else None

    @pl.when(i == 0)
    def _():
        gain_out[...] = start[...]
        if half:
            grad_w[...] = jnp.zeros_like(grad_w)

    normed = n_t[...]
    if half:
        for p in range(3):
            grad_w[p, :, 128:] += nn(normed, dkv[p])

    def finish(grad):
        near[...] = grad[:384].astype(BF)
        far[...] = grad[384:].astype(BF)
        product = grad * normed.astype(F32)
        inner[...] = jnp.sum(product, axis=0, keepdims=True)
        gain_out[...] += jnp.sum(product, axis=1, keepdims=True)

    def key_part():
        total = 0.0
        for p in range(3):
            total = total + nt(w[:, p * 384 + 128 : (p + 1) * 384], dkv[p])
        return total

    @pl.when(i < 2)
    def _():
        total = key_part()
        for p in range(3):
            total = total + nn(w[:, p * 384 : p * 384 + 128], dq[p])
            if half:
                grad_w[p, :, :128] += nt(normed, dq[p])
        finish(total)

    @pl.when(i >= 2)
    def _():
        finish(key_part())


def project_back(order, w, n_t, dq, dkv, half, start, *deps):
    whole = lambda shape: pl.BlockSpec(shape, lambda i, t: (0,) * len(shape))

    def cols_of(rows):
        return pl.BlockSpec((rows, B), lambda i, t: (0, t[i]))

    def own(rows):
        return pl.BlockSpec((rows, B), lambda i, t: (0, jnp.minimum(i, 1)))

    low = jax.ShapeDtypeStruct((384, HALF), BF)
    counts = (3,) if half else (2, 1)
    specs = [own(128 * n) for n in counts]
    specs += [pl.BlockSpec((n, B, 256), lambda i, t: (0, t[i], 0)) for n in counts] + [whole((D, 1))]
    return pl.pallas_call(
        functools.partial(qkv_back_kernel, half=half),
        grid_spec=pltpu.PrefetchScalarGridSpec(
            num_scalar_prefetch=1,
            grid=(HALF // B,),
            in_specs=[whole((D, 1152)), cols_of(D)] + specs + [ANY] * len(deps),
            out_specs=[cols_of(384), cols_of(384), cols_of(1), whole((D, 1))] + [whole((3, D, 384))] * half,
        ),
        out_shape=[low, low, jax.ShapeDtypeStruct((1, HALF), F32), jax.ShapeDtypeStruct((D, 1), F32)]
        + [jax.ShapeDtypeStruct((3, D, 384), F32)] * half,
        compiler_params=pltpu.CompilerParams(vmem_limit_bytes=56 * MIB),
        cost_estimate=cost(15 if half else 10),
    )(order, w, n_t, *dq, *dkv, *start, *deps)


def weights_kernel(tab, n_t, dq_t, dkv, start, *refs):
    near, far = refs[-2:]
    kv = start[0, :, 128:] + nn(n_t[...], dkv[0])
    q = start[0, :, :128]
    for i in range(2):
        q = q + nt(n_t[:, pl.ds(pl.multiple_of(tab[i] * B, B), B)], dq_t[:, i * B : (i + 1) * B])
    near[0, :, :128] = q[:384].astype(BF)
    far[0, :, :128] = q[384:].astype(BF)
    near[0, :, 128:] = kv[:384].astype(BF)
    far[0, :, 128:] = kv[384:].astype(BF)


def weights_back(order, n_t, dq_t, dkv, start, pairs, *deps):
    base, count = pairs
    each = lambda shape, base: pl.BlockSpec((1, *shape), lambda i, t: (base + i, 0, 0))
    part = jax.ShapeDtypeStruct((count, 384, 384), BF)
    return pl.pallas_call(
        weights_kernel,
        grid_spec=pltpu.PrefetchScalarGridSpec(
            num_scalar_prefetch=1,
            grid=(count,),
            in_specs=[
                pl.BlockSpec((D, HALF), lambda i, t: (0, 0)),
                pl.BlockSpec((128, 2 * B), lambda i, t: (i, 0)),
                each((HALF, 256), 0),
                each((D, 384), base),
            ]
            + [ANY] * len(deps),
            out_specs=[each((384, 384), 0)] * 2,
        ),
        out_shape=[part, part],
        compiler_params=pltpu.CompilerParams(vmem_limit_bytes=48 * MIB),
        cost_estimate=cost(2 + 2 * count),
    )(order, n_t, dq_t, dkv, start, *deps)


def finish_kernel(sel, *refs):
    here, cross, there = refs[:3]
    near, core_part, pair_part, x, scale, inner, gain = refs[3:10]
    out, grad_x = refs[-2:]
    i = pl.program_id(0)
    pair, device = sel[2 + i], sel[6 + i]
    same, own = pair == sel[0], device == sel[1]
    mine = jnp.where(own, here[...], cross[...])
    theirs = jnp.where(own, there[:, 0], there[:, 1])
    both = jnp.where(same, mine, theirs)
    out[...] = both[0]
    total = near[...].astype(F32) + core_part[...].astype(F32) + pair_part[...].astype(F32)
    r1 = scale[...]
    grad_x[...] = both[1].astype(F32) + r1 * gain[...] * total - x[...].astype(F32) * (r1 * r1 * inner[...] * (1.0 / D))


def finish_half(sel, here, cross, there, near, core_part, pair_part, x, scale, inner, gain, half, old, *deps):
    base = half * (HALF // B)
    piece = pl.BlockSpec((2, FB, B), lambda i, t: (0, 0, half))
    cols = pl.BlockSpec((FB, B), lambda i, t: (0, i))
    into = pl.BlockSpec((FB, B), lambda i, t: (0, base + i))
    row = pl.BlockSpec((1, B), lambda i, t: (0, i))
    return pl.pallas_call(
        finish_kernel,
        grid_spec=pltpu.PrefetchScalarGridSpec(
            num_scalar_prefetch=1,
            grid=(HALF // B,),
            in_specs=[
                piece,
                piece,
                pl.BlockSpec((2, 2, FB, B), lambda i, t: (0, 0, 0, half)),
                cols,
                cols,
                cols,
                into,
                row,
                row,
                pl.BlockSpec((FB, 1), lambda i, t: (0, 0)),
            ]
            + [ANY] * (len(old) + len(deps)),
            out_specs=[into, into],
        ),
        out_shape=[jax.ShapeDtypeStruct((FB, LEN), BF), jax.ShapeDtypeStruct((FB, LEN), F32)],
        input_output_aliases={11 + n: n for n in range(len(old))},
        cost_estimate=cost(6),
    )(sel, here, cross, there, near, core_part, pair_part, x, scale, inner, gain, *old, *deps)


def per_device(
    block_input,
    norm_gain_one,
    w_query,
    w_key,
    w_value,
    w_out,
    norm_gain_two,
    w_up,
    w_down,
    piece_start,
    piece_len,
    grad_y,
):
    c = lax.axis_index("cols")
    r = lax.axis_index("rows")
    y, core = c // 2, c % 2
    parity = lax.axis_index("dp") % 2

    def order_of(table):
        return jnp.array(table, jnp.int32)[c]

    low_order = order_of([[0, 3, 1, 2], [3, 0, 1, 2], [1, 2, 0, 3], [2, 1, 0, 3]])
    high_order = order_of([[0, 1, 2, 3], [1, 0, 2, 3], [2, 3, 0, 1], [3, 2, 0, 1]])
    away = order_of([[3, 5, 1, 6, 2, 7], [0, 4, 2, 7, 1, 6], [2, 7, 0, 4, 3, 5], [1, 6, 3, 5, 0, 4]])

    small = jnp.concatenate(
        [norm_gain_one, norm_gain_two, piece_start[0].astype(F32), piece_len[0].astype(F32)]
    )
    small = jnp.stack([small, cols_swap(small, 2)])
    small = jnp.concatenate([small, cols_swap(small, 1)])
    gain_one = small[:, :FB].reshape(D, 1)
    gain_two = small[:, FB : 2 * FB].reshape(D, 1)
    apart = jnp.bitwise_xor(c, r)
    mine = jnp.where(apart == 0, 0, jnp.where(apart == 2, 1, jnp.where(apart == 1, 2, 3)))
    pieces = lax.dynamic_index_in_dim(small, mine, 0, keepdims=False)[2 * FB :].astype(jnp.int32)
    firsts = pieces[:8] - jnp.arange(8, dtype=jnp.int32) * B
    lasts = firsts + pieces[8:]

    def table(order, half):
        blocks = order[:2] + half * 4
        return jnp.concatenate([blocks, firsts[blocks], lasts[blocks]])

    low_table, high_table = table(low_order, 0), table(high_order, 1)
    low_order = jnp.concatenate([low_order, core[None].astype(jnp.int32)])
    high_order = jnp.concatenate([high_order, core[None].astype(jnp.int32)])

    own_low = block_input[:, :HALF]
    pair_low = cols_swap(own_low, 2)
    w_slots = [
        jnp.concatenate(
            [w[:, :128] for w in (w_query, w_key, w_value)] + [w[:, 128:] for w in (w_query, w_key, w_value)], axis=1
        )
    ]
    w_slots += [rows_shift(w_slots[0], step) for step in (1, 2, 3)]

    def merge(first, second):
        parts = [first[:, :384], second[:, :384]]
        for n in range(3):
            cols = slice(384 + n * HD, 384 + (n + 1) * HD)
            parts += [first[:, cols], second[:, cols]]
        return jnp.concatenate(parts, axis=1)

    w_near = jnp.stack([merge(*w_slots[:2]), merge(*w_slots[2:])])
    cross_low = cols_swap(jnp.stack([own_low, pair_low]), 1)
    x_low = (pair_low, cross_low)
    own_pack = jnp.concatenate([w_up, w_out.T, jnp.zeros((FB, 64), BF), w_down], axis=1)
    ring = [tie(own_pack, w_near)]
    ring.append(rows_shift(ring[0], 1))
    w_pair = tie(cols_swap(w_near, 2), cross_low)
    w_cross = cols_swap(
        jnp.stack([lax.dynamic_index_in_dim(part, 1 - core, 0, keepdims=False) for part in (w_near, w_pair)]), 1
    )

    pair_high = cols_swap(tie(block_input[:, HALF:], w_pair), 2)

    normed_low, scale_low, q_low, *kv, w_qkv = project_half(
        low_order, (block_input, *x_low), gain_one, (w_near, w_pair, w_cross), 0, (), ()
    )
    ring[1] = tie(ring[1], scale_low)
    first_sent = jnp.stack(ring)
    first_sent = jnp.where(parity == 0, first_sent[:, :, :896], first_sent[:, :, 896:])
    outs_low = [attend(low_table, q_low, kv[0], kv[3], 0, (0, 1), first_sent)]
    first_pairs = cols_swap(first_sent, 2)
    ring.append(rows_shift(ring[1], 1))
    pair_high = tie(pair_high, outs_low[0][2])
    cross_sent = jnp.stack([block_input[:, HALF:], pair_high])
    outs_low.append(attend(low_table, q_low, kv[0], kv[3], 0, (1, 2), outs_low[0][2], cross_sent))
    ring[2] = tie(ring[2], outs_low[1][2])
    ring.append(rows_shift(ring[2], 1))
    cross_high = cols_swap(cross_sent, 1)
    x_high = (pair_high, cross_high)
    low_got = cols_swap(jnp.concatenate([out[1] for out in outs_low]), 1)
    dy_core = hold(away[:2], grad_y, B, scale_low)
    dy_away = tie(hold(away[2:], grad_y, B, scale_low), outs_low[1][2])
    normed_high, scale_high, q_high, *kv = project_half(
        high_order, (block_input, *x_high), gain_one, (w_qkv,), 1, tuple(kv), (outs_low[1][2], dy_away, first_pairs)
    )
    k, k_t, v, v_t = kv
    first_crossed = dp_swap(first_pairs)
    dy_pair = cols_swap(dy_away, 2)
    third_pair = cols_swap(ring[2], 2)
    outs_high = [attend(high_table, q_high, k, v_t, 1, (0, 1), low_got)]
    ring[3] = tie(ring[3], outs_high[0][2])
    dy_pair, third_pair = tie(dy_pair, outs_high[0][2]), tie(third_pair, outs_high[0][2])
    dy_cross_sent = jnp.concatenate([dy_core, dy_pair[1:]])
    third_sent = jnp.stack([ring[2], third_pair])
    outs_high.append(
        attend(high_table, q_high, k, v_t, 1, (1, 2), outs_high[0][2], ring[3], dy_cross_sent, third_sent)
    )
    dy_cross = cols_swap(dy_cross_sent, 1)
    third_cross = cols_swap(third_sent, 1)
    first_crossed = tie(first_crossed, outs_high[0][2])
    first_cross = cols_swap(jnp.concatenate([jnp.stack(ring[:2]), first_pairs, first_crossed], axis=2), 1)
    last_pair = cols_swap(ring[3], 2)
    last_pair = tie(last_pair, outs_high[1][2])
    last_cross = cols_swap(jnp.stack([ring[3], last_pair]), 1)
    high_got = cols_swap(jnp.concatenate([out[1] for out in outs_high]), 1)

    sel = jnp.stack([core.astype(jnp.int32), low_order[0], high_order[0], parity.astype(jnp.int32)])
    both_near, both_far, ga_own, ga_other, gain_two_sum, g_near, g_one, g_rest = feed_forward(
        sel,
        gain_two,
        ring,
        (first_pairs, first_crossed, third_pair, last_pair),
        (first_cross, third_cross, last_cross),
        [out[0] for out in outs_low + outs_high] + [low_got, high_got],
        (grad_y, dy_pair, dy_cross),
        (block_input, *x_low, *x_high),
    )

    def three(first, second, third):
        return (first.astype(F32) + second.astype(F32) + third.astype(F32)).astype(BF)

    def two(first, second):
        return (first.astype(F32) + second.astype(F32)).astype(BF)

    ga_got = cols_swap(ga_other, 1)
    total = two(g_near[1], cols_swap(g_one, 1))
    both_cross = cols_swap(both_far, 1)
    there_sent = jnp.stack([both_near[:, FB:], both_cross[:, FB:]], axis=1)
    g_got = cols_swap(g_rest, 1)
    out_low = [jnp.concatenate(parts) for parts in zip(*outs_low)]
    out_high = [jnp.concatenate(parts) for parts in zip(*outs_high)]
    grads = (ga_own, ga_got)
    dq_high, dkv_high, dkv_low = attend_back(
        high_table, q_high, grads, out_high[:2], out_high[2], k, v, k_t, 1, (0, 3), (), total, there_sent
    )
    there = cols_swap(there_sent, 2)
    total = three(tie(rows_shift(total, 1), dq_high), g_near[2], g_got[1])
    near_high, far_high, inner_high, gain_part, w_part = project_back(
        high_order, w_qkv, normed_high, (dq_high,), (dkv_high,), 1, (jnp.zeros((D, 1), F32),), total, there
    )
    low = (low_table, q_low, grads, out_low[:2], out_low[2], k, v, k_t, 0)
    got_high = cols_swap(far_high, 1)
    dq_first, dkv_first = attend_back(*low, (0, 2), (dkv_low,), near_high)
    got_high = tie(got_high, dq_first)
    sent_high = two(near_high[FB:], got_high[FB:])
    total = three(tie(rows_shift(total, 1), dq_first), g_near[3], g_got[2])
    wg_first = weights_back(low_order, normed_low, dq_first, dkv_first, w_part, (0, 2), sent_high, total)
    pair_sent = cols_swap(sent_high, 2)
    dq_last, dkv_last = attend_back(*low, (2, 1), (dkv_low,), wg_first[0])

    def by_core(near, got):
        return jnp.where(core == 0, near, got), jnp.where(core == 0, got, near)

    def half_of(part, which):
        return jnp.concatenate([part[:, n * 128 + which * HD : n * 128 + (which + 1) * HD] for n in range(3)], axis=1)

    got = tie(cols_swap(wg_first[1], 1), dq_last)
    pair_zero, pair_one = by_core(wg_first[0][0], got[0]), by_core(wg_first[0][1], got[1])
    total = three(tie(rows_shift(total, 1), dq_last), g_near[0], g_got[0])
    total_far = total[FB:]
    near_low, far_low, inner_low, gain_part = project_back(
        low_order,
        w_qkv,
        normed_low,
        (dq_first, dq_last),
        (dkv_first, dkv_last),
        0,
        (gain_part,),
        pair_zero[1],
        *pair_one,
        pair_sent,
        total_far,
    )
    firsts = [rows_shift(pair_zero[1], -2), rows_shift(pair_one[0], -1), rows_shift(pair_one[1], -3)]
    feed_got = cols_swap(total_far, 2)
    wg_last = weights_back(low_order, normed_low, dq_last, dkv_last, w_part, (2, 1), near_low, firsts[0])
    got_low = tie(cols_swap(far_low, 1), wg_last[0])
    sent_low = two(near_low[FB:], got_low[FB:])
    got = tie(cols_swap(wg_last[1], 1), sent_low)
    last = by_core(wg_last[0][0], got[0])
    slots = [half_of(last[slot // 2], slot % 2) for slot in range(4)]

    def dp_sum(part, *deps):
        if lax.axis_size("dp") == 2:
            got = dp_swap(part)
            got = tie(got, *deps) if deps else got
            return part.astype(F32) + got.astype(F32)
        return lax.psum(part.astype(F32), "dp")

    feed_sum = two(total[:FB], feed_got)
    pair_got = cols_swap(sent_low, 2)
    gain_one_sum = gain_part / gain_one
    small_near = jnp.concatenate([inner_high[0], inner_low[0], gain_one_sum[:384, 0], gain_two_sum[:384, 0]])
    small_far = jnp.concatenate([inner_high[0], inner_low[0], gain_one_sum[384:, 0], gain_two_sum[384:, 0]])
    small = small_near + cols_swap(small_far, 1)
    inners, gains = small[: 2 * HALF], small[2 * HALF :].reshape(2, 2, FB)
    small = jnp.concatenate([inners, gains[:, 0].reshape(-1)]) + cols_swap(
        jnp.concatenate([inners, gains[:, 1].reshape(-1)]), 2
    )
    inners, gains = small[: 2 * HALF].reshape(2, 1, HALF), small[2 * HALF :]
    where = jnp.stack([y, core]).astype(jnp.int32)
    low_sel = jnp.concatenate([where, jnp.array([0, 1, 1, 0, 0, 0, 1, 1], jnp.int32)])
    high_sel = jnp.concatenate([where, jnp.array([0, 0, 1, 1, 0, 1, 0, 1], jnp.int32)])
    gain_column = norm_gain_one.reshape(FB, 1)
    outputs = finish_half(
        high_sel, both_near, both_cross, there, near_high, got_high, pair_sent, block_input, scale_high,
        inners[0], gain_column, 1, (), sent_low, slots[3],
    )
    output, grad_x = finish_half(
        low_sel, both_near, both_cross, there, near_low, got_low, pair_got, block_input, scale_low,
        inners[1], gain_column, 0, tuple(outputs),
    )

    lasts = [rows_shift(slots[slot], -slot) for slot in (1, 2, 3)]
    lasts[0] = tie(lasts[0], grad_x)

    def total_of(parts):
        return sum(part.astype(F32) for part in parts).astype(BF)

    joined = jnp.concatenate([total_of([pair_zero[0]] + firsts), total_of([slots[0]] + lasts)], axis=1)
    joined_sent = joined
    joined = dp_sum(two(joined[:FB], cols_swap(joined[FB:], 2)))

    feed_total = dp_sum(feed_sum, grad_x)

    def joined_grad(n):
        return jnp.concatenate(
            [joined[:, n * 128 : (n + 1) * 128], joined[:, 384 + n * HD : 384 + (n + 1) * HD]], axis=1
        )

    gains = tie(gains, grad_x)
    slots = jnp.stack([gains] + [rows_shift(gains, step) for step in (1, 2, 3)])
    slots = slots[jnp.mod(r - jnp.arange(4), 4)]
    gains = dp_sum((slots[0] + slots[1]) + (slots[2] + slots[3]))
    return (
        output,
        grad_x,
        gains[:FB],
        joined_grad(0),
        joined_grad(1),
        joined_grad(2),
        feed_total[:, D : D + FB].T,
        gains[FB:],
        feed_total[:, :D],
        feed_total[:, D + 256 :],
    )


def solution(mesh):
    return jax.shard_map(
        per_device,
        mesh=mesh,
        in_specs=(
            P("cols", ("dp", "rows")),
            P("cols"),
            P("cols", "rows"),
            P("cols", "rows"),
            P("cols", "rows"),
            P("rows", "cols"),
            P("cols"),
            P("cols", "rows"),
            P("cols", "rows"),
            P(("dp", "cols"), None),
            P(("dp", "cols"), None),
            P("cols", ("dp", "rows")),
        ),
        out_specs=(
            P("cols", ("dp", "rows")),
            P("cols", ("dp", "rows")),
            P("cols"),
            P("cols", "rows"),
            P("cols", "rows"),
            P("cols", "rows"),
            P("rows", "cols"),
            P("cols"),
            P("cols", "rows"),
            P("cols", "rows"),
        ),
        check_vma=False,
    )
```

```python
import functools
import math

import jax
import jax.numpy as jnp
from jax import lax
from jax.experimental import pallas as pl
from jax.experimental.pallas import tpu as pltpu
from jax.sharding import PartitionSpec as P


D = 768
HD = 64
LEN = 4096
HALF = 2048
B = 512
FB = 192
FF = 3072
EPSILON = 1e-06
MASKED = -1e30
SCALE = HD**-0.5
LOG2E = math.log2(math.e)
BF = jnp.bfloat16
F32 = jnp.float32
MIB = 1 << 20


def cost(us):
    return pl.CostEstimate(flops=int(us * 1_150_000_000), bytes_accessed=0, transcendentals=0)


def contract(left, right, dims):
    return lax.dot_general(left, right, (dims, ((), ())), preferred_element_type=F32)


def nn(left, right):
    return contract(left, right, ((1,), (0,)))


def nt(left, right):
    return contract(left, right, ((1,), (1,)))


def cols_swap(value, distance):
    return lax.ppermute(value, "cols", [(i, i ^ distance) for i in range(lax.axis_size("cols"))])


def rows_shift(value, step):
    count = lax.axis_size("rows")
    return lax.ppermute(value, "rows", [(i, (i + step) % count) for i in range(count)])


def dp_swap(value):
    return lax.ppermute(value, "dp", [(i, i ^ 1) for i in range(lax.axis_size("dp"))])


ANY = pl.BlockSpec(memory_space=pl.ANY)


def hold_kernel(tab, source, *refs):
    refs[-1][0] = source[...]


def hold(blocks, source, width, *deps):
    count = blocks.shape[0]
    return pl.pallas_call(
        hold_kernel,
        grid_spec=pltpu.PrefetchScalarGridSpec(
            num_scalar_prefetch=1,
            grid=(count,),
            in_specs=[pl.BlockSpec((FB, width), lambda i, t: (0, t[i]))] + [ANY] * len(deps),
            out_specs=pl.BlockSpec((1, FB, width), lambda i, t: (i // 2, 0, i % 2)),
        ),
        out_shape=jax.ShapeDtypeStruct((count // 2, FB, 2 * width), source.dtype),
        cost_estimate=cost(3),
    )(blocks, source, *deps)


def join_kernel(first, second, *refs):
    refs[-1][:, :D] = first[...]
    refs[-1][:, D:] = second[...]


def join(first, second, *deps):
    vmem = pl.BlockSpec(memory_space=pltpu.VMEM)
    return pl.pallas_call(
        join_kernel,
        in_specs=[vmem, vmem] + [ANY] * len(deps),
        out_specs=vmem,
        out_shape=jax.ShapeDtypeStruct((FB, 2 * D), BF),
        cost_estimate=cost(2),
    )(first, second, *deps)


def pack_kernel(q, k, v, out):
    for n, w in enumerate((q, k, v)):
        out[:, n * 128 : (n + 1) * 128] = w[:, :128]
        out[:, 384 + n * HD : 384 + (n + 1) * HD] = w[:, 128:]


def pack(*weights):
    vmem = pl.BlockSpec(memory_space=pltpu.VMEM)
    return pl.pallas_call(
        pack_kernel,
        in_specs=[vmem] * 3,
        out_specs=vmem,
        out_shape=jax.ShapeDtypeStruct((FB, 576), BF),
        cost_estimate=cost(1),
    )(*weights)


def pick_kernel(tab, first, second, out):
    out[0] = first[0]
    out[1] = second[0]


def pick(index, first, second):
    part = pl.BlockSpec((1, *first.shape[1:]), lambda i, t: (t[0], 0, 0))
    shape = (2, *first.shape[1:])
    return pl.pallas_call(
        pick_kernel,
        grid_spec=pltpu.PrefetchScalarGridSpec(
            num_scalar_prefetch=1,
            grid=(1,),
            in_specs=[part, part],
            out_specs=pl.BlockSpec(shape, lambda i, t: (0, 0, 0)),
        ),
        out_shape=jax.ShapeDtypeStruct(shape, first.dtype),
        cost_estimate=cost(1),
    )(index[None].astype(jnp.int32), first, second)


def tie(value, *deps):
    return pl.pallas_call(
        lambda *refs: None,
        in_specs=[ANY] * (1 + len(deps)),
        out_specs=ANY,
        out_shape=jax.ShapeDtypeStruct(value.shape, value.dtype),
        input_output_aliases={0: 0},
        cost_estimate=cost(0),
    )(value, *deps)


def qkv_kernel(tab, *refs, first, extra):
    x0, x1, x2, x3, gain = refs[:5]
    normed, scale, q_t, k, k_t, v, v_t = refs[5 + extra : 12 + extra]
    i = pl.program_id(0)
    if first:
        w = refs[12 + extra]

        @pl.when(i == 0)
        def _():
            w[0:FB, :] = refs[5][0]
            w[FB : 2 * FB, :] = refs[6][0]
            w[2 * FB : 3 * FB, :] = refs[7][0]
            w[3 * FB :, :] = refs[7][1]
    else:
        w = refs[5]
    x = jnp.concatenate([x0[...], x1[...], x2[...], x3[...]], axis=0).astype(F32)
    r1 = lax.rsqrt(jnp.sum(x * x, axis=0, keepdims=True) * (1.0 / D) + EPSILON)
    n_t = (x * r1 * gain[...]).astype(BF)
    normed[...] = n_t
    scale[...] = r1
    n = n_t.T
    for p in range(3):
        first_col = p * 384
        kv = nn(n, w[:, first_col + 128 : first_col + 384])
        cols = slice(p * 128, (p + 1) * 128)
        k[:, cols] = kv[:, :128].astype(BF)
        v[:, cols] = kv[:, 128:].astype(BF)
        kv_t = kv.T.astype(BF)
        k_t[cols, :] = kv_t[:128]
        v_t[cols, :] = kv_t[128:]

    @pl.when(i < 2)
    def _():
        for p in range(3):
            q = nn(n, w[:, p * 384 : p * 384 + 128]) * (SCALE * LOG2E)
            q_t[p * 128 : (p + 1) * 128, :] = q.T.astype(BF)


def project_half(order, x, gain, weights, half, old, deps):
    base = half * (HALF // B)
    first = half == 0

    def cols_of(rows, offset=0):
        return pl.BlockSpec((rows, B), lambda i, t: (0, offset + t[i]))

    whole = lambda shape: pl.BlockSpec(shape, lambda i, t: (0, 0))
    slots = pl.BlockSpec((1, FB, 1152), lambda i, t: (t[4], 0, 0))
    major = pl.BlockSpec((B, 384), lambda i, t: (base + t[i], 0))
    minor = pl.BlockSpec((384, B), lambda i, t: (0, base + t[i]))
    kv = [jax.ShapeDtypeStruct(s, BF) for s in ((LEN, 384), (384, LEN)) * 2]
    cross = pl.BlockSpec((2, FB, 1152), lambda i, t: (0, 0, 0))
    w_specs = [slots, slots, cross] if first else [whole((D, 1152))]
    extra = len(w_specs) + len(old) + len(deps)
    return pl.pallas_call(
        functools.partial(qkv_kernel, first=first, extra=extra),
        grid_spec=pltpu.PrefetchScalarGridSpec(
            num_scalar_prefetch=1,
            grid=(HALF // B,),
            in_specs=[cols_of(FB, base)] + [cols_of(FB)] * 3 + [whole((D, 1))]
            + w_specs
            + [ANY] * (len(old) + len(deps)),
            out_specs=[
                cols_of(D),
                cols_of(1),
                pl.BlockSpec((384, B), lambda i, t: (0, jnp.minimum(i, 1))),
                major,
                minor,
                major,
                minor,
            ]
            + [whole((D, 1152))] * first,
        ),
        out_shape=[
            jax.ShapeDtypeStruct((D, HALF), BF),
            jax.ShapeDtypeStruct((1, HALF), F32),
            jax.ShapeDtypeStruct((384, HALF // 2), BF),
        ]
        + kv
        + [jax.ShapeDtypeStruct((D, 1152), BF)] * first,
        input_output_aliases={6 + len(w_specs) + n: 3 + n for n in range(len(old))},
        compiler_params=pltpu.CompilerParams(vmem_limit_bytes=62 * MIB),
        cost_estimate=cost(12),
    )(order, *x, gain, *weights, *old, *deps)


def block_masks(first, last):
    key = lax.broadcasted_iota(jnp.int32, (B, B), 0)
    query = lax.broadcasted_iota(jnp.int32, (B, B), 1)
    piece = (key >= first) & (key < last) & (query >= first) & (query < last)
    return (key > query, (key <= query) | piece)


def masked(scores, masks, step, count):
    if step == count - 1:
        scores = jnp.where(masks[1], scores, MASKED)
    if count == 4 and step == 0:
        scores = jnp.where(masks[0], scores, MASKED)
    return scores


def head_rows(pair_t):
    row = lax.broadcasted_iota(jnp.int32, pair_t.shape, 0)
    zero = jnp.zeros((), pair_t.dtype)
    return [jnp.where((row // HD) == h, pair_t, zero) for h in range(2)]


def head_cols(pair):
    col = lax.broadcasted_iota(jnp.int32, pair.shape, 1)
    zero = jnp.zeros((), pair.dtype)
    return [jnp.where((col // HD) == h, pair, zero) for h in range(2)]


def for_counts(block, counts, body):
    if len(counts) == 1:
        body(counts[0])
        return
    visible = jnp.minimum(block, 3) + 1
    for count in counts:
        pl.when(visible == count)(functools.partial(body, count))


def attend_kernel(tab, q_t, k, v_t, *refs, counts):
    o_own, o_other, log_total = refs[-3:]
    i = pl.program_id(1)
    block = tab[i]
    first, last = tab[2 + block], tab[10 + block]

    def body(count):
        masks = block_masks(first, last)
        starts = [pl.multiple_of((block - (count - 1) + t) * B, B) for t in range(count)]
        for h, q_head in enumerate(head_rows(q_t[...])):
            scores = [masked(nn(k[pl.ds(s, B), :], q_head), masks, t, count) for t, s in enumerate(starts)]
            peak = functools.reduce(jnp.maximum, [jnp.max(s, axis=0, keepdims=True) for s in scores])
            total, mixed = 0.0, 0.0
            for score, s in zip(scores, starts):
                part = jnp.exp2(score - peak)
                total = total + jnp.sum(part, axis=0, keepdims=True)
                mixed = mixed + nn(v_t[h * HD : (h + 1) * HD, pl.ds(s, B)], part.astype(BF))
            out = (mixed * (1.0 / total)).astype(BF)

            @pl.when(i == 0)
            def _():
                o_own[h * HD : (h + 1) * HD, :] = out

            @pl.when(i == 1)
            def _():
                o_other[h * HD : (h + 1) * HD, :] = out

            log_total[0, h : h + 1, :] = peak + jnp.log2(total)

    for_counts(block, counts, body)


def attend(tab, q_t, k, v_t, half, pairs, old, *deps):
    base, count = pairs
    span = LEN if half else HALF
    one = pl.BlockSpec((128, B), lambda p, i, t: (base + p, 0))
    block = jax.ShapeDtypeStruct((384, B), BF)
    return pl.pallas_call(
        functools.partial(attend_kernel, counts=(4,) if half else (1, 2, 3, 4)),
        grid_spec=pltpu.PrefetchScalarGridSpec(
            num_scalar_prefetch=1,
            grid=(count, 2),
            in_specs=[
                pl.BlockSpec((128, B), lambda p, i, t: (base + p, i)),
                pl.BlockSpec((span, 128), lambda p, i, t: (0, base + p)),
                pl.BlockSpec((128, span), lambda p, i, t: (base + p, 0)),
            ]
            + [ANY] * (len(old) + len(deps)),
            out_specs=[one, one, pl.BlockSpec((1, 2, B), lambda p, i, t: (p, 0, i))],
        ),
        out_shape=[block, block, jax.ShapeDtypeStruct((count, 2, 2 * B), F32)],
        input_output_aliases={4 + n: n for n in range(len(old))},
        compiler_params=pltpu.CompilerParams(vmem_limit_bytes=62 * MIB),
        cost_estimate=cost((8 if half else 6) * count),
    )(tab, q_t, k, v_t, *old, *deps)


def attend_back_kernel(tab, q_t, do_own, do_other, o_own, o_other, log_total, k, v, k_t, *refs, counts, half):
    if half:
        dq_t, high, low, dkv = refs[-4:]
    else:
        start = refs[0]
        dq_t, low, dkv = refs[-3:]
    i = pl.program_id(1)
    block = tab[i]
    first, last = tab[2 + block], tab[10 + block]

    @pl.when(i == 0)
    def _():
        dkv[...] = jnp.zeros_like(dkv) if half else start[0]

    def body(count):
        masks = block_masks(first, last)
        queries, grads = q_t[...], jnp.where(i == 0, do_own[...], do_other[...])
        mixed = jnp.where(i == 0, o_own[...], o_other[...])
        q_rows, g_rows = head_rows(queries), head_rows(grads)
        q_cols, g_cols = head_cols(queries.T), head_cols(grads.T)
        product = grads.astype(F32) * mixed.astype(F32)
        inner = [jnp.sum(product[h * HD : (h + 1) * HD], axis=0, keepdims=True) for h in range(2)]
        dq = [0.0, 0.0]
        for t in range(count):
            rows = pl.ds(pl.multiple_of((block - (count - 1) + t) * B, B), B)
            key_rows, value_rows = k[rows, :], v[rows, :]
            dk_part = dv_part = 0.0
            for h in range(2):
                score = masked(nn(key_rows, q_rows[h]), masks, t, count)
                probs = jnp.exp2(score - log_total[0, h : h + 1, :])
                grad_probs = nn(value_rows, g_rows[h])
                grad_scores = (probs * (grad_probs - inner[h])).astype(BF)
                dv_part = dv_part + nn(probs.astype(BF), g_cols[h])
                dk_part = dk_part + nn(grad_scores, q_cols[h])
                dq[h] = dq[h] + nn(k_t[h * HD : (h + 1) * HD, rows], grad_scores)
            dkv[rows, :128] += dk_part
            dkv[rows, 128:] += dv_part
        for h in range(2):
            dq_t[h * HD : (h + 1) * HD, :] = (dq[h] * SCALE).astype(BF)

    for_counts(block, counts, body)

    @pl.when(i == 1)
    def _():
        target, rows = (high, slice(HALF, LEN)) if half else (low, slice(0, HALF))
        target[0, :, :128] = (dkv[rows, :128] * (1.0 / LOG2E)).astype(BF)
        target[0, :, 128:] = dkv[rows, 128:].astype(BF)
        if half:
            low[0] = dkv[:HALF, :]


def attend_back(tab, q_t, grads, outs, log_total, k, v, k_t, half, pairs, start, *deps):
    base, count = pairs
    one = pl.BlockSpec((128, B), lambda p, i, t: (base + p, 0))
    one_of = pl.BlockSpec((128, B), lambda p, i, t: (base + p, half))
    span = LEN if half else HALF
    query = pl.BlockSpec((128, B), lambda p, i, t: (base + p, i))
    stat = pl.BlockSpec((1, 2, B), lambda p, i, t: (base + p, 0, i))
    major = pl.BlockSpec((span, 128), lambda p, i, t: (0, base + p))
    minor = pl.BlockSpec((128, span), lambda p, i, t: (base + p, 0))
    grad = pl.BlockSpec((1, HALF, 256), lambda p, i, t: (p, 0, 0))
    grad_in = pl.BlockSpec((1, HALF, 256), lambda p, i, t: (base + p, 0, 0))
    return pl.pallas_call(
        functools.partial(attend_back_kernel, counts=(4,) if half else (1, 2, 3, 4), half=half),
        grid_spec=pltpu.PrefetchScalarGridSpec(
            num_scalar_prefetch=1,
            grid=(count, 2),
            in_specs=[query, one_of, one_of, one, one, stat, major, major, minor]
            + [grad_in] * len(start)
            + [ANY] * len(deps),
            out_specs=[pl.BlockSpec((128, B), lambda p, i, t: (p, i)), grad] + [grad] * half,
            scratch_shapes=[pltpu.VMEM((span, 256), F32)],
        ),
        out_shape=[
            jax.ShapeDtypeStruct((count * 128, 2 * B), BF),
            jax.ShapeDtypeStruct((count, HALF, 256), BF),
        ]
        + [jax.ShapeDtypeStruct((count, HALF, 256), F32)] * half,
        compiler_params=pltpu.CompilerParams(vmem_limit_bytes=62 * MIB),
        cost_estimate=cost((16 if half else 12) * count),
    )(tab, q_t, *grads, *outs, log_total, k, v, k_t, *start, *deps)


HEAD_ROWS = ((0, 0, 128), (128, 192, 128), (256, 128, 64), (320, 320, 64))
ROOT = math.sqrt(2.0 / math.pi)


def feed_chunk(up):
    square = up * up
    half = 0.5 + 0.5 * jnp.tanh(up * (ROOT + (ROOT * 0.044715) * square))
    act = (up * half).astype(BF)
    slope = half + (2.0 * up) * (half - half * half) * (ROOT + (3.0 * ROOT * 0.044715) * square)
    return act, slope


def feed_kernel(sel, gain, *refs):
    nears, pairs, crosses = refs[:4], refs[4:8], refs[8:11]
    a_parts, dy_parts, x_parts = refs[11:15], refs[15:18], refs[18:25]
    outs = refs[-28:]
    boths, (ga_own, ga_other, gain_sum) = outs[:4], outs[4:7]
    g_near, g_one, g_rest = outs[7:10]
    outs = outs[2:]
    w_up, w_down, w_out, a_t, dy_t, x_t, n, dy, mid, mlp, gn, stage, stage_out = outs[8:21]
    w_sems, a_sems, in_sems, out_sems, last_sems = outs[21:26]
    core, parity = sel[0], sel[3]

    def start(copies):
        for copy in copies:
            copy.start()

    def wait(copies):
        for copy in copies:
            copy.wait()

    halves = (((0, 768, 0, 0), (768, 896, 1, 0)), ((0, 128, 1, 128), (128, 896, 2, 0)))
    targets = (w_up, w_out, w_down)

    def loads(slot, swapped, kinds):
        count = 0
        copies = []

        def add(source, offset, which_half, rel):
            nonlocal count
            for first, last, which, at in halves[which_half]:
                if which in kinds:
                    copies.append(
                        pltpu.make_async_copy(
                            source.at[:, offset + first : offset + last],
                            targets[which].at[slot, rel * FB : (rel + 1) * FB, at : at + last - first],
                            w_sems.at[slot, count],
                        )
                    )
                count += 1

        for half in range(2):
            add(nears[slot], half * 896, half, 0)
            if slot < 2:
                add(pairs[half ^ swapped].at[slot], 0, half, 1)
                add(crosses[0].at[slot], half * 896, half, 2)
                add(crosses[0].at[slot], 1792 + (half ^ swapped) * 896, half, 3)
            else:
                add(pairs[slot], half * 896, half, 1)
                add(crosses[slot - 1].at[0], half * 896, half, 2)
                add(crosses[slot - 1].at[1], half * 896, half, 3)
        return copies

    def a_loads():
        copies = []
        for half in range(2):
            cols = slice(half * B, (half + 1) * B)
            for side in range(2):
                for source, target, size in HEAD_ROWS:
                    part = a_parts[2 * side + half]
                    copies.append(
                        pltpu.make_async_copy(
                            part.at[source : source + size, :],
                            a_t.at[side * 384 + target : side * 384 + target + size, cols],
                            a_sems.at[len(copies)],
                        )
                    )
        return copies

    def token_loads():
        copies = []

        def add(source, target):
            copies.append(pltpu.make_async_copy(source, target, in_sems.at[len(copies)]))

        for half in range(2):
            cols = slice(half * B, (half + 1) * B)
            place = pl.ds(pl.multiple_of(sel[1 + half] * B, B), B)
            at_whole = pl.ds(pl.multiple_of((sel[1 + half] + 4 * half) * B, B), B)
            add(dy_parts[0].at[:, at_whole], dy_t.at[0:FB, cols])
            add(x_parts[0].at[:, at_whole], x_t.at[0:FB, cols])
            for rel in range(1, 4):
                add(x_parts[half * 3 + rel].at[:, place], x_t.at[rel * FB : (rel + 1) * FB, cols])
        add(dy_parts[1].at[0], dy_t.at[FB : 2 * FB, :])
        add(dy_parts[2].at[0], dy_t.at[2 * FB : 3 * FB, :])
        add(dy_parts[2].at[1], dy_t.at[3 * FB :, :])
        return copies

    def stores(slot):
        far = g_one if slot == 1 else g_rest.at[(0, 0, 1, 2)[slot]]
        copies = []
        for side, target in enumerate((g_near.at[slot], far)):
            for which in range(2):
                copies.append(
                    pltpu.make_async_copy(
                        stage.at[slot % 2, which, pl.ds(side * 384, 384), :],
                        target.at[:, which * 1024 : which * 1024 + D],
                        out_sems.at[slot % 2, side * 2 + which],
                    )
                )
        return copies

    def last_stores(slot):
        far = g_one if slot == 1 else g_rest.at[(0, 0, 1, 2)[slot]]
        return [
            pltpu.make_async_copy(
                stage_out.at[slot, pl.ds(side * 384, 384), :],
                target.at[:, D : D + 256],
                last_sems.at[slot, side],
            )
            for side, target in enumerate((g_near.at[slot], far))
        ]

    start(a_loads())

    def start_weights(kinds):
        for swapped in range(2):

            @pl.when(parity == swapped)
            def _():
                for slot in range(4):
                    start(loads(slot, swapped, kinds))

    start_weights((1,))
    start(token_loads())
    start_weights((0, 2))

    a_t[D:, :] = jnp.zeros((64, a_t.shape[1]), BF)

    def a_rows(slot, count):
        place = lax.rem(slot + 2 * core, 4) * FB
        return pl.ds(pl.multiple_of(place, FB), count)

    wait(token_loads())
    dy[...] = dy_t[...].T
    wait(a_loads())
    for slot in range(4):
        wait(loads(slot, 0, (1,)))
    mixed = nn(w_out[0], a_t[a_rows(0, 256), :])
    for slot in range(1, 4):
        mixed = mixed + nn(w_out[slot], a_t[a_rows(slot, 256), :])
    mid[...] = x_t[...].astype(F32) + mixed
    mlp[...] = mid[...]
    gn[...] = jnp.zeros_like(gn)
    r2 = lax.rsqrt(jnp.sum(mid[...] * mid[...], axis=0, keepdims=True) * (1.0 / D) + EPSILON)
    n_t = x_t
    n_t[...] = (mid[...] * r2 * gain[...]).astype(BF)
    n[...] = n_t[...].T

    def chunk(slot, carry):
        buffer = lax.rem(slot, 2)
        for before in range(2):

            @pl.when(slot == before + 2)
            def _():
                wait(stores(before))

        for now in range(4):

            @pl.when(slot == now)
            def _():
                wait(loads(now, 0, (0, 2)))

        up = nn(n[...], w_up[slot])
        act, slope = feed_chunk(up)
        stage[buffer, 1] = nn(dy_t[...], act).astype(BF)
        mlp[...] += nt(w_down[slot], act)
        grad_up = (nn(dy[...], w_down[slot]) * slope).astype(BF)
        stage[buffer, 0] = nn(n_t[...], grad_up).astype(BF)
        gn[...] += nt(w_up[slot], grad_up)
        for now in range(4):

            @pl.when(slot == now)
            def _():
                start(stores(now))

        return carry

    lax.fori_loop(0, 4, chunk, 0)
    for rel, both in enumerate(boths):
        both[0] = mlp[rel * FB : (rel + 1) * FB].astype(BF)
    weighted = gn[...] * gain[...]
    inner = jnp.sum(mid[...] * weighted, axis=0, keepdims=True)
    cubed = r2 * r2 * r2 * inner * (1.0 / D)
    gm = (dy_t[...].astype(F32) + r2 * weighted - mid[...] * cubed).astype(BF)
    x_t[...] = gm
    for rel, both in enumerate(boths):
        both[1] = gm[rel * FB : (rel + 1) * FB]
    gain_sum[...] = jnp.sum(gn[...] * mid[...] * r2, axis=1, keepdims=True)
    for slot in range(4):
        grad_a = contract(w_out[slot], x_t[...], ((0,), (0,)))[:FB].astype(BF)

        def place(target):
            for to, source, size in HEAD_ROWS:
                if source // FB == slot % 2:
                    target[to : to + size, :] = grad_a[source % FB : source % FB + size]

        pl.when((slot // 2) == core)(functools.partial(place, ga_own))
        pl.when((slot // 2) != core)(functools.partial(place, ga_other))
        part = nt(x_t[...], a_t[a_rows(slot, FB), :])
        stage_out[slot] = jnp.concatenate([part, jnp.zeros((D, 64), F32)], axis=1).astype(BF)
        start(last_stores(slot))
    wait(stores(2))
    wait(stores(3))
    for slot in range(4):
        wait(last_stores(slot))


def feed_forward(sel, gain, nears, pairs, crosses, a_parts, dy_parts, x_parts, *deps):
    count = 2 * B
    vmem = pl.BlockSpec(memory_space=pltpu.VMEM)
    both = jax.ShapeDtypeStruct((2, FB, count), BF)
    heads = jax.ShapeDtypeStruct((384, count), BF)
    inputs = (*nears, *pairs, *crosses, *a_parts, *dy_parts, *x_parts, *deps)
    return pl.pallas_call(
        feed_kernel,
        in_specs=[pl.BlockSpec(memory_space=pltpu.SMEM), vmem] + [ANY] * len(inputs),
        out_specs=[vmem] * 7 + [ANY] * 3,
        out_shape=[both, both, both, both, heads, heads, jax.ShapeDtypeStruct((D, 1), F32)]
        + [jax.ShapeDtypeStruct(shape, BF) for shape in ((4, 384, 1792), (384, 1792), (3, 384, 1792))],
        scratch_shapes=[
            pltpu.VMEM((4, D, D), BF),
            pltpu.VMEM((4, D, D), BF),
            pltpu.VMEM((4, D, 256), BF),
            pltpu.VMEM((D + 64, count), BF),
            pltpu.VMEM((D, count), BF),
            pltpu.VMEM((D, count), BF),
            pltpu.VMEM((count, D), BF),
            pltpu.VMEM((count, D), BF),
            pltpu.VMEM((D, count), F32),
            pltpu.VMEM((D, count), F32),
            pltpu.VMEM((D, count), F32),
            pltpu.VMEM((2, 2, D, D), BF),
            pltpu.VMEM((4, D, 256), BF),
            pltpu.SemaphoreType.DMA((4, 16)),
            pltpu.SemaphoreType.DMA((16,)),
            pltpu.SemaphoreType.DMA((13,)),
            pltpu.SemaphoreType.DMA((2, 4)),
            pltpu.SemaphoreType.DMA((4, 2)),
        ],
        compiler_params=pltpu.CompilerParams(vmem_limit_bytes=62 * MIB),
        cost_estimate=cost(50),
    )(sel, gain, *inputs)


def qkv_back_kernel(tab, w, n_t, *refs, half):
    dq, dkv, start = refs[:3]
    dq, dkv = [dq[p * 128 : (p + 1) * 128, :] for p in range(3)], [dkv[p] for p in range(3)]
    near, far, gain_out, *grads = refs[-4:] if half else refs[-3:]
    i = pl.program_id(0)
    grad_w = grads[0] if half else None

    @pl.when(i == 0)
    def _():
        gain_out[...] = start[...]
        if half:
            grad_w[...] = jnp.zeros_like(grad_w)

    normed = n_t[...]
    if half:
        for p in range(3):
            grad_w[p, :, 128:] += nn(normed, dkv[p])

    def finish(grad):
        near[:384, :] = grad[:384].astype(BF)
        far[:384, :] = grad[384:].astype(BF)
        product = grad * normed.astype(F32)
        inner = jnp.broadcast_to(jnp.sum(product, axis=0, keepdims=True), (16, B)).astype(BF)
        near[384:, :] = inner
        far[384:, :] = inner
        gain_out[...] += jnp.sum(product, axis=1, keepdims=True)

    def key_part():
        total = 0.0
        for p in range(3):
            total = total + nt(w[:, p * 384 + 128 : (p + 1) * 384], dkv[p])
        return total

    @pl.when(i < 2)
    def _():
        total = key_part()
        for p in range(3):
            total = total + nn(w[:, p * 384 : p * 384 + 128], dq[p])
            if half:
                grad_w[p, :, :128] += nt(normed, dq[p])
        finish(total)

    @pl.when(i >= 2)
    def _():
        finish(key_part())


def project_back(order, w, n_t, dq, dkv, half, start, *deps):
    whole = lambda shape: pl.BlockSpec(shape, lambda i, t: (0,) * len(shape))

    def cols_of(rows):
        return pl.BlockSpec((rows, B), lambda i, t: (0, t[i]))

    def own(rows):
        return pl.BlockSpec((rows, B), lambda i, t: (0, jnp.minimum(i, 1)))

    low = jax.ShapeDtypeStruct((400, HALF), BF)
    specs = [own(384), pl.BlockSpec((3, B, 256), lambda i, t: (0, t[i], 0)), whole((D, 1))]
    return pl.pallas_call(
        functools.partial(qkv_back_kernel, half=half),
        grid_spec=pltpu.PrefetchScalarGridSpec(
            num_scalar_prefetch=1,
            grid=(HALF // B,),
            in_specs=[whole((D, 1152)), cols_of(D)] + specs + [ANY] * len(deps),
            out_specs=[cols_of(400), cols_of(400), whole((D, 1))] + [whole((3, D, 384))] * half,
        ),
        out_shape=[low, low, jax.ShapeDtypeStruct((D, 1), F32)]
        + [jax.ShapeDtypeStruct((3, D, 384), F32)] * half,
        compiler_params=pltpu.CompilerParams(vmem_limit_bytes=62 * MIB),
        cost_estimate=cost(15 if half else 10),
    )(order, w, n_t, dq, dkv, start, *deps)


def weights_kernel(tab, n_t, dq_t, dkv, start, *refs):
    near, far = refs[-2:]
    kv = start[0, :, 128:] + nn(n_t[...], dkv[0])
    q = start[0, :, :128]
    for i in range(2):
        q = q + nt(n_t[:, pl.ds(pl.multiple_of(tab[i] * B, B), B)], dq_t[:, i * B : (i + 1) * B])
    near[0, :, :128] = q[:384].astype(BF)
    far[0, :, :128] = q[384:].astype(BF)
    near[0, :, 128:] = kv[:384].astype(BF)
    far[0, :, 128:] = kv[384:].astype(BF)


def weights_back(order, n_t, dq_t, dkv, start, pairs, *deps):
    base, count = pairs
    each = lambda shape, base: pl.BlockSpec((1, *shape), lambda i, t: (base + i, 0, 0))
    part = jax.ShapeDtypeStruct((count, 384, 384), BF)
    return pl.pallas_call(
        weights_kernel,
        grid_spec=pltpu.PrefetchScalarGridSpec(
            num_scalar_prefetch=1,
            grid=(count,),
            in_specs=[
                pl.BlockSpec((D, HALF), lambda i, t: (0, 0)),
                pl.BlockSpec((128, 2 * B), lambda i, t: (i, 0)),
                each((HALF, 256), 0),
                each((D, 384), base),
            ]
            + [ANY] * len(deps),
            out_specs=[each((384, 384), 0)] * 2,
        ),
        out_shape=[part, part],
        compiler_params=pltpu.CompilerParams(vmem_limit_bytes=62 * MIB),
        cost_estimate=cost(2 + 2 * count),
    )(order, n_t, dq_t, dkv, start, *deps)


def finish_kernel(sel, *refs):
    here, cross, there, there_cross = refs[:4]
    near, core_part, pair_part, near_inner, core_inner, pair_inner, x, scale, gain = refs[4:13]
    out, grad_x = refs[-2:]
    i = pl.program_id(0)
    pair, device = sel[2 + i], sel[6 + i]
    same, own = pair == sel[0], device == sel[1]
    mine = jnp.where(own, here[...], cross[...])
    theirs = jnp.where(own, there[...], there_cross[...])
    both = jnp.where(same, mine, theirs)
    out[...] = both[0]
    total = near[...].astype(F32) + core_part[...].astype(F32) + pair_part[...].astype(F32)
    inner = near_inner[:1].astype(F32) + core_inner[:1].astype(F32) + pair_inner[:1].astype(F32)
    r1 = scale[...]
    grad_x[...] = both[1].astype(F32) + r1 * gain[...] * total - x[...].astype(F32) * (r1 * r1 * inner * (1.0 / D))


def finish_half(sel, here, cross, there, there_cross, near, core_part, pair_part, x, scale, gain, half, old, *deps):
    base = half * (HALF // B)
    piece = pl.BlockSpec((2, FB, B), lambda i, t: (0, 0, half))
    cols = pl.BlockSpec((FB, B), lambda i, t: (0, i))
    into = pl.BlockSpec((FB, B), lambda i, t: (0, base + i))
    row = pl.BlockSpec((1, B), lambda i, t: (0, i))
    inner = lambda first: pl.BlockSpec((16, B), lambda i, t: (first // 16, i))
    return pl.pallas_call(
        finish_kernel,
        grid_spec=pltpu.PrefetchScalarGridSpec(
            num_scalar_prefetch=1,
            grid=(HALF // B,),
            in_specs=[
                piece,
                piece,
                piece,
                piece,
                cols,
                cols,
                cols,
                inner(384),
                inner(384),
                inner(FB),
                into,
                row,
                pl.BlockSpec((FB, 1), lambda i, t: (0, 0)),
            ]
            + [ANY] * (len(old) + len(deps)),
            out_specs=[into, into],
        ),
        out_shape=[jax.ShapeDtypeStruct((FB, LEN), BF), jax.ShapeDtypeStruct((FB, LEN), F32)],
        input_output_aliases={14 + n: n for n in range(len(old))},
        cost_estimate=cost(6),
    )(sel, here, cross, there, there_cross, near, core_part, pair_part, near, core_part, pair_part, x, scale, gain, *old, *deps)


def per_device(
    block_input,
    norm_gain_one,
    w_query,
    w_key,
    w_value,
    w_out,
    norm_gain_two,
    w_up,
    w_down,
    piece_start,
    piece_len,
    grad_y,
):
    c = lax.axis_index("cols")
    r = lax.axis_index("rows")
    y, core = c // 2, c % 2
    parity = lax.axis_index("dp") % 2

    def order_of(table):
        return jnp.array(table, jnp.int32)[c]

    low_order = order_of([[0, 3, 1, 2], [3, 0, 1, 2], [1, 2, 0, 3], [2, 1, 0, 3]])
    high_order = order_of([[0, 1, 2, 3], [1, 0, 2, 3], [2, 3, 0, 1], [3, 2, 0, 1]])
    away = order_of([[3, 5, 1, 6, 2, 7], [0, 4, 2, 7, 1, 6], [2, 7, 0, 4, 3, 5], [1, 6, 3, 5, 0, 4]])

    small = jnp.concatenate(
        [norm_gain_one, norm_gain_two, piece_start[0].astype(F32), piece_len[0].astype(F32)]
    )
    small = jnp.stack([small, cols_swap(small, 2)])
    small = jnp.concatenate([small, cols_swap(small, 1)])
    gain_one = small[:, :FB].reshape(D, 1)
    gain_two = small[:, FB : 2 * FB].reshape(D, 1)
    apart = jnp.bitwise_xor(c, r)
    mine = jnp.where(apart == 0, 0, jnp.where(apart == 2, 1, jnp.where(apart == 1, 2, 3)))
    pieces = lax.dynamic_index_in_dim(small, mine, 0, keepdims=False)[2 * FB :].astype(jnp.int32)
    firsts = pieces[:8] - jnp.arange(8, dtype=jnp.int32) * B
    lasts = firsts + pieces[8:]

    def table(order, half):
        blocks = order[:2] + half * 4
        return jnp.concatenate([blocks, firsts, lasts])

    low_table, high_table = table(low_order, 0), table(high_order, 1)
    low_order = jnp.concatenate([low_order, core[None].astype(jnp.int32)])
    high_order = jnp.concatenate([high_order, core[None].astype(jnp.int32)])

    own_low, own_high = block_input[:, :HALF], block_input[:, HALF:]
    w_slots = [pack(w_query, w_key, w_value)]
    w_slots += [rows_shift(w_slots[0], step) for step in (1, 2, 3)]

    def merge(first, second):
        parts = [first[:, :384], second[:, :384]]
        for n in range(3):
            cols = slice(384 + n * HD, 384 + (n + 1) * HD)
            parts += [first[:, cols], second[:, cols]]
        return jnp.concatenate(parts, axis=1)

    w_near = jnp.stack([merge(*w_slots[:2]), merge(*w_slots[2:])])
    pair_low = tie(cols_swap(own_low, 2), w_near)
    x_low = (pair_low, cols_swap(own_low, 1), cols_swap(pair_low, 1))
    own_pack = jnp.concatenate([w_up, w_out.T, jnp.zeros((FB, 64), BF), w_down], axis=1)
    dy_core = hold(away[:2], grad_y, B)
    dy_away = hold(away[2:], grad_y, B)
    ring = [tie(own_pack, w_near)]
    ring.append(rows_shift(ring[0], 1))
    cross_high = cols_swap(own_high, 1)
    w_pair = tie(cols_swap(w_near, 2), x_low[1], x_low[2], dy_core, dy_away, ring[1])
    w_cross = cols_swap(pick(1 - core, w_near, w_pair), 1)
    pair_high = cols_swap(tie(own_high, w_pair), 2)

    normed_low, scale_low, q_low, *kv, w_qkv = project_half(
        low_order, (block_input, *x_low), gain_one, (w_near, w_pair, w_cross), 0, (), ()
    )
    ring.append(rows_shift(ring[1], 1))
    first_sent = jnp.stack(ring[:2])
    first_sent = tie(jnp.where(parity == 0, first_sent[:, :, :896], first_sent[:, :, 896:]), scale_low)
    *out_low, log_first = attend(low_table, q_low, kv[0], kv[3], 0, (0, 1), (), first_sent)
    first_pairs = cols_swap(first_sent, 2)
    ring[2] = tie(ring[2], log_first)
    ring.append(rows_shift(ring[2], 1))
    pair_high = tie(pair_high, log_first)
    *out_low, log_low = attend(low_table, q_low, kv[0], kv[3], 0, (1, 2), out_low, log_first, pair_high, ring[2])
    x_high = (pair_high, cross_high, cols_swap(pair_high, 1))
    low_got = cols_swap(out_low[1], 1)
    dy_sent, third_sent = tie(dy_away, log_low), tie(ring[2], log_low)
    ring[2] = third_sent
    normed_high, scale_high, q_high, *kv = project_half(
        high_order, (block_input, *x_high), gain_one, (w_qkv,), 1, tuple(kv), (log_low, first_pairs)
    )
    k, k_t, v, v_t = kv
    first_crossed = dp_swap(first_pairs)
    dy_pair = cols_swap(dy_sent, 2)
    third_pair = cols_swap(third_sent, 2)
    *out_high, log_other = attend(high_table, q_high, k, v_t, 1, (0, 1), (), low_got)
    ring[3] = tie(ring[3], log_other)
    dy_pair, third_pair = tie(dy_pair, log_other), tie(third_pair, log_other)
    first_crossed = tie(first_crossed, log_other)
    dy_cross_sent = jnp.concatenate([dy_core, dy_pair[1:]])
    third_cross_sent = jnp.stack([ring[2], third_pair])
    *out_high, log_high = attend(
        high_table, q_high, k, v_t, 1, (1, 2), out_high, log_other, ring[3], dy_cross_sent, third_cross_sent
    )
    dy_cross = cols_swap(dy_cross_sent, 1)
    third_cross = cols_swap(third_cross_sent, 1)
    first_cross = cols_swap(jnp.concatenate([jnp.stack(ring[:2]), first_pairs, first_crossed], axis=2), 1)
    last_pair = tie(cols_swap(ring[3], 2), log_high)
    last_cross = cols_swap(jnp.stack([ring[3], last_pair]), 1)
    high_got = cols_swap(out_high[1], 1)
    log_low, log_high = jnp.concatenate([log_first, log_low]), jnp.concatenate([log_other, log_high])

    sel = jnp.stack([core.astype(jnp.int32), low_order[0], high_order[0], parity.astype(jnp.int32)])
    *boths, ga_own, ga_other, gain_two_sum, g_near, g_one, g_rest = feed_forward(
        sel,
        gain_two,
        ring,
        (first_pairs, first_crossed, third_pair, last_pair),
        (first_cross, third_cross, last_cross),
        (out_low[0], out_high[0], low_got, high_got),
        (grad_y, dy_pair, dy_cross),
        (block_input, *x_low, *x_high),
    )

    def three(first, second, third):
        return (first.astype(F32) + second.astype(F32) + third.astype(F32)).astype(BF)

    def two(first, second):
        return (first.astype(F32) + second.astype(F32)).astype(BF)

    ga_got = cols_swap(ga_other, 1)
    total = two(g_near[1], cols_swap(g_one, 1))
    crosses = [cols_swap(both, 1) for both in boths[2:]]
    g_got = cols_swap(g_rest, 1)
    grads = (ga_own, ga_got)
    dq_high, dkv_high, dkv_low = attend_back(
        high_table, q_high, grads, out_high, log_high, k, v, k_t, 1, (0, 3), (), total, *crosses
    )
    theres = [cols_swap(boths[1], 2), cols_swap(crosses[1], 2)]
    total = three(tie(rows_shift(total, 1), dq_high), g_near[2], g_got[1])
    near_high, far_high, gain_part, w_part = project_back(
        high_order, w_qkv, normed_high, dq_high, dkv_high, 1, jnp.zeros((D, 1), F32), total, *theres
    )
    got_high = cols_swap(far_high, 1)
    dq_low, dkv_low = attend_back(
        low_table, q_low, grads, out_low, log_low, k, v, k_t, 0, (0, 3), (dkv_low,), near_high
    )
    got_high = tie(got_high, dq_low)
    sent_high = two(near_high[FB:], got_high[FB:])
    total = three(tie(rows_shift(total, 1), sent_high), g_near[3], g_got[2])
    pair_sent = cols_swap(sent_high, 2)
    wg_near, wg_far = weights_back(low_order, normed_low, dq_low, dkv_low, w_part, (0, 3), sent_high, total)
    near_low, far_low, gain_part = project_back(
        low_order, w_qkv, normed_low, dq_low, dkv_low, 0, gain_part, wg_near, pair_sent
    )

    wg_got = tie(cols_swap(wg_far, 1), near_low)
    by_core = jnp.where(core == 0, wg_near, wg_got), jnp.where(core == 0, wg_got, wg_near)

    def split(values):
        high = lax.reduce_precision(values, 8, 7)
        middle = lax.reduce_precision(values - high, 8, 7)
        parts = [high, middle, values - high - middle, jnp.zeros((values.shape[0], 58), F32)]
        return jnp.concatenate(parts, axis=1).astype(BF)

    def unsplit(columns):
        columns = columns.astype(F32)
        return columns[:, 576:578] + columns[:, 578:580] + columns[:, 580:582]

    gains = jnp.concatenate([gain_part / gain_one, gain_two_sum], axis=1).T
    gains = split((gains[:, :384] + cols_swap(gains[:, 384:], 1)).T)

    def slot_of(slot):
        part = by_core[slot // 2]
        which = slot % 2
        last = [part[2, :, n * 128 + which * HD : n * 128 + (which + 1) * HD] for n in range(3)]
        return jnp.concatenate([part[which]] + last + [gains], axis=1)

    slots = [slot_of(slot) for slot in range(4)]
    got_low = tie(cols_swap(far_low, 1), wg_near)
    sent_low = two(near_low[FB:], got_low[FB:])
    total = three(tie(rows_shift(total, 1), near_low), g_near[0], g_got[0])

    def dp_sum(part, *deps):
        if lax.axis_size("dp") == 2:
            got = dp_swap(part)
            got = tie(got, *deps) if deps else got
            return part.astype(F32) + got.astype(F32)
        return lax.psum(part.astype(F32), "dp")

    pair_got = cols_swap(sent_low, 2)
    feed_sum = two(total[:FB], cols_swap(total[FB:], 2))
    parts = [slots[0]] + [rows_shift(slots[slot], -slot) for slot in (1, 2, 3)]
    parts[1] = tie(parts[1], pair_got, total)
    joined = sum(part[:, :576].astype(F32) for part in parts).astype(BF)
    shares = [unsplit(part) for part in parts]

    def share_of(row):
        slot = jnp.mod(r - row, 4)
        last = jnp.where(slot == 2, shares[2], shares[3])
        return jnp.where(slot == 0, shares[0], jnp.where(slot == 1, shares[1], last))

    shares = [share_of(row) for row in range(4)]
    gains = (shares[0] + shares[1]) + (shares[2] + shares[3])
    joined_sent = jnp.concatenate([joined[FB:], split(gains[FB:])], axis=1)
    joined_got = cols_swap(joined_sent, 2)
    joined_pair = jnp.concatenate(
        [two(joined[:FB], joined_got[:, :576]), split(gains[:FB] + unsplit(joined_got))], axis=1
    )

    where = jnp.stack([y, core]).astype(jnp.int32)
    low_sel = jnp.concatenate([where, jnp.array([0, 1, 1, 0, 0, 0, 1, 1], jnp.int32)])
    high_sel = jnp.concatenate([where, jnp.array([0, 0, 1, 1, 0, 1, 0, 1], jnp.int32)])
    gain_column = norm_gain_one.reshape(FB, 1)
    outputs = finish_half(
        high_sel, boths[0], crosses[0], *theres, near_high, got_high, pair_sent, block_input, scale_high,
        gain_column, 1, (), joined_sent,
    )
    output, grad_x = finish_half(
        low_sel, boths[0], crosses[0], *theres, near_low, got_low, pair_got, block_input, scale_low,
        gain_column, 0, tuple(outputs), joined_pair, feed_sum,
    )

    joined = dp_sum(joined_pair)
    gains = unsplit(joined)
    feed_total = dp_sum(feed_sum, grad_x)

    def joined_grad(n):
        return jnp.concatenate(
            [joined[:, n * 128 : (n + 1) * 128], joined[:, 384 + n * HD : 384 + (n + 1) * HD]], axis=1
        )

    return (
        output,
        grad_x,
        gains[:, 0],
        joined_grad(0),
        joined_grad(1),
        joined_grad(2),
        feed_total[:, D : D + FB].T,
        gains[:, 1],
        feed_total[:, :D],
        feed_total[:, D + 256 :],
    )


def solution(mesh):
    return jax.shard_map(
        per_device,
        mesh=mesh,
        in_specs=(
            P("cols", ("dp", "rows")),
            P("cols"),
            P("cols", "rows"),
            P("cols", "rows"),
            P("cols", "rows"),
            P("rows", "cols"),
            P("cols"),
            P("cols", "rows"),
            P("cols", "rows"),
            P(("dp", "cols"), None),
            P(("dp", "cols"), None),
            P("cols", ("dp", "rows")),
        ),
        out_specs=(
            P("cols", ("dp", "rows")),
            P("cols", ("dp", "rows")),
            P("cols"),
            P("cols", "rows"),
            P("cols", "rows"),
            P("cols", "rows"),
            P("rows", "cols"),
            P("cols"),
            P("cols", "rows"),
            P("cols", "rows"),
        ),
        check_vma=False,
    )
```

```python
import functools
import math

import jax
import jax.numpy as jnp
from jax import lax
from jax.experimental import pallas as pl
from jax.experimental.pallas import tpu as pltpu
from jax.sharding import PartitionSpec as P


D = 768
HD = 64
LEN = 4096
HALF = 2048
B = 512
FB = 192
FF = 3072
EPSILON = 1e-06
MASKED = -1e30
SCALE = HD**-0.5
LOG2E = math.log2(math.e)
BF = jnp.bfloat16
F32 = jnp.float32
MIB = 1 << 20


def cost(us):
    return pl.CostEstimate(flops=int(us * 1_150_000_000), bytes_accessed=0, transcendentals=0)


def contract(left, right, dims):
    return lax.dot_general(left, right, (dims, ((), ())), preferred_element_type=F32)


def nn(left, right):
    return contract(left, right, ((1,), (0,)))


def nt(left, right):
    return contract(left, right, ((1,), (1,)))


def cols_swap(value, distance):
    return lax.ppermute(value, "cols", [(i, i ^ distance) for i in range(lax.axis_size("cols"))])


def rows_shift(value, step):
    count = lax.axis_size("rows")
    return lax.ppermute(value, "rows", [(i, (i + step) % count) for i in range(count)])


def dp_swap(value):
    return lax.ppermute(value, "dp", [(i, i ^ 1) for i in range(lax.axis_size("dp"))])


ANY = pl.BlockSpec(memory_space=pl.ANY)


def hold_kernel(tab, source, *refs):
    refs[-1][0] = source[...]


def hold(blocks, source, width, *deps):
    count = blocks.shape[0]
    return pl.pallas_call(
        hold_kernel,
        grid_spec=pltpu.PrefetchScalarGridSpec(
            num_scalar_prefetch=1,
            grid=(count,),
            in_specs=[pl.BlockSpec((FB, width), lambda i, t: (0, t[i]))] + [ANY] * len(deps),
            out_specs=pl.BlockSpec((1, FB, width), lambda i, t: (i // 2, 0, i % 2)),
        ),
        out_shape=jax.ShapeDtypeStruct((count // 2, FB, 2 * width), source.dtype),
        cost_estimate=cost(3),
    )(blocks, source, *deps)


def join_kernel(first, second, *refs):
    refs[-1][:, :D] = first[...]
    refs[-1][:, D:] = second[...]


def join(first, second, *deps):
    vmem = pl.BlockSpec(memory_space=pltpu.VMEM)
    return pl.pallas_call(
        join_kernel,
        in_specs=[vmem, vmem] + [ANY] * len(deps),
        out_specs=vmem,
        out_shape=jax.ShapeDtypeStruct((FB, 2 * D), BF),
        cost_estimate=cost(2),
    )(first, second, *deps)


def pack_kernel(q, k, v, out):
    for n, w in enumerate((q, k, v)):
        out[:, n * 128 : (n + 1) * 128] = w[:, :128]
        out[:, 384 + n * HD : 384 + (n + 1) * HD] = w[:, 128:]


def pack(*weights):
    vmem = pl.BlockSpec(memory_space=pltpu.VMEM)
    return pl.pallas_call(
        pack_kernel,
        in_specs=[vmem] * 3,
        out_specs=vmem,
        out_shape=jax.ShapeDtypeStruct((FB, 576), BF),
        cost_estimate=cost(1),
    )(*weights)


def pick_kernel(tab, first, second, out):
    out[0] = first[0]
    out[1] = second[0]


def pick(index, first, second):
    part = pl.BlockSpec((1, *first.shape[1:]), lambda i, t: (t[0], 0, 0))
    shape = (2, *first.shape[1:])
    return pl.pallas_call(
        pick_kernel,
        grid_spec=pltpu.PrefetchScalarGridSpec(
            num_scalar_prefetch=1,
            grid=(1,),
            in_specs=[part, part],
            out_specs=pl.BlockSpec(shape, lambda i, t: (0, 0, 0)),
        ),
        out_shape=jax.ShapeDtypeStruct(shape, first.dtype),
        cost_estimate=cost(1),
    )(index[None].astype(jnp.int32), first, second)


def tie(value, *deps):
    return pl.pallas_call(
        lambda *refs: None,
        in_specs=[ANY] * (1 + len(deps)),
        out_specs=ANY,
        out_shape=jax.ShapeDtypeStruct(value.shape, value.dtype),
        input_output_aliases={0: 0},
        cost_estimate=cost(0),
    )(value, *deps)


def qkv_kernel(tab, *refs, first, extra):
    x0, x1, x2, x3, gain = refs[:5]
    normed, scale, q_t, k, k_t, v, v_t = refs[5 + extra : 12 + extra]
    i = pl.program_id(0)
    if first:
        w = refs[12 + extra]

        @pl.when(i == 0)
        def _():
            w[0:FB, :] = refs[5][0]
            w[FB : 2 * FB, :] = refs[6][0]
            w[2 * FB : 3 * FB, :] = refs[7][0]
            w[3 * FB :, :] = refs[7][1]
    else:
        w = refs[5]
    x = jnp.concatenate([x0[...], x1[...], x2[...], x3[...]], axis=0).astype(F32)
    r1 = lax.rsqrt(jnp.sum(x * x, axis=0, keepdims=True) * (1.0 / D) + EPSILON)
    n_t = (x * r1 * gain[...]).astype(BF)
    normed[...] = n_t
    scale[...] = r1
    n = n_t.T
    for p in range(3):
        first_col = p * 384
        kv = nn(n, w[:, first_col + 128 : first_col + 384])
        cols = slice(p * 128, (p + 1) * 128)
        k[:, cols] = kv[:, :128].astype(BF)
        v[:, cols] = kv[:, 128:].astype(BF)
        kv_t = kv.T.astype(BF)
        k_t[cols, :] = kv_t[:128]
        v_t[cols, :] = kv_t[128:]

    @pl.when(i < 2)
    def _():
        for p in range(3):
            q = nn(n, w[:, p * 384 : p * 384 + 128]) * (SCALE * LOG2E)
            q_t[p * 128 : (p + 1) * 128, :] = q.T.astype(BF)


def project_half(order, x, gain, weights, half, old, deps):
    base = half * (HALF // B)
    first = half == 0

    def cols_of(rows, offset=0):
        return pl.BlockSpec((rows, B), lambda i, t: (0, offset + t[i]))

    whole = lambda shape: pl.BlockSpec(shape, lambda i, t: (0, 0))
    slots = pl.BlockSpec((1, FB, 1152), lambda i, t: (t[4], 0, 0))
    major = pl.BlockSpec((B, 384), lambda i, t: (base + t[i], 0))
    minor = pl.BlockSpec((384, B), lambda i, t: (0, base + t[i]))
    kv = [jax.ShapeDtypeStruct(s, BF) for s in ((LEN, 384), (384, LEN)) * 2]
    cross = pl.BlockSpec((2, FB, 1152), lambda i, t: (0, 0, 0))
    w_specs = [slots, slots, cross] if first else [whole((D, 1152))]
    extra = len(w_specs) + len(old) + len(deps)
    return pl.pallas_call(
        functools.partial(qkv_kernel, first=first, extra=extra),
        grid_spec=pltpu.PrefetchScalarGridSpec(
            num_scalar_prefetch=1,
            grid=(HALF // B,),
            in_specs=[cols_of(FB, base)] + [cols_of(FB)] * 3 + [whole((D, 1))]
            + w_specs
            + [ANY] * (len(old) + len(deps)),
            out_specs=[
                cols_of(D),
                cols_of(1),
                pl.BlockSpec((384, B), lambda i, t: (0, jnp.minimum(i, 1))),
                major,
                minor,
                major,
                minor,
            ]
            + [whole((D, 1152))] * first,
        ),
        out_shape=[
            jax.ShapeDtypeStruct((D, HALF), BF),
            jax.ShapeDtypeStruct((1, HALF), F32),
            jax.ShapeDtypeStruct((384, HALF // 2), BF),
        ]
        + kv
        + [jax.ShapeDtypeStruct((D, 1152), BF)] * first,
        input_output_aliases={6 + len(w_specs) + n: 3 + n for n in range(len(old))},
        compiler_params=pltpu.CompilerParams(vmem_limit_bytes=62 * MIB),
        cost_estimate=cost(12),
    )(order, *x, gain, *weights, *old, *deps)


def block_masks(first, last):
    key = lax.broadcasted_iota(jnp.int32, (B, B), 0)
    query = lax.broadcasted_iota(jnp.int32, (B, B), 1)
    piece = (key >= first) & (key < last) & (query >= first) & (query < last)
    return (key > query, (key <= query) | piece)


def masked(scores, masks, step, count):
    if step == count - 1:
        scores = jnp.where(masks[1], scores, MASKED)
    if count == 4 and step == 0:
        scores = jnp.where(masks[0], scores, MASKED)
    return scores


def head_rows(pair_t):
    row = lax.broadcasted_iota(jnp.int32, pair_t.shape, 0)
    zero = jnp.zeros((), pair_t.dtype)
    return [jnp.where((row // HD) == h, pair_t, zero) for h in range(2)]


def head_cols(pair):
    col = lax.broadcasted_iota(jnp.int32, pair.shape, 1)
    zero = jnp.zeros((), pair.dtype)
    return [jnp.where((col // HD) == h, pair, zero) for h in range(2)]


def for_counts(block, counts, body):
    if len(counts) == 1:
        body(counts[0])
        return
    visible = jnp.minimum(block, 3) + 1
    for count in counts:
        pl.when(visible == count)(functools.partial(body, count))


def attend_kernel(tab, q_t, k, v_t, *refs, counts):
    o_own, o_other, log_total = refs[-3:]
    i = pl.program_id(1)
    block = tab[i]
    first, last = tab[2 + block], tab[10 + block]

    def body(count):
        masks = block_masks(first, last)
        starts = [pl.multiple_of((block - (count - 1) + t) * B, B) for t in range(count)]
        for h, q_head in enumerate(head_rows(q_t[...])):
            scores = [masked(nn(k[pl.ds(s, B), :], q_head), masks, t, count) for t, s in enumerate(starts)]
            peak = functools.reduce(jnp.maximum, [jnp.max(s, axis=0, keepdims=True) for s in scores])
            total, mixed = 0.0, 0.0
            for score, s in zip(scores, starts):
                part = jnp.exp2(score - peak)
                total = total + jnp.sum(part, axis=0, keepdims=True)
                mixed = mixed + nn(v_t[h * HD : (h + 1) * HD, pl.ds(s, B)], part.astype(BF))
            out = (mixed * (1.0 / total)).astype(BF)

            @pl.when(i == 0)
            def _():
                o_own[h * HD : (h + 1) * HD, :] = out

            @pl.when(i == 1)
            def _():
                o_other[h * HD : (h + 1) * HD, :] = out

            log_total[0, h : h + 1, :] = peak + jnp.log2(total)

    for_counts(block, counts, body)


def attend(tab, q_t, k, v_t, half, pairs, old, *deps):
    base, count = pairs
    span = LEN if half else HALF
    one = pl.BlockSpec((128, B), lambda p, i, t: (base + p, 0))
    block = jax.ShapeDtypeStruct((384, B), BF)
    return pl.pallas_call(
        functools.partial(attend_kernel, counts=(4,) if half else (1, 2, 3, 4)),
        grid_spec=pltpu.PrefetchScalarGridSpec(
            num_scalar_prefetch=1,
            grid=(count, 2),
            in_specs=[
                pl.BlockSpec((128, B), lambda p, i, t: (base + p, i)),
                pl.BlockSpec((span, 128), lambda p, i, t: (0, base + p)),
                pl.BlockSpec((128, span), lambda p, i, t: (base + p, 0)),
            ]
            + [ANY] * (len(old) + len(deps)),
            out_specs=[one, one, pl.BlockSpec((1, 2, B), lambda p, i, t: (p, 0, i))],
        ),
        out_shape=[block, block, jax.ShapeDtypeStruct((count, 2, 2 * B), F32)],
        input_output_aliases={4 + n: n for n in range(len(old))},
        compiler_params=pltpu.CompilerParams(vmem_limit_bytes=62 * MIB),
        cost_estimate=cost((8 if half else 6) * count),
    )(tab, q_t, k, v_t, *old, *deps)


def attend_back_kernel(tab, q_t, do_own, do_other, o_own, o_other, log_total, k, v, k_t, *refs, counts, half):
    if half:
        dq_t, high, low, dkv = refs[-4:]
    else:
        start = refs[0]
        dq_t, low, dkv = refs[-3:]
    i = pl.program_id(1)
    block = tab[i]
    first, last = tab[2 + block], tab[10 + block]

    @pl.when(i == 0)
    def _():
        dkv[...] = jnp.zeros_like(dkv) if half else start[0]

    def body(count):
        masks = block_masks(first, last)
        queries, grads = q_t[...], jnp.where(i == 0, do_own[...], do_other[...])
        mixed = jnp.where(i == 0, o_own[...], o_other[...])
        q_rows, g_rows = head_rows(queries), head_rows(grads)
        q_cols, g_cols = head_cols(queries.T), head_cols(grads.T)
        product = grads.astype(F32) * mixed.astype(F32)
        inner = [jnp.sum(product[h * HD : (h + 1) * HD], axis=0, keepdims=True) for h in range(2)]
        dq = [0.0, 0.0]
        for t in range(count):
            rows = pl.ds(pl.multiple_of((block - (count - 1) + t) * B, B), B)
            key_rows, value_rows = k[rows, :], v[rows, :]
            dk_part = dv_part = 0.0
            for h in range(2):
                score = masked(nn(key_rows, q_rows[h]), masks, t, count)
                probs = jnp.exp2(score - log_total[0, h : h + 1, :])
                grad_probs = nn(value_rows, g_rows[h])
                grad_scores = (probs * (grad_probs - inner[h])).astype(BF)
                dv_part = dv_part + nn(probs.astype(BF), g_cols[h])
                dk_part = dk_part + nn(grad_scores, q_cols[h])
                dq[h] = dq[h] + nn(k_t[h * HD : (h + 1) * HD, rows], grad_scores)
            dkv[rows, :128] += dk_part
            dkv[rows, 128:] += dv_part
        for h in range(2):
            dq_t[h * HD : (h + 1) * HD, :] = (dq[h] * SCALE).astype(BF)

    for_counts(block, counts, body)

    @pl.when(i == 1)
    def _():
        target, rows = (high, slice(HALF, LEN)) if half else (low, slice(0, HALF))
        target[0, :, :128] = (dkv[rows, :128] * (1.0 / LOG2E)).astype(BF)
        target[0, :, 128:] = dkv[rows, 128:].astype(BF)
        if half:
            low[0] = dkv[:HALF, :]


def attend_back(tab, q_t, grads, outs, log_total, k, v, k_t, half, pairs, start, *deps):
    base, count = pairs
    one = pl.BlockSpec((128, B), lambda p, i, t: (base + p, 0))
    one_of = pl.BlockSpec((128, B), lambda p, i, t: (base + p, half))
    span = LEN if half else HALF
    query = pl.BlockSpec((128, B), lambda p, i, t: (base + p, i))
    stat = pl.BlockSpec((1, 2, B), lambda p, i, t: (base + p, 0, i))
    major = pl.BlockSpec((span, 128), lambda p, i, t: (0, base + p))
    minor = pl.BlockSpec((128, span), lambda p, i, t: (base + p, 0))
    grad = pl.BlockSpec((1, HALF, 256), lambda p, i, t: (p, 0, 0))
    grad_in = pl.BlockSpec((1, HALF, 256), lambda p, i, t: (base + p, 0, 0))
    return pl.pallas_call(
        functools.partial(attend_back_kernel, counts=(4,) if half else (1, 2, 3, 4), half=half),
        grid_spec=pltpu.PrefetchScalarGridSpec(
            num_scalar_prefetch=1,
            grid=(count, 2),
            in_specs=[query, one_of, one_of, one, one, stat, major, major, minor]
            + [grad_in] * len(start)
            + [ANY] * len(deps),
            out_specs=[pl.BlockSpec((128, B), lambda p, i, t: (p, i)), grad] + [grad] * half,
            scratch_shapes=[pltpu.VMEM((span, 256), F32)],
        ),
        out_shape=[
            jax.ShapeDtypeStruct((count * 128, 2 * B), BF),
            jax.ShapeDtypeStruct((count, HALF, 256), BF),
        ]
        + [jax.ShapeDtypeStruct((count, HALF, 256), F32)] * half,
        compiler_params=pltpu.CompilerParams(vmem_limit_bytes=62 * MIB),
        cost_estimate=cost((16 if half else 12) * count),
    )(tab, q_t, *grads, *outs, log_total, k, v, k_t, *start, *deps)


HEAD_ROWS = ((0, 0, 128), (128, 192, 128), (256, 128, 64), (320, 320, 64))
ROOT = math.sqrt(2.0 / math.pi)


def feed_chunk(up):
    square = up * up
    half = 0.5 + 0.5 * jnp.tanh(up * (ROOT + (ROOT * 0.044715) * square))
    act = (up * half).astype(BF)
    slope = half + (2.0 * up) * (half - half * half) * (ROOT + (3.0 * ROOT * 0.044715) * square)
    return act, slope


def feed_kernel(sel, gain, *refs):
    nears, pairs, crosses = refs[:4], refs[4:8], refs[8:12]
    a_parts, dy_parts, x_parts = refs[12:16], refs[16:19], refs[19:26]
    outs = refs[-28:]
    boths, (ga_own, ga_other, gain_sum) = outs[:4], outs[4:7]
    g_near, g_one, g_rest = outs[7:10]
    outs = outs[2:]
    w_up, w_down, w_out, a_t, dy_t, x_t, n, dy, mid, mlp, gn, stage, stage_out = outs[8:21]
    w_sems, a_sems, in_sems, out_sems, last_sems = outs[21:26]
    core, parity = sel[0], sel[3]

    def start(copies):
        for copy in copies:
            copy.start()

    def wait(copies):
        for copy in copies:
            copy.wait()

    halves = (((0, 768, 0, 0), (768, 896, 1, 0)), ((0, 128, 1, 128), (128, 896, 2, 0)))
    targets = (w_up, w_out, w_down)

    def loads(slot, swapped, kinds):
        count = 0
        copies = []

        def add(source, offset, which_half, rel):
            nonlocal count
            for first, last, which, at in halves[which_half]:
                if which in kinds:
                    rows = slice(rel * FB, (rel + 1) * FB)
                    if which == 1:
                        target = w_out.at[rows, slot * 256 + at : slot * 256 + at + last - first]
                    else:
                        target = targets[which].at[slot, rows, at : at + last - first]
                    copies.append(
                        pltpu.make_async_copy(source.at[:, offset + first : offset + last], target, w_sems.at[slot, count])
                    )
                count += 1

        for half in range(2):
            add(nears[slot], half * 896, half, 0)
            if slot < 2:
                add(pairs[half ^ swapped].at[slot], 0, half, 1)
                add(crosses[0].at[slot], half * 896, half, 2)
                add(crosses[0].at[slot], 1792 + (half ^ swapped) * 896, half, 3)
            else:
                add(pairs[slot], half * 896, half, 1)
                near, pair = (crosses[1].at[0], crosses[1].at[1]) if slot == 2 else crosses[2:]
                add(near, half * 896, half, 2)
                add(pair, half * 896, half, 3)
        return copies

    def a_loads():
        copies = []
        for half in range(2):
            cols = slice(half * B, (half + 1) * B)
            for side in range(2):
                first_row = 512 * (core if side == 0 else 1 - core)
                for source, target, size in HEAD_ROWS:
                    at = pl.multiple_of(first_row + target // FB * 256 + target % FB, 64)
                    copies.append(
                        pltpu.make_async_copy(
                            a_parts[2 * side + half].at[source : source + size, :],
                            a_t.at[pl.ds(at, size), cols],
                            a_sems.at[len(copies)],
                        )
                    )
        return copies

    def token_loads(group):
        copies = []

        def add(source, target):
            copies.append(pltpu.make_async_copy(source, target, in_sems.at[group, len(copies)]))

        for half in range(2):
            cols = slice(half * B, (half + 1) * B)
            place = pl.ds(pl.multiple_of(sel[1 + half] * B, B), B)
            at_whole = pl.ds(pl.multiple_of((sel[1 + half] + 4 * half) * B, B), B)
            if group:
                add(dy_parts[0].at[:, at_whole], dy_t.at[0:FB, cols])
                continue
            add(x_parts[0].at[:, at_whole], x_t.at[0:FB, cols])
            for rel in range(1, 4):
                add(x_parts[half * 3 + rel].at[:, place], x_t.at[rel * FB : (rel + 1) * FB, cols])
        if group:
            add(dy_parts[1].at[0], dy_t.at[FB : 2 * FB, :])
            add(dy_parts[2].at[0], dy_t.at[2 * FB : 3 * FB, :])
            add(dy_parts[2].at[1], dy_t.at[3 * FB :, :])
        return copies

    def stores(slot):
        far = g_one if slot == 1 else g_rest.at[(0, 0, 1, 2)[slot]]
        copies = []
        for side, target in enumerate((g_near.at[slot], far)):
            for which in range(2):
                copies.append(
                    pltpu.make_async_copy(
                        stage.at[slot % 2, which, pl.ds(side * 384, 384), :],
                        target.at[:, which * 1024 : which * 1024 + D],
                        out_sems.at[slot % 2, side * 2 + which],
                    )
                )
        return copies

    def last_stores(slot):
        far = g_one if slot == 1 else g_rest.at[(0, 0, 1, 2)[slot]]
        return [
            pltpu.make_async_copy(
                stage_out.at[pl.ds(side * 384, 384), slot * 256 : (slot + 1) * 256],
                target.at[:, D : D + 256],
                last_sems.at[slot, side],
            )
            for side, target in enumerate((g_near.at[slot], far))
        ]

    start(a_loads())

    def start_weights(kinds):
        for swapped in range(2):

            @pl.when(parity == swapped)
            def _():
                for slot in range(4):
                    start(loads(slot, swapped, kinds))

    start_weights((1,))
    start(token_loads(0))
    for slot in range(4):
        a_t[slot * 256 + FB : (slot + 1) * 256, :] = jnp.zeros((64, a_t.shape[1]), BF)
    wait(a_loads())
    for slot in range(4):
        wait(loads(slot, 0, (1,)))
    wait(token_loads(0))
    start(token_loads(1))
    start_weights((0, 2))
    mid[...] = x_t[...].astype(F32) + nn(w_out[...], a_t[...])
    mlp[...] = mid[...]
    gn[...] = jnp.zeros_like(gn)
    r2 = lax.rsqrt(jnp.sum(mid[...] * mid[...], axis=0, keepdims=True) * (1.0 / D) + EPSILON)
    n_t = x_t
    n_t[...] = (mid[...] * r2 * gain[...]).astype(BF)
    n[...] = n_t[...].T
    wait(token_loads(1))
    dy[...] = dy_t[...].T

    def chunk(slot, carry):
        buffer = lax.rem(slot, 2)
        for before in range(2):

            @pl.when(slot == before + 2)
            def _():
                wait(stores(before))

        for now in range(4):

            @pl.when(slot == now)
            def _():
                wait(loads(now, 0, (0, 2)))

        up = nn(n[...], w_up[slot])
        act, slope = feed_chunk(up)
        stage[buffer, 1] = nn(dy_t[...], act).astype(BF)
        mlp[...] += nt(w_down[slot], act)
        grad_up = (nn(dy[...], w_down[slot]) * slope).astype(BF)
        stage[buffer, 0] = nn(n_t[...], grad_up).astype(BF)
        gn[...] += nt(w_up[slot], grad_up)
        for now in range(4):

            @pl.when(slot == now)
            def _():
                start(stores(now))

        return carry

    lax.fori_loop(0, 4, chunk, 0)
    for rel, both in enumerate(boths):
        both[0] = mlp[rel * FB : (rel + 1) * FB].astype(BF)
    weighted = gn[...] * gain[...]
    inner = jnp.sum(mid[...] * weighted, axis=0, keepdims=True)
    cubed = r2 * r2 * r2 * inner * (1.0 / D)
    gm = (dy_t[...].astype(F32) + r2 * weighted - mid[...] * cubed).astype(BF)
    x_t[...] = gm
    for rel, both in enumerate(boths):
        both[1] = gm[rel * FB : (rel + 1) * FB]
    gain_sum[...] = jnp.sum(gn[...] * mid[...] * r2, axis=1, keepdims=True)
    stage_out[...] = nt(x_t[...], a_t[...]).astype(BF)
    for slot in range(4):
        start(last_stores(slot))
    grad_a = contract(w_out[...], x_t[...], ((0,), (0,))).astype(BF)
    for slot in range(4):

        def place(target):
            for to, source, size in HEAD_ROWS:
                if source // FB == slot % 2:
                    row = slot * 256 + source % FB
                    target[to : to + size, :] = grad_a[row : row + size]

        pl.when((slot // 2) == core)(functools.partial(place, ga_own))
        pl.when((slot // 2) != core)(functools.partial(place, ga_other))
    wait(stores(2))
    wait(stores(3))
    for slot in range(4):
        wait(last_stores(slot))


def feed_forward(sel, gain, nears, pairs, crosses, a_parts, dy_parts, x_parts, *deps):
    count = 2 * B
    vmem = pl.BlockSpec(memory_space=pltpu.VMEM)
    both = jax.ShapeDtypeStruct((2, FB, count), BF)
    heads = jax.ShapeDtypeStruct((384, count), BF)
    inputs = (*nears, *pairs, *crosses, *a_parts, *dy_parts, *x_parts, *deps)
    return pl.pallas_call(
        feed_kernel,
        in_specs=[pl.BlockSpec(memory_space=pltpu.SMEM), vmem] + [ANY] * len(inputs),
        out_specs=[vmem] * 7 + [ANY] * 3,
        out_shape=[both, both, both, both, heads, heads, jax.ShapeDtypeStruct((D, 1), F32)]
        + [jax.ShapeDtypeStruct(shape, BF) for shape in ((4, 384, 1792), (384, 1792), (3, 384, 1792))],
        scratch_shapes=[
            pltpu.VMEM((4, D, D), BF),
            pltpu.VMEM((4, D, D), BF),
            pltpu.VMEM((D, 1024), BF),
            pltpu.VMEM((1024, count), BF),
            pltpu.VMEM((D, count), BF),
            pltpu.VMEM((D, count), BF),
            pltpu.VMEM((count, D), BF),
            pltpu.VMEM((count, D), BF),
            pltpu.VMEM((D, count), F32),
            pltpu.VMEM((D, count), F32),
            pltpu.VMEM((D, count), F32),
            pltpu.VMEM((2, 2, D, D), BF),
            pltpu.VMEM((D, 1024), BF),
            pltpu.SemaphoreType.DMA((4, 16)),
            pltpu.SemaphoreType.DMA((16,)),
            pltpu.SemaphoreType.DMA((2, 8)),
            pltpu.SemaphoreType.DMA((2, 4)),
            pltpu.SemaphoreType.DMA((4, 2)),
        ],
        compiler_params=pltpu.CompilerParams(vmem_limit_bytes=62 * MIB),
        cost_estimate=cost(50),
    )(sel, gain, *inputs)


def qkv_back_kernel(tab, w, n_t, *refs, half):
    dq, dkv, start = refs[:3]
    dq, dkv = [dq[p * 128 : (p + 1) * 128, :] for p in range(3)], [dkv[p] for p in range(3)]
    near, far, gain_out, *grads = refs[-4:] if half else refs[-3:]
    i = pl.program_id(0)
    grad_w = grads[0] if half else None

    @pl.when(i == 0)
    def _():
        gain_out[...] = start[...]
        if half:
            grad_w[...] = jnp.zeros_like(grad_w)

    normed = n_t[...]
    if half:
        for p in range(3):
            grad_w[p, :, 128:] += nn(normed, dkv[p])

    def finish(grad):
        near[:384, :] = grad[:384].astype(BF)
        far[:384, :] = grad[384:].astype(BF)
        product = grad * normed.astype(F32)
        inner = jnp.broadcast_to(jnp.sum(product, axis=0, keepdims=True), (16, B)).astype(BF)
        near[384:, :] = inner
        far[384:, :] = inner
        gain_out[...] += jnp.sum(product, axis=1, keepdims=True)

    def key_part():
        total = 0.0
        for p in range(3):
            total = total + nt(w[:, p * 384 + 128 : (p + 1) * 384], dkv[p])
        return total

    @pl.when(i < 2)
    def _():
        total = key_part()
        for p in range(3):
            total = total + nn(w[:, p * 384 : p * 384 + 128], dq[p])
            if half:
                grad_w[p, :, :128] += nt(normed, dq[p])
        finish(total)

    @pl.when(i >= 2)
    def _():
        finish(key_part())


def project_back(order, w, n_t, dq, dkv, half, start, *deps):
    whole = lambda shape: pl.BlockSpec(shape, lambda i, t: (0,) * len(shape))

    def cols_of(rows):
        return pl.BlockSpec((rows, B), lambda i, t: (0, t[i]))

    def own(rows):
        return pl.BlockSpec((rows, B), lambda i, t: (0, jnp.minimum(i, 1)))

    low = jax.ShapeDtypeStruct((400, HALF), BF)
    specs = [own(384), pl.BlockSpec((3, B, 256), lambda i, t: (0, t[i], 0)), whole((D, 1))]
    return pl.pallas_call(
        functools.partial(qkv_back_kernel, half=half),
        grid_spec=pltpu.PrefetchScalarGridSpec(
            num_scalar_prefetch=1,
            grid=(HALF // B,),
            in_specs=[whole((D, 1152)), cols_of(D)] + specs + [ANY] * len(deps),
            out_specs=[cols_of(400), cols_of(400), whole((D, 1))] + [whole((3, D, 384))] * half,
        ),
        out_shape=[low, low, jax.ShapeDtypeStruct((D, 1), F32)]
        + [jax.ShapeDtypeStruct((3, D, 384), F32)] * half,
        compiler_params=pltpu.CompilerParams(vmem_limit_bytes=62 * MIB),
        cost_estimate=cost(15 if half else 10),
    )(order, w, n_t, dq, dkv, start, *deps)


def weights_kernel(tab, n_t, dq_t, dkv, start, *refs):
    near, far = refs[-2:]
    kv = start[0, :, 128:] + nn(n_t[...], dkv[0])
    q = start[0, :, :128]
    for i in range(2):
        q = q + nt(n_t[:, pl.ds(pl.multiple_of(tab[i] * B, B), B)], dq_t[:, i * B : (i + 1) * B])
    near[0, :, :128] = q[:384].astype(BF)
    far[0, :, :128] = q[384:].astype(BF)
    near[0, :, 128:] = kv[:384].astype(BF)
    far[0, :, 128:] = kv[384:].astype(BF)


def weights_back(order, n_t, dq_t, dkv, start, pairs, *deps):
    base, count = pairs
    each = lambda shape, base: pl.BlockSpec((1, *shape), lambda i, t: (base + i, 0, 0))
    part = jax.ShapeDtypeStruct((count, 384, 384), BF)
    return pl.pallas_call(
        weights_kernel,
        grid_spec=pltpu.PrefetchScalarGridSpec(
            num_scalar_prefetch=1,
            grid=(count,),
            in_specs=[
                pl.BlockSpec((D, HALF), lambda i, t: (0, 0)),
                pl.BlockSpec((128, 2 * B), lambda i, t: (i, 0)),
                each((HALF, 256), 0),
                each((D, 384), base),
            ]
            + [ANY] * len(deps),
            out_specs=[each((384, 384), 0)] * 2,
        ),
        out_shape=[part, part],
        compiler_params=pltpu.CompilerParams(vmem_limit_bytes=62 * MIB),
        cost_estimate=cost(2 + 2 * count),
    )(order, n_t, dq_t, dkv, start, *deps)


def finish_kernel(sel, *refs):
    here, cross, there, there_cross = refs[:4]
    near, core_part, pair_part, near_inner, core_inner, pair_inner, x, scale, gain = refs[4:13]
    out, grad_x = refs[-2:]
    i = pl.program_id(0)
    pair, device = sel[2 + i], sel[6 + i]
    same, own = pair == sel[0], device == sel[1]
    mine = jnp.where(own, here[...], cross[...])
    theirs = jnp.where(own, there[...], there_cross[...])
    both = jnp.where(same, mine, theirs)
    out[...] = both[0]
    total = near[...].astype(F32) + core_part[...].astype(F32) + pair_part[...].astype(F32)
    inner = near_inner[:1].astype(F32) + core_inner[:1].astype(F32) + pair_inner[:1].astype(F32)
    r1 = scale[...]
    grad_x[...] = both[1].astype(F32) + r1 * gain[...] * total - x[...].astype(F32) * (r1 * r1 * inner * (1.0 / D))


def finish_half(sel, here, cross, there, there_cross, near, core_part, pair_part, x, scale, gain, half, old, *deps):
    base = half * (HALF // B)
    piece = pl.BlockSpec((2, FB, B), lambda i, t: (0, 0, half))
    cols = pl.BlockSpec((FB, B), lambda i, t: (0, i))
    into = pl.BlockSpec((FB, B), lambda i, t: (0, base + i))
    row = pl.BlockSpec((1, B), lambda i, t: (0, i))
    inner = lambda first: pl.BlockSpec((16, B), lambda i, t: (first // 16, i))
    return pl.pallas_call(
        finish_kernel,
        grid_spec=pltpu.PrefetchScalarGridSpec(
            num_scalar_prefetch=1,
            grid=(HALF // B,),
            in_specs=[
                piece,
                piece,
                piece,
                piece,
                cols,
                cols,
                cols,
                inner(384),
                inner(384),
                inner(FB),
                into,
                row,
                pl.BlockSpec((FB, 1), lambda i, t: (0, 0)),
            ]
            + [ANY] * (len(old) + len(deps)),
            out_specs=[into, into],
        ),
        out_shape=[jax.ShapeDtypeStruct((FB, LEN), BF), jax.ShapeDtypeStruct((FB, LEN), F32)],
        input_output_aliases={14 + n: n for n in range(len(old))},
        cost_estimate=cost(6),
    )(sel, here, cross, there, there_cross, near, core_part, pair_part, near, core_part, pair_part, x, scale, gain, *old, *deps)


def per_device(
    block_input,
    norm_gain_one,
    w_query,
    w_key,
    w_value,
    w_out,
    norm_gain_two,
    w_up,
    w_down,
    piece_start,
    piece_len,
    grad_y,
):
    c = lax.axis_index("cols")
    r = lax.axis_index("rows")
    y, core = c // 2, c % 2
    parity = lax.axis_index("dp") % 2

    def order_of(table):
        return jnp.array(table, jnp.int32)[c]

    low_order = order_of([[0, 3, 1, 2], [3, 0, 1, 2], [1, 2, 0, 3], [2, 1, 0, 3]])
    high_order = order_of([[0, 1, 2, 3], [1, 0, 2, 3], [2, 3, 0, 1], [3, 2, 0, 1]])
    away = order_of([[3, 5, 1, 6, 2, 7], [0, 4, 2, 7, 1, 6], [2, 7, 0, 4, 3, 5], [1, 6, 3, 5, 0, 4]])

    small = jnp.concatenate(
        [norm_gain_one, norm_gain_two, piece_start[0].astype(F32), piece_len[0].astype(F32)]
    )
    small = jnp.stack([small, cols_swap(small, 2)])
    small = jnp.concatenate([small, cols_swap(small, 1)])
    gain_one = small[:, :FB].reshape(D, 1)
    gain_two = small[:, FB : 2 * FB].reshape(D, 1)
    apart = jnp.bitwise_xor(c, r)
    mine = jnp.where(apart == 0, 0, jnp.where(apart == 2, 1, jnp.where(apart == 1, 2, 3)))
    pieces = lax.dynamic_index_in_dim(small, mine, 0, keepdims=False)[2 * FB :].astype(jnp.int32)
    firsts = pieces[:8] - jnp.arange(8, dtype=jnp.int32) * B
    lasts = firsts + pieces[8:]

    def table(order, half):
        blocks = order[:2] + half * 4
        return jnp.concatenate([blocks, firsts, lasts])

    low_table, high_table = table(low_order, 0), table(high_order, 1)
    low_order = jnp.concatenate([low_order, core[None].astype(jnp.int32)])
    high_order = jnp.concatenate([high_order, core[None].astype(jnp.int32)])

    own_low, own_high = block_input[:, :HALF], block_input[:, HALF:]
    w_slots = [pack(w_query, w_key, w_value)]
    w_slots += [rows_shift(w_slots[0], step) for step in (1, 2, 3)]

    def merge(first, second):
        parts = [first[:, :384], second[:, :384]]
        for n in range(3):
            cols = slice(384 + n * HD, 384 + (n + 1) * HD)
            parts += [first[:, cols], second[:, cols]]
        return jnp.concatenate(parts, axis=1)

    w_near = jnp.stack([merge(*w_slots[:2]), merge(*w_slots[2:])])
    pair_low = tie(cols_swap(own_low, 2), w_near)
    x_low = (pair_low, cols_swap(tie(own_low, w_near), 1), cols_swap(pair_low, 1))
    own_pack = jnp.concatenate([w_up, w_out.T, jnp.zeros((FB, 64), BF), w_down], axis=1)
    dy_core = hold(away[:2], grad_y, B)
    dy_away = hold(away[2:], grad_y, B)
    ring = [tie(own_pack, w_near)]
    ring.append(rows_shift(ring[0], 1))
    cross_high = cols_swap(own_high, 1)
    w_pair = tie(cols_swap(w_near, 2), x_low[1], x_low[2], dy_core, dy_away, ring[1])
    w_cross = cols_swap(pick(1 - core, w_near, w_pair), 1)
    pair_high = cols_swap(tie(own_high, w_pair), 2)

    normed_low, scale_low, q_low, *kv, w_qkv = project_half(
        low_order, (block_input, *x_low), gain_one, (w_near, w_pair, w_cross), 0, (), ()
    )
    ring.append(rows_shift(ring[1], 1))
    first_sent = jnp.stack(ring[:2])
    first_sent = tie(jnp.where(parity == 0, first_sent[:, :, :896], first_sent[:, :, 896:]), scale_low)
    *out_low, log_first = attend(low_table, q_low, kv[0], kv[3], 0, (0, 1), (), first_sent)
    first_pairs = cols_swap(first_sent, 2)
    ring[2] = tie(ring[2], log_first)
    ring.append(rows_shift(ring[2], 1))
    pair_high = tie(pair_high, log_first)
    *out_low, log_low = attend(low_table, q_low, kv[0], kv[3], 0, (1, 2), out_low, log_first, pair_high, ring[2])
    x_high = (pair_high, cross_high, cols_swap(pair_high, 1))
    low_got = cols_swap(out_low[1], 1)
    dy_sent, third_sent = tie(dy_away, log_low), tie(ring[2], log_low)
    ring[2] = third_sent
    normed_high, scale_high, q_high, *kv = project_half(
        high_order, (block_input, *x_high), gain_one, (w_qkv,), 1, tuple(kv), (log_low, first_pairs)
    )
    k, k_t, v, v_t = kv
    first_crossed = dp_swap(first_pairs)
    dy_pair = cols_swap(dy_sent, 2)
    third_pair = cols_swap(third_sent, 2)
    *out_high, log_other = attend(high_table, q_high, k, v_t, 1, (0, 1), (), low_got)
    ring[3] = tie(ring[3], log_other)
    dy_pair, third_pair = tie(dy_pair, log_other), tie(third_pair, log_other)
    first_crossed = tie(first_crossed, log_other)
    dy_cross_sent = jnp.concatenate([dy_core, dy_pair[1:]])
    third_cross_sent = jnp.stack([ring[2], third_pair])
    *out_high, log_high = attend(
        high_table, q_high, k, v_t, 1, (1, 2), out_high, log_other, ring[3], dy_cross_sent, third_cross_sent
    )
    dy_cross = cols_swap(dy_cross_sent, 1)
    third_cross = cols_swap(third_cross_sent, 1)
    first_cross = cols_swap(jnp.concatenate([jnp.stack(ring[:2]), first_pairs, first_crossed], axis=2), 1)
    last_cross = cols_swap(ring[3], 1)
    last_pair = tie(cols_swap(ring[3], 2), log_high)
    last_cross = (last_cross, cols_swap(last_pair, 1))
    high_got = cols_swap(out_high[1], 1)
    log_low, log_high = jnp.concatenate([log_first, log_low]), jnp.concatenate([log_other, log_high])

    sel = jnp.stack([core.astype(jnp.int32), low_order[0], high_order[0], parity.astype(jnp.int32)])
    *boths, ga_own, ga_other, gain_two_sum, g_near, g_one, g_rest = feed_forward(
        sel,
        gain_two,
        ring,
        (first_pairs, first_crossed, third_pair, last_pair),
        (first_cross, third_cross, *last_cross),
        (out_low[0], out_high[0], low_got, high_got),
        (grad_y, dy_pair, dy_cross),
        (block_input, *x_low, *x_high),
    )

    def three(first, second, third):
        return (first.astype(F32) + second.astype(F32) + third.astype(F32)).astype(BF)

    def two(first, second):
        return (first.astype(F32) + second.astype(F32)).astype(BF)

    ga_got = cols_swap(ga_other, 1)
    total = two(g_near[1], cols_swap(g_one, 1))
    crosses = [cols_swap(both, 1) for both in boths[2:]]
    g_got = cols_swap(g_rest, 1)
    grads = (ga_own, ga_got)
    dq_high, dkv_high, dkv_low = attend_back(
        high_table, q_high, grads, out_high, log_high, k, v, k_t, 1, (0, 3), (), total, *crosses
    )
    theres = [cols_swap(boths[1], 2), cols_swap(crosses[1], 2)]
    total = three(tie(rows_shift(total, 1), dq_high), g_near[2], g_got[1])
    near_high, far_high, gain_part, w_part = project_back(
        high_order, w_qkv, normed_high, dq_high, dkv_high, 1, jnp.zeros((D, 1), F32), total, *theres
    )
    got_high = cols_swap(far_high, 1)
    dq_low, dkv_low = attend_back(
        low_table, q_low, grads, out_low, log_low, k, v, k_t, 0, (0, 3), (dkv_low,), near_high
    )
    got_high = tie(got_high, dq_low)
    sent_high = two(near_high[FB:], got_high[FB:])
    total = three(tie(rows_shift(total, 1), sent_high), g_near[3], g_got[2])
    pair_sent = cols_swap(sent_high, 2)
    wg_near, wg_far = weights_back(low_order, normed_low, dq_low, dkv_low, w_part, (0, 3), sent_high, total)
    near_low, far_low, gain_part = project_back(
        low_order, w_qkv, normed_low, dq_low, dkv_low, 0, gain_part, wg_near, pair_sent
    )

    ring_got = tie(rows_shift(total, 1), near_low)
    wg_got = tie(cols_swap(wg_far, 1), near_low, ring_got)
    by_core = jnp.where(core == 0, wg_near, wg_got), jnp.where(core == 0, wg_got, wg_near)

    def split(values):
        high = lax.reduce_precision(values, 8, 7)
        middle = lax.reduce_precision(values - high, 8, 7)
        parts = [high, middle, values - high - middle, jnp.zeros((values.shape[0], 58), F32)]
        return jnp.concatenate(parts, axis=1).astype(BF)

    def unsplit(columns):
        columns = columns[:, 576:582].astype(F32)
        return columns[:, :2] + columns[:, 2:4] + columns[:, 4:]

    gains = jnp.concatenate([gain_part / gain_one, gain_two_sum], axis=1).T
    gains = split((gains[:, :384] + cols_swap(gains[:, 384:], 1)).T)

    def slot_of(slot):
        part = by_core[slot // 2]
        which = slot % 2
        last = [part[2, :, n * 128 + which * HD : n * 128 + (which + 1) * HD] for n in range(3)]
        return jnp.concatenate([part[which]] + last + [gains], axis=1)

    slots = [slot_of(slot) for slot in range(4)]
    got_low = tie(cols_swap(far_low, 1), wg_near)
    sent_low = two(near_low[FB:], got_low[FB:])
    total = three(ring_got, g_near[0], g_got[0])

    def dp_sum(part, *deps):
        if lax.axis_size("dp") == 2:
            got = dp_swap(part)
            got = tie(got, *deps) if deps else got
            return part.astype(F32) + got.astype(F32)
        return lax.psum(part.astype(F32), "dp")

    pair_got = cols_swap(sent_low, 2)
    feed_sum = two(total[:FB], cols_swap(total[FB:], 2))
    parts = [slots[0]] + [rows_shift(slots[slot], -slot) for slot in (1, 2, 3)]
    parts[1] = tie(parts[1], pair_got, total)
    joined = sum(part[:, :576].astype(F32) for part in parts).astype(BF)
    shares = [unsplit(part) for part in parts]

    def share_of(row):
        slot = jnp.mod(r - row, 4)
        last = jnp.where(slot == 2, shares[2], shares[3])
        return jnp.where(slot == 0, shares[0], jnp.where(slot == 1, shares[1], last))

    shares = [share_of(row) for row in range(4)]
    gains = (shares[0] + shares[1]) + (shares[2] + shares[3])
    joined_sent = jnp.concatenate([joined[FB:], split(gains[FB:])], axis=1)
    joined_got = cols_swap(joined_sent, 2)
    joined_pair = jnp.concatenate(
        [two(joined[:FB], joined_got[:, :576]), split(gains[:FB] + unsplit(joined_got))], axis=1
    )

    where = jnp.stack([y, core]).astype(jnp.int32)
    low_sel = jnp.concatenate([where, jnp.array([0, 1, 1, 0, 0, 0, 1, 1], jnp.int32)])
    high_sel = jnp.concatenate([where, jnp.array([0, 0, 1, 1, 0, 1, 0, 1], jnp.int32)])
    gain_column = norm_gain_one.reshape(FB, 1)
    outputs = finish_half(
        high_sel, boths[0], crosses[0], *theres, near_high, got_high, pair_sent, block_input, scale_high,
        gain_column, 1, (), joined_sent,
    )
    output, grad_x = finish_half(
        low_sel, boths[0], crosses[0], *theres, near_low, got_low, pair_got, block_input, scale_low,
        gain_column, 0, tuple(outputs), joined_pair, feed_sum,
    )

    joined = dp_sum(joined_pair)
    gains = unsplit(joined)
    feed_total = dp_sum(feed_sum, grad_x)

    def joined_grad(n):
        return jnp.concatenate(
            [joined[:, n * 128 : (n + 1) * 128], joined[:, 384 + n * HD : 384 + (n + 1) * HD]], axis=1
        )

    return (
        output,
        grad_x,
        gains[:, 0],
        joined_grad(0),
        joined_grad(1),
        joined_grad(2),
        feed_total[:, D : D + FB].T,
        gains[:, 1],
        feed_total[:, :D],
        feed_total[:, D + 256 :],
    )


def solution(mesh):
    return jax.shard_map(
        per_device,
        mesh=mesh,
        in_specs=(
            P("cols", ("dp", "rows")),
            P("cols"),
            P("cols", "rows"),
            P("cols", "rows"),
            P("cols", "rows"),
            P("rows", "cols"),
            P("cols"),
            P("cols", "rows"),
            P("cols", "rows"),
            P(("dp", "cols"), None),
            P(("dp", "cols"), None),
            P("cols", ("dp", "rows")),
        ),
        out_specs=(
            P("cols", ("dp", "rows")),
            P("cols", ("dp", "rows")),
            P("cols"),
            P("cols", "rows"),
            P("cols", "rows"),
            P("cols", "rows"),
            P("rows", "cols"),
            P("cols"),
            P("cols", "rows"),
            P("cols", "rows"),
        ),
        check_vma=False,
    )
```

```python
import functools
import math

import jax
import jax.numpy as jnp
from jax import lax
from jax.experimental import pallas as pl
from jax.experimental.pallas import tpu as pltpu
from jax.sharding import PartitionSpec as P


D = 768
HD = 64
LEN = 4096
HALF = 2048
B = 512
FB = 192
FF = 3072
EPSILON = 1e-06
MASKED = -1e30
SCALE = HD**-0.5
LOG2E = math.log2(math.e)
BF = jnp.bfloat16
F32 = jnp.float32
MIB = 1 << 20


def cost(us):
    return pl.CostEstimate(flops=int(us * 1_150_000_000), bytes_accessed=0, transcendentals=0)


def contract(left, right, dims):
    return lax.dot_general(left, right, (dims, ((), ())), preferred_element_type=F32)


def nn(left, right):
    return contract(left, right, ((1,), (0,)))


def nt(left, right):
    return contract(left, right, ((1,), (1,)))


def cols_swap(value, distance):
    return lax.ppermute(value, "cols", [(i, i ^ distance) for i in range(lax.axis_size("cols"))])


def rows_shift(value, step):
    count = lax.axis_size("rows")
    return lax.ppermute(value, "rows", [(i, (i + step) % count) for i in range(count)])


def dp_swap(value):
    return lax.ppermute(value, "dp", [(i, i ^ 1) for i in range(lax.axis_size("dp"))])


ANY = pl.BlockSpec(memory_space=pl.ANY)


def hold_kernel(tab, source, *refs):
    refs[-1][0] = source[...]


def hold(blocks, source, width, *deps):
    count = blocks.shape[0]
    return pl.pallas_call(
        hold_kernel,
        grid_spec=pltpu.PrefetchScalarGridSpec(
            num_scalar_prefetch=1,
            grid=(count,),
            in_specs=[pl.BlockSpec((FB, width), lambda i, t: (0, t[i]))] + [ANY] * len(deps),
            out_specs=pl.BlockSpec((1, FB, width), lambda i, t: (i // 2, 0, i % 2)),
        ),
        out_shape=jax.ShapeDtypeStruct((count // 2, FB, 2 * width), source.dtype),
        cost_estimate=cost(3),
    )(blocks, source, *deps)


def join_kernel(first, second, *refs):
    refs[-1][:, :D] = first[...]
    refs[-1][:, D:] = second[...]


def join(first, second, *deps):
    vmem = pl.BlockSpec(memory_space=pltpu.VMEM)
    return pl.pallas_call(
        join_kernel,
        in_specs=[vmem, vmem] + [ANY] * len(deps),
        out_specs=vmem,
        out_shape=jax.ShapeDtypeStruct((FB, 2 * D), BF),
        cost_estimate=cost(2),
    )(first, second, *deps)


def pack_kernel(q, k, v, out):
    for n, w in enumerate((q, k, v)):
        out[:, n * 128 : (n + 1) * 128] = w[:, :128]
        out[:, 384 + n * HD : 384 + (n + 1) * HD] = w[:, 128:]


def pack(*weights):
    vmem = pl.BlockSpec(memory_space=pltpu.VMEM)
    return pl.pallas_call(
        pack_kernel,
        in_specs=[vmem] * 3,
        out_specs=vmem,
        out_shape=jax.ShapeDtypeStruct((FB, 576), BF),
        cost_estimate=cost(1),
    )(*weights)


def pick_kernel(tab, first, second, out):
    out[0] = first[0]
    out[1] = second[0]


def pick(index, first, second):
    part = pl.BlockSpec((1, *first.shape[1:]), lambda i, t: (t[0], 0, 0))
    shape = (2, *first.shape[1:])
    return pl.pallas_call(
        pick_kernel,
        grid_spec=pltpu.PrefetchScalarGridSpec(
            num_scalar_prefetch=1,
            grid=(1,),
            in_specs=[part, part],
            out_specs=pl.BlockSpec(shape, lambda i, t: (0, 0, 0)),
        ),
        out_shape=jax.ShapeDtypeStruct(shape, first.dtype),
        cost_estimate=cost(1),
    )(index[None].astype(jnp.int32), first, second)


def tie(value, *deps):
    return pl.pallas_call(
        lambda *refs: None,
        in_specs=[ANY] * (1 + len(deps)),
        out_specs=ANY,
        out_shape=jax.ShapeDtypeStruct(value.shape, value.dtype),
        input_output_aliases={0: 0},
        cost_estimate=cost(0),
    )(value, *deps)


def qkv_kernel(tab, *refs, first, extra):
    x0, x1, x2, x3, gain = refs[:5]
    normed, scale, q_t, k, k_t, v, v_t = refs[5 + extra : 12 + extra]
    i = pl.program_id(0)
    if first:
        w = refs[12 + extra]

        @pl.when(i == 0)
        def _():
            w[0:FB, :] = refs[5][0]
            w[FB : 2 * FB, :] = refs[6][0]
            w[2 * FB : 3 * FB, :] = refs[7][0]
            w[3 * FB :, :] = refs[7][1]
    else:
        w = refs[5]
    x = jnp.concatenate([x0[...], x1[...], x2[...], x3[...]], axis=0).astype(F32)
    r1 = lax.rsqrt(jnp.sum(x * x, axis=0, keepdims=True) * (1.0 / D) + EPSILON)
    n_t = (x * r1 * gain[...]).astype(BF)
    normed[...] = n_t
    scale[...] = r1
    n = n_t.T
    for p in range(3):
        first_col = p * 384
        kv = nn(n, w[:, first_col + 128 : first_col + 384])
        cols = slice(p * 128, (p + 1) * 128)
        k[:, cols] = kv[:, :128].astype(BF)
        v[:, cols] = kv[:, 128:].astype(BF)
        kv_t = kv.T.astype(BF)
        k_t[cols, :] = kv_t[:128]
        v_t[cols, :] = kv_t[128:]

    @pl.when(i < 2)
    def _():
        for p in range(3):
            q = nn(n, w[:, p * 384 : p * 384 + 128]) * (SCALE * LOG2E)
            q_t[p * 128 : (p + 1) * 128, :] = q.T.astype(BF)


def project_half(order, x, gain, weights, half, old, deps):
    base = half * (HALF // B)
    first = half == 0

    def cols_of(rows, offset=0):
        return pl.BlockSpec((rows, B), lambda i, t: (0, offset + t[i]))

    whole = lambda shape: pl.BlockSpec(shape, lambda i, t: (0, 0))
    slots = pl.BlockSpec((1, FB, 1152), lambda i, t: (t[4], 0, 0))
    major = pl.BlockSpec((B, 384), lambda i, t: (base + t[i], 0))
    minor = pl.BlockSpec((384, B), lambda i, t: (0, base + t[i]))
    kv = [jax.ShapeDtypeStruct(s, BF) for s in ((LEN, 384), (384, LEN)) * 2]
    cross = pl.BlockSpec((2, FB, 1152), lambda i, t: (0, 0, 0))
    w_specs = [slots, slots, cross] if first else [whole((D, 1152))]
    extra = len(w_specs) + len(old) + len(deps)
    return pl.pallas_call(
        functools.partial(qkv_kernel, first=first, extra=extra),
        grid_spec=pltpu.PrefetchScalarGridSpec(
            num_scalar_prefetch=1,
            grid=(HALF // B,),
            in_specs=[cols_of(FB, base)] + [cols_of(FB)] * 3 + [whole((D, 1))]
            + w_specs
            + [ANY] * (len(old) + len(deps)),
            out_specs=[
                cols_of(D),
                cols_of(1),
                pl.BlockSpec((384, B), lambda i, t: (0, jnp.minimum(i, 1))),
                major,
                minor,
                major,
                minor,
            ]
            + [whole((D, 1152))] * first,
        ),
        out_shape=[
            jax.ShapeDtypeStruct((D, HALF), BF),
            jax.ShapeDtypeStruct((1, HALF), F32),
            jax.ShapeDtypeStruct((384, HALF // 2), BF),
        ]
        + kv
        + [jax.ShapeDtypeStruct((D, 1152), BF)] * first,
        input_output_aliases={6 + len(w_specs) + n: 3 + n for n in range(len(old))},
        compiler_params=pltpu.CompilerParams(vmem_limit_bytes=62 * MIB),
        cost_estimate=cost(12),
    )(order, *x, gain, *weights, *old, *deps)


def block_masks(first, last):
    key = lax.broadcasted_iota(jnp.int32, (B, B), 0)
    query = lax.broadcasted_iota(jnp.int32, (B, B), 1)
    piece = (key >= first) & (key < last) & (query >= first) & (query < last)
    return (key > query, (key <= query) | piece)


def masked(scores, masks, step, count):
    if step == count - 1:
        scores = jnp.where(masks[1], scores, MASKED)
    if count == 4 and step == 0:
        scores = jnp.where(masks[0], scores, MASKED)
    return scores


def head_rows(pair_t):
    row = lax.broadcasted_iota(jnp.int32, pair_t.shape, 0)
    zero = jnp.zeros((), pair_t.dtype)
    return [jnp.where((row // HD) == h, pair_t, zero) for h in range(2)]


def head_cols(pair):
    col = lax.broadcasted_iota(jnp.int32, pair.shape, 1)
    zero = jnp.zeros((), pair.dtype)
    return [jnp.where((col // HD) == h, pair, zero) for h in range(2)]


def for_counts(block, counts, body):
    if len(counts) == 1:
        body(counts[0])
        return
    visible = jnp.minimum(block, 3) + 1
    for count in counts:
        pl.when(visible == count)(functools.partial(body, count))


def attend_kernel(tab, q_t, k, v_t, *refs, counts):
    o_own, o_other, log_total = refs[-3:]
    i = pl.program_id(1)
    block = tab[i]
    first, last = tab[2 + block], tab[10 + block]

    def body(count):
        masks = block_masks(first, last)
        starts = [pl.multiple_of((block - (count - 1) + t) * B, B) for t in range(count)]
        for h, q_head in enumerate(head_rows(q_t[...])):
            scores = [masked(nn(k[pl.ds(s, B), :], q_head), masks, t, count) for t, s in enumerate(starts)]
            peak = functools.reduce(jnp.maximum, [jnp.max(s, axis=0, keepdims=True) for s in scores])
            total, mixed = 0.0, 0.0
            for score, s in zip(scores, starts):
                part = jnp.exp2(score - peak)
                total = total + jnp.sum(part, axis=0, keepdims=True)
                mixed = mixed + nn(v_t[h * HD : (h + 1) * HD, pl.ds(s, B)], part.astype(BF))
            out = (mixed * (1.0 / total)).astype(BF)

            @pl.when(i == 0)
            def _():
                o_own[h * HD : (h + 1) * HD, :] = out

            @pl.when(i == 1)
            def _():
                o_other[h * HD : (h + 1) * HD, :] = out

            log_total[0, h : h + 1, :] = peak + jnp.log2(total)

    for_counts(block, counts, body)


def attend(tab, q_t, k, v_t, half, pairs, old, *deps):
    base, count = pairs
    span = LEN if half else HALF
    one = pl.BlockSpec((128, B), lambda p, i, t: (base + p, 0))
    block = jax.ShapeDtypeStruct((384, B), BF)
    return pl.pallas_call(
        functools.partial(attend_kernel, counts=(4,) if half else (1, 2, 3, 4)),
        grid_spec=pltpu.PrefetchScalarGridSpec(
            num_scalar_prefetch=1,
            grid=(count, 2),
            in_specs=[
                pl.BlockSpec((128, B), lambda p, i, t: (base + p, i)),
                pl.BlockSpec((span, 128), lambda p, i, t: (0, base + p)),
                pl.BlockSpec((128, span), lambda p, i, t: (base + p, 0)),
            ]
            + [ANY] * (len(old) + len(deps)),
            out_specs=[one, one, pl.BlockSpec((1, 2, B), lambda p, i, t: (p, 0, i))],
        ),
        out_shape=[block, block, jax.ShapeDtypeStruct((count, 2, 2 * B), F32)],
        input_output_aliases={4 + n: n for n in range(len(old))},
        compiler_params=pltpu.CompilerParams(vmem_limit_bytes=62 * MIB),
        cost_estimate=cost((8 if half else 6) * count),
    )(tab, q_t, k, v_t, *old, *deps)


def attend_back_kernel(tab, q_t, do_own, do_other, o_own, o_other, log_total, k, v, k_t, *refs, counts, half):
    if half:
        dq_t, high, low, dkv = refs[-4:]
    else:
        start = refs[0]
        dq_t, low, dkv = refs[-3:]
    i = pl.program_id(1)
    block = tab[i]
    first, last = tab[2 + block], tab[10 + block]

    @pl.when(i == 0)
    def _():
        dkv[...] = jnp.zeros_like(dkv) if half else start[0]

    def body(count):
        masks = block_masks(first, last)
        queries, grads = q_t[...], jnp.where(i == 0, do_own[...], do_other[...])
        mixed = jnp.where(i == 0, o_own[...], o_other[...])
        q_rows, g_rows = head_rows(queries), head_rows(grads)
        q_cols, g_cols = head_cols(queries.T), head_cols(grads.T)
        product = grads.astype(F32) * mixed.astype(F32)
        inner = [jnp.sum(product[h * HD : (h + 1) * HD], axis=0, keepdims=True) for h in range(2)]
        dq = [0.0, 0.0]
        for t in range(count):
            rows = pl.ds(pl.multiple_of((block - (count - 1) + t) * B, B), B)
            key_rows, value_rows = k[rows, :], v[rows, :]
            dk_part = dv_part = 0.0
            for h in range(2):
                score = masked(nn(key_rows, q_rows[h]), masks, t, count)
                probs = jnp.exp2(score - log_total[0, h : h + 1, :])
                grad_probs = nn(value_rows, g_rows[h])
                grad_scores = (probs * (grad_probs - inner[h])).astype(BF)
                dv_part = dv_part + nn(probs.astype(BF), g_cols[h])
                dk_part = dk_part + nn(grad_scores, q_cols[h])
                dq[h] = dq[h] + nn(k_t[h * HD : (h + 1) * HD, rows], grad_scores)
            dkv[rows, :128] += dk_part
            dkv[rows, 128:] += dv_part
        for h in range(2):
            dq_t[h * HD : (h + 1) * HD, :] = (dq[h] * SCALE).astype(BF)

    for_counts(block, counts, body)

    @pl.when(i == 1)
    def _():
        target, rows = (high, slice(HALF, LEN)) if half else (low, slice(0, HALF))
        target[0, :, :128] = (dkv[rows, :128] * (1.0 / LOG2E)).astype(BF)
        target[0, :, 128:] = dkv[rows, 128:].astype(BF)
        if half:
            low[0] = dkv[:HALF, :]


def attend_back(tab, q_t, grads, outs, log_total, k, v, k_t, half, pairs, start, *deps):
    base, count = pairs
    one = pl.BlockSpec((128, B), lambda p, i, t: (base + p, 0))
    one_of = pl.BlockSpec((128, B), lambda p, i, t: (base + p, half))
    span = LEN if half else HALF
    query = pl.BlockSpec((128, B), lambda p, i, t: (base + p, i))
    stat = pl.BlockSpec((1, 2, B), lambda p, i, t: (base + p, 0, i))
    major = pl.BlockSpec((span, 128), lambda p, i, t: (0, base + p))
    minor = pl.BlockSpec((128, span), lambda p, i, t: (base + p, 0))
    grad = pl.BlockSpec((1, HALF, 256), lambda p, i, t: (p, 0, 0))
    grad_in = pl.BlockSpec((1, HALF, 256), lambda p, i, t: (base + p, 0, 0))
    return pl.pallas_call(
        functools.partial(attend_back_kernel, counts=(4,) if half else (1, 2, 3, 4), half=half),
        grid_spec=pltpu.PrefetchScalarGridSpec(
            num_scalar_prefetch=1,
            grid=(count, 2),
            in_specs=[query, one_of, one_of, one, one, stat, major, major, minor]
            + [grad_in] * len(start)
            + [ANY] * len(deps),
            out_specs=[pl.BlockSpec((128, B), lambda p, i, t: (p, i)), grad] + [grad] * half,
            scratch_shapes=[pltpu.VMEM((span, 256), F32)],
        ),
        out_shape=[
            jax.ShapeDtypeStruct((count * 128, 2 * B), BF),
            jax.ShapeDtypeStruct((count, HALF, 256), BF),
        ]
        + [jax.ShapeDtypeStruct((count, HALF, 256), F32)] * half,
        compiler_params=pltpu.CompilerParams(vmem_limit_bytes=62 * MIB),
        cost_estimate=cost((16 if half else 12) * count),
    )(tab, q_t, *grads, *outs, log_total, k, v, k_t, *start, *deps)


HEAD_ROWS = ((0, 0, 128), (128, 192, 128), (256, 128, 64), (320, 320, 64))
ROOT = math.sqrt(2.0 / math.pi)


def feed_chunk(up):
    square = up * up
    half = 0.5 + 0.5 * jnp.tanh(up * (ROOT + (ROOT * 0.044715) * square))
    act = (up * half).astype(BF)
    slope = half + (2.0 * up) * (half - half * half) * (ROOT + (3.0 * ROOT * 0.044715) * square)
    return act, slope


def feed_kernel(sel, gain, *refs):
    nears, pairs, crosses = refs[:4], refs[4:8], refs[8:12]
    a_parts, dy_parts, x_parts = refs[12:16], refs[16:19], refs[19:26]
    outs = refs[-28:]
    boths, (ga_own, ga_other, gain_sum) = outs[:4], outs[4:7]
    g_near, g_one, g_rest = outs[7:10]
    outs = outs[2:]
    w_up, w_down, w_out, a_t, dy_t, x_t, n, dy, mid, mlp, gn, stage, stage_out = outs[8:21]
    w_sems, a_sems, in_sems, out_sems, last_sems = outs[21:26]
    core, parity = sel[0], sel[3]

    def start(copies):
        for copy in copies:
            copy.start()

    def wait(copies):
        for copy in copies:
            copy.wait()

    halves = (((0, 768, 0, 0), (768, 896, 1, 0)), ((0, 128, 1, 128), (128, 896, 2, 0)))
    targets = (w_up, w_out, w_down)

    def loads(slot, swapped, kinds):
        count = 0
        copies = []

        def add(source, offset, which_half, rel):
            nonlocal count
            for first, last, which, at in halves[which_half]:
                if which in kinds:
                    rows = slice(rel * FB, (rel + 1) * FB)
                    if which == 1:
                        target = w_out.at[rows, slot * 256 + at : slot * 256 + at + last - first]
                    else:
                        target = targets[which].at[slot, rows, at : at + last - first]
                    copies.append(
                        pltpu.make_async_copy(source.at[:, offset + first : offset + last], target, w_sems.at[slot, count])
                    )
                count += 1

        for half in range(2):
            add(nears[slot], half * 896, half, 0)
            if slot < 2:
                add(pairs[half ^ swapped].at[slot], 0, half, 1)
                add(crosses[0].at[slot], half * 896, half, 2)
                add(crosses[0].at[slot], 1792 + (half ^ swapped) * 896, half, 3)
            else:
                add(pairs[slot], half * 896, half, 1)
                near, pair = (crosses[1].at[0], crosses[1].at[1]) if slot == 2 else crosses[2:]
                add(near, half * 896, half, 2)
                add(pair, half * 896, half, 3)
        return copies

    def a_loads():
        copies = []
        for half in range(2):
            cols = slice(half * B, (half + 1) * B)
            for side in range(2):
                first_row = 512 * (core if side == 0 else 1 - core)
                for source, target, size in HEAD_ROWS:
                    at = pl.multiple_of(first_row + target // FB * 256 + target % FB, 64)
                    copies.append(
                        pltpu.make_async_copy(
                            a_parts[2 * side + half].at[source : source + size, :],
                            a_t.at[pl.ds(at, size), cols],
                            a_sems.at[len(copies)],
                        )
                    )
        return copies

    def token_loads(group):
        copies = []

        def add(source, target):
            copies.append(pltpu.make_async_copy(source, target, in_sems.at[group, len(copies)]))

        for half in range(2):
            cols = slice(half * B, (half + 1) * B)
            place = pl.ds(pl.multiple_of(sel[1 + half] * B, B), B)
            at_whole = pl.ds(pl.multiple_of((sel[1 + half] + 4 * half) * B, B), B)
            if group:
                add(dy_parts[0].at[:, at_whole], dy_t.at[0:FB, cols])
                continue
            add(x_parts[0].at[:, at_whole], x_t.at[0:FB, cols])
            for rel in range(1, 4):
                add(x_parts[half * 3 + rel].at[:, place], x_t.at[rel * FB : (rel + 1) * FB, cols])
        if group:
            add(dy_parts[1].at[0], dy_t.at[FB : 2 * FB, :])
            add(dy_parts[2].at[0], dy_t.at[2 * FB : 3 * FB, :])
            add(dy_parts[2].at[1], dy_t.at[3 * FB :, :])
        return copies

    def stores(slot):
        far = g_one if slot == 1 else g_rest.at[(0, 0, 1, 2)[slot]]
        copies = []
        for side, target in enumerate((g_near.at[slot], far)):
            for which in range(2):
                copies.append(
                    pltpu.make_async_copy(
                        stage.at[slot % 2, which, pl.ds(side * 384, 384), :],
                        target.at[:, which * 1024 : which * 1024 + D],
                        out_sems.at[slot % 2, side * 2 + which],
                    )
                )
        return copies

    def last_stores(slot):
        far = g_one if slot == 1 else g_rest.at[(0, 0, 1, 2)[slot]]
        return [
            pltpu.make_async_copy(
                stage_out.at[pl.ds(side * 384, 384), slot * 256 : (slot + 1) * 256],
                target.at[:, D : D + 256],
                last_sems.at[slot, side],
            )
            for side, target in enumerate((g_near.at[slot], far))
        ]

    start(a_loads())

    def start_weights(kinds):
        for swapped in range(2):

            @pl.when(parity == swapped)
            def _():
                for slot in range(4):
                    start(loads(slot, swapped, kinds))

    start_weights((1,))
    start(token_loads(0))
    for slot in range(4):
        a_t[slot * 256 + FB : (slot + 1) * 256, :] = jnp.zeros((64, a_t.shape[1]), BF)
    wait(a_loads())
    for slot in range(4):
        wait(loads(slot, 0, (1,)))
    wait(token_loads(0))
    start(token_loads(1))
    start_weights((0, 2))
    mid[...] = x_t[...].astype(F32) + nn(w_out[...], a_t[...])
    mlp[...] = mid[...]
    gn[...] = jnp.zeros_like(gn)
    r2 = lax.rsqrt(jnp.sum(mid[...] * mid[...], axis=0, keepdims=True) * (1.0 / D) + EPSILON)
    n_t = x_t
    n_t[...] = (mid[...] * r2 * gain[...]).astype(BF)
    n[...] = n_t[...].T
    wait(token_loads(1))
    dy[...] = dy_t[...].T

    def chunk(slot, carry):
        buffer = lax.rem(slot, 2)
        for before in range(2):

            @pl.when(slot == before + 2)
            def _():
                wait(stores(before))

        for now in range(4):

            @pl.when(slot == now)
            def _():
                wait(loads(now, 0, (0, 2)))

        up = nn(n[...], w_up[slot])
        act, slope = feed_chunk(up)
        stage[buffer, 1] = nn(dy_t[...], act).astype(BF)
        mlp[...] += nt(w_down[slot], act)
        grad_up = (nn(dy[...], w_down[slot]) * slope).astype(BF)
        stage[buffer, 0] = nn(n_t[...], grad_up).astype(BF)
        gn[...] += nt(w_up[slot], grad_up)
        for now in range(4):

            @pl.when(slot == now)
            def _():
                start(stores(now))

        return carry

    lax.fori_loop(0, 4, chunk, 0)
    for rel, both in enumerate(boths):
        both[0] = mlp[rel * FB : (rel + 1) * FB].astype(BF)
    weighted = gn[...] * gain[...]
    inner = jnp.sum(mid[...] * weighted, axis=0, keepdims=True)
    cubed = r2 * r2 * r2 * inner * (1.0 / D)
    gm = (dy_t[...].astype(F32) + r2 * weighted - mid[...] * cubed).astype(BF)
    x_t[...] = gm
    for rel, both in enumerate(boths):
        both[1] = gm[rel * FB : (rel + 1) * FB]
    gain_sum[...] = jnp.sum(gn[...] * mid[...] * r2, axis=1, keepdims=True)
    stage_out[...] = nt(x_t[...], a_t[...]).astype(BF)
    for slot in range(4):
        start(last_stores(slot))
    grad_a = contract(w_out[...], x_t[...], ((0,), (0,))).astype(BF)
    for slot in range(4):

        def place(target):
            for to, source, size in HEAD_ROWS:
                if source // FB == slot % 2:
                    row = slot * 256 + source % FB
                    target[to : to + size, :] = grad_a[row : row + size]

        pl.when((slot // 2) == core)(functools.partial(place, ga_own))
        pl.when((slot // 2) != core)(functools.partial(place, ga_other))
    wait(stores(2))
    wait(stores(3))
    for slot in range(4):
        wait(last_stores(slot))


def feed_forward(sel, gain, nears, pairs, crosses, a_parts, dy_parts, x_parts, *deps):
    count = 2 * B
    vmem = pl.BlockSpec(memory_space=pltpu.VMEM)
    both = jax.ShapeDtypeStruct((2, FB, count), BF)
    heads = jax.ShapeDtypeStruct((384, count), BF)
    inputs = (*nears, *pairs, *crosses, *a_parts, *dy_parts, *x_parts, *deps)
    return pl.pallas_call(
        feed_kernel,
        in_specs=[pl.BlockSpec(memory_space=pltpu.SMEM), vmem] + [ANY] * len(inputs),
        out_specs=[vmem] * 7 + [ANY] * 3,
        out_shape=[both, both, both, both, heads, heads, jax.ShapeDtypeStruct((D, 1), F32)]
        + [jax.ShapeDtypeStruct(shape, BF) for shape in ((4, 384, 1792), (384, 1792), (3, 384, 1792))],
        scratch_shapes=[
            pltpu.VMEM((4, D, D), BF),
            pltpu.VMEM((4, D, D), BF),
            pltpu.VMEM((D, 1024), BF),
            pltpu.VMEM((1024, count), BF),
            pltpu.VMEM((D, count), BF),
            pltpu.VMEM((D, count), BF),
            pltpu.VMEM((count, D), BF),
            pltpu.VMEM((count, D), BF),
            pltpu.VMEM((D, count), F32),
            pltpu.VMEM((D, count), F32),
            pltpu.VMEM((D, count), F32),
            pltpu.VMEM((2, 2, D, D), BF),
            pltpu.VMEM((D, 1024), BF),
            pltpu.SemaphoreType.DMA((4, 16)),
            pltpu.SemaphoreType.DMA((16,)),
            pltpu.SemaphoreType.DMA((2, 8)),
            pltpu.SemaphoreType.DMA((2, 4)),
            pltpu.SemaphoreType.DMA((4, 2)),
        ],
        compiler_params=pltpu.CompilerParams(vmem_limit_bytes=62 * MIB),
        cost_estimate=cost(50),
    )(sel, gain, *inputs)


def qkv_back_kernel(tab, w, n_t, *refs, half):
    dq, dkv, start = refs[:3]
    dq, dkv = [dq[p * 128 : (p + 1) * 128, :] for p in range(3)], [dkv[p] for p in range(3)]
    near, far, gain_out, *grads = refs[-4:] if half else refs[-3:]
    i = pl.program_id(0)
    grad_w = grads[0] if half else None

    @pl.when(i == 0)
    def _():
        gain_out[...] = start[...]
        if half:
            grad_w[...] = jnp.zeros_like(grad_w)

    normed = n_t[...]
    if half:
        for p in range(3):
            grad_w[p, :, 128:] += nn(normed, dkv[p])

    def finish(grad):
        near[:384, :] = grad[:384].astype(BF)
        far[:384, :] = grad[384:].astype(BF)
        product = grad * normed.astype(F32)
        inner = jnp.broadcast_to(jnp.sum(product, axis=0, keepdims=True), (16, B)).astype(BF)
        near[384:, :] = inner
        far[384:, :] = inner
        gain_out[...] += jnp.sum(product, axis=1, keepdims=True)

    def key_part():
        total = 0.0
        for p in range(3):
            total = total + nt(w[:, p * 384 + 128 : (p + 1) * 384], dkv[p])
        return total

    @pl.when(i < 2)
    def _():
        total = key_part()
        for p in range(3):
            total = total + nn(w[:, p * 384 : p * 384 + 128], dq[p])
            if half:
                grad_w[p, :, :128] += nt(normed, dq[p])
        finish(total)

    @pl.when(i >= 2)
    def _():
        finish(key_part())


def project_back(order, w, n_t, dq, dkv, half, start, *deps):
    whole = lambda shape: pl.BlockSpec(shape, lambda i, t: (0,) * len(shape))

    def cols_of(rows):
        return pl.BlockSpec((rows, B), lambda i, t: (0, t[i]))

    def own(rows):
        return pl.BlockSpec((rows, B), lambda i, t: (0, jnp.minimum(i, 1)))

    low = jax.ShapeDtypeStruct((400, HALF), BF)
    specs = [own(384), pl.BlockSpec((3, B, 256), lambda i, t: (0, t[i], 0)), whole((D, 1))]
    return pl.pallas_call(
        functools.partial(qkv_back_kernel, half=half),
        grid_spec=pltpu.PrefetchScalarGridSpec(
            num_scalar_prefetch=1,
            grid=(HALF // B,),
            in_specs=[whole((D, 1152)), cols_of(D)] + specs + [ANY] * len(deps),
            out_specs=[cols_of(400), cols_of(400), whole((D, 1))] + [whole((3, D, 384))] * half,
        ),
        out_shape=[low, low, jax.ShapeDtypeStruct((D, 1), F32)]
        + [jax.ShapeDtypeStruct((3, D, 384), F32)] * half,
        compiler_params=pltpu.CompilerParams(vmem_limit_bytes=62 * MIB),
        cost_estimate=cost(15 if half else 10),
    )(order, w, n_t, dq, dkv, start, *deps)


def weights_kernel(tab, n_t, dq_t, dkv, start, *refs):
    near, far = refs[-2:]
    kv = start[0, :, 128:] + nn(n_t[...], dkv[0])
    q = start[0, :, :128]
    for i in range(2):
        q = q + nt(n_t[:, pl.ds(pl.multiple_of(tab[i] * B, B), B)], dq_t[:, i * B : (i + 1) * B])
    near[0, :, :128] = q[:384].astype(BF)
    far[0, :, :128] = q[384:].astype(BF)
    near[0, :, 128:] = kv[:384].astype(BF)
    far[0, :, 128:] = kv[384:].astype(BF)


def weights_back(order, n_t, dq_t, dkv, start, pairs, *deps):
    base, count = pairs
    each = lambda shape, base: pl.BlockSpec((1, *shape), lambda i, t: (base + i, 0, 0))
    part = jax.ShapeDtypeStruct((count, 384, 384), BF)
    return pl.pallas_call(
        weights_kernel,
        grid_spec=pltpu.PrefetchScalarGridSpec(
            num_scalar_prefetch=1,
            grid=(count,),
            in_specs=[
                pl.BlockSpec((D, HALF), lambda i, t: (0, 0)),
                pl.BlockSpec((128, 2 * B), lambda i, t: (i, 0)),
                each((HALF, 256), 0),
                each((D, 384), base),
            ]
            + [ANY] * len(deps),
            out_specs=[each((384, 384), 0)] * 2,
        ),
        out_shape=[part, part],
        compiler_params=pltpu.CompilerParams(vmem_limit_bytes=62 * MIB),
        cost_estimate=cost(2 + 2 * count),
    )(order, n_t, dq_t, dkv, start, *deps)


def finish_kernel(sel, *refs):
    here, cross, there, there_cross = refs[:4]
    near, core_part, pair_part, near_inner, core_inner, pair_inner, x, scale, gain = refs[4:13]
    out, grad_x = refs[-2:]
    i = pl.program_id(0)
    pair, device = sel[2 + i], sel[6 + i]
    same, own = pair == sel[0], device == sel[1]
    mine = jnp.where(own, here[...], cross[...])
    theirs = jnp.where(own, there[...], there_cross[...])
    both = jnp.where(same, mine, theirs)
    out[...] = both[0]
    total = near[...].astype(F32) + core_part[...].astype(F32) + pair_part[...].astype(F32)
    inner = near_inner[:1].astype(F32) + core_inner[:1].astype(F32) + pair_inner[:1].astype(F32)
    r1 = scale[...]
    grad_x[...] = both[1].astype(F32) + r1 * gain[...] * total - x[...].astype(F32) * (r1 * r1 * inner * (1.0 / D))


def finish_half(sel, here, cross, there, there_cross, near, core_part, pair_part, x, scale, gain, half, old, *deps):
    base = half * (HALF // B)
    piece = pl.BlockSpec((2, FB, B), lambda i, t: (0, 0, half))
    cols = pl.BlockSpec((FB, B), lambda i, t: (0, i))
    into = pl.BlockSpec((FB, B), lambda i, t: (0, base + i))
    row = pl.BlockSpec((1, B), lambda i, t: (0, i))
    inner = lambda first: pl.BlockSpec((16, B), lambda i, t: (first // 16, i))
    return pl.pallas_call(
        finish_kernel,
        grid_spec=pltpu.PrefetchScalarGridSpec(
            num_scalar_prefetch=1,
            grid=(HALF // B,),
            in_specs=[
                piece,
                piece,
                piece,
                piece,
                cols,
                cols,
                cols,
                inner(384),
                inner(384),
                inner(FB),
                into,
                row,
                pl.BlockSpec((FB, 1), lambda i, t: (0, 0)),
            ]
            + [ANY] * (len(old) + len(deps)),
            out_specs=[into, into],
        ),
        out_shape=[jax.ShapeDtypeStruct((FB, LEN), BF), jax.ShapeDtypeStruct((FB, LEN), F32)],
        input_output_aliases={14 + n: n for n in range(len(old))},
        cost_estimate=cost(6),
    )(sel, here, cross, there, there_cross, near, core_part, pair_part, near, core_part, pair_part, x, scale, gain, *old, *deps)


def per_device(
    block_input,
    norm_gain_one,
    w_query,
    w_key,
    w_value,
    w_out,
    norm_gain_two,
    w_up,
    w_down,
    piece_start,
    piece_len,
    grad_y,
):
    c = lax.axis_index("cols")
    r = lax.axis_index("rows")
    y, core = c // 2, c % 2
    parity = lax.axis_index("dp") % 2

    def order_of(table):
        return jnp.array(table, jnp.int32)[c]

    low_order = order_of([[0, 3, 1, 2], [3, 0, 1, 2], [1, 2, 0, 3], [2, 1, 0, 3]])
    high_order = order_of([[0, 1, 2, 3], [1, 0, 2, 3], [2, 3, 0, 1], [3, 2, 0, 1]])
    away = order_of([[3, 5, 1, 6, 2, 7], [0, 4, 2, 7, 1, 6], [2, 7, 0, 4, 3, 5], [1, 6, 3, 5, 0, 4]])

    small = jnp.concatenate(
        [norm_gain_one, norm_gain_two, piece_start[0].astype(F32), piece_len[0].astype(F32)]
    )
    small = jnp.stack([small, cols_swap(small, 2)])
    small = jnp.concatenate([small, cols_swap(small, 1)])
    gain_one = small[:, :FB].reshape(D, 1)
    gain_two = small[:, FB : 2 * FB].reshape(D, 1)
    apart = jnp.bitwise_xor(c, r)
    mine = jnp.where(apart == 0, 0, jnp.where(apart == 2, 1, jnp.where(apart == 1, 2, 3)))
    pieces = lax.dynamic_index_in_dim(small, mine, 0, keepdims=False)[2 * FB :].astype(jnp.int32)
    firsts = pieces[:8] - jnp.arange(8, dtype=jnp.int32) * B
    lasts = firsts + pieces[8:]

    def table(order, half):
        blocks = order[:2] + half * 4
        return jnp.concatenate([blocks, firsts, lasts])

    low_table, high_table = table(low_order, 0), table(high_order, 1)
    low_order = jnp.concatenate([low_order, core[None].astype(jnp.int32)])
    high_order = jnp.concatenate([high_order, core[None].astype(jnp.int32)])

    own_low, own_high = block_input[:, :HALF], block_input[:, HALF:]
    w_slots = [pack(w_query, w_key, w_value)]
    w_slots += [rows_shift(w_slots[0], step) for step in (1, 2, 3)]

    def merge(first, second):
        parts = [first[:, :384], second[:, :384]]
        for n in range(3):
            cols = slice(384 + n * HD, 384 + (n + 1) * HD)
            parts += [first[:, cols], second[:, cols]]
        return jnp.concatenate(parts, axis=1)

    w_near = jnp.stack([merge(*w_slots[:2]), merge(*w_slots[2:])])
    pair_low = tie(cols_swap(own_low, 2), w_near)
    x_low = (pair_low, cols_swap(tie(own_low, w_near), 1), cols_swap(pair_low, 1))
    own_pack = jnp.concatenate([w_up, w_out.T, jnp.zeros((FB, 64), BF), w_down], axis=1)
    dy_core = hold(away[:2], grad_y, B)
    dy_away = hold(away[2:], grad_y, B)
    ring = [tie(own_pack, w_near)]
    ring.append(rows_shift(ring[0], 1))
    cross_high = cols_swap(own_high, 1)
    w_pair = tie(cols_swap(w_near, 2), x_low[1], x_low[2], dy_core, dy_away, ring[1])
    w_cross = cols_swap(pick(1 - core, w_near, w_pair), 1)
    pair_high = cols_swap(tie(own_high, w_pair), 2)

    normed_low, scale_low, q_low, *kv, w_qkv = project_half(
        low_order, (block_input, *x_low), gain_one, (w_near, w_pair, w_cross), 0, (), ()
    )
    ring.append(rows_shift(ring[1], 1))
    first_sent = jnp.stack(ring[:2])
    first_sent = tie(jnp.where(parity == 0, first_sent[:, :, :896], first_sent[:, :, 896:]), scale_low)
    *out_low, log_first = attend(low_table, q_low, kv[0], kv[3], 0, (0, 1), (), first_sent)
    first_pairs = cols_swap(first_sent, 2)
    ring[2] = tie(ring[2], log_first)
    ring.append(rows_shift(ring[2], 1))
    pair_high = tie(pair_high, log_first)
    *out_low, log_low = attend(low_table, q_low, kv[0], kv[3], 0, (1, 2), out_low, log_first, pair_high, ring[2])
    x_high = (pair_high, cross_high, cols_swap(pair_high, 1))
    low_got = cols_swap(out_low[1], 1)
    dy_sent, third_sent = tie(dy_away, log_low), tie(ring[2], log_low)
    ring[2] = third_sent
    normed_high, scale_high, q_high, *kv = project_half(
        high_order, (block_input, *x_high), gain_one, (w_qkv,), 1, tuple(kv), (log_low, first_pairs)
    )
    k, k_t, v, v_t = kv
    first_crossed = dp_swap(first_pairs)
    dy_pair = cols_swap(dy_sent, 2)
    third_pair = cols_swap(third_sent, 2)
    *out_high, log_other = attend(high_table, q_high, k, v_t, 1, (0, 1), (), low_got)
    ring[3] = tie(ring[3], log_other)
    dy_pair, third_pair = tie(dy_pair, log_other), tie(third_pair, log_other)
    first_crossed = tie(first_crossed, log_other)
    dy_cross_sent = jnp.concatenate([dy_core, dy_pair[1:]])
    third_cross_sent = jnp.stack([ring[2], third_pair])
    *out_high, log_high = attend(
        high_table, q_high, k, v_t, 1, (1, 2), out_high, log_other, ring[3], dy_cross_sent, third_cross_sent
    )
    dy_cross = cols_swap(dy_cross_sent, 1)
    third_cross = cols_swap(third_cross_sent, 1)
    first_cross = cols_swap(jnp.concatenate([jnp.stack(ring[:2]), first_pairs, first_crossed], axis=2), 1)
    last_cross = cols_swap(ring[3], 1)
    last_pair = tie(cols_swap(ring[3], 2), log_high)
    last_cross = (last_cross, cols_swap(last_pair, 1))
    high_got = cols_swap(out_high[1], 1)
    log_low, log_high = jnp.concatenate([log_first, log_low]), jnp.concatenate([log_other, log_high])

    sel = jnp.stack([core.astype(jnp.int32), low_order[0], high_order[0], parity.astype(jnp.int32)])
    *boths, ga_own, ga_other, gain_two_sum, g_near, g_one, g_rest = feed_forward(
        sel,
        gain_two,
        ring,
        (first_pairs, first_crossed, third_pair, last_pair),
        (first_cross, third_cross, *last_cross),
        (out_low[0], out_high[0], low_got, high_got),
        (grad_y, dy_pair, dy_cross),
        (block_input, *x_low, *x_high),
    )

    def three(first, second, third):
        return (first.astype(F32) + second.astype(F32) + third.astype(F32)).astype(BF)

    def two(first, second):
        return (first.astype(F32) + second.astype(F32)).astype(BF)

    ga_got = cols_swap(ga_other, 1)
    total = two(g_near[1], cols_swap(g_one, 1))
    crosses = [cols_swap(both, 1) for both in boths[2:]]
    g_got = cols_swap(g_rest, 1)
    grads = (ga_own, ga_got)
    dq_high, dkv_high, dkv_low = attend_back(
        high_table, q_high, grads, out_high, log_high, k, v, k_t, 1, (0, 3), (), total, *crosses
    )
    theres = [cols_swap(boths[1], 2), cols_swap(crosses[1], 2)]
    total = three(tie(rows_shift(total, 1), dq_high), g_near[2], g_got[1])
    near_high, far_high, gain_part, w_part = project_back(
        high_order, w_qkv, normed_high, dq_high, dkv_high, 1, jnp.zeros((D, 1), F32), total, *theres
    )
    got_high = cols_swap(far_high, 1)
    dq_low, dkv_low = attend_back(
        low_table, q_low, grads, out_low, log_low, k, v, k_t, 0, (0, 3), (dkv_low,), near_high
    )
    total = three(tie(rows_shift(total, 1), dq_low), g_near[3], g_got[2])
    got_high = tie(got_high, dq_low, total)
    sent_high = two(near_high[FB:], got_high[FB:])
    pair_sent = cols_swap(sent_high, 2)
    wg_near, wg_far = weights_back(low_order, normed_low, dq_low, dkv_low, w_part, (0, 3), sent_high, total)
    near_low, far_low, gain_part = project_back(
        low_order, w_qkv, normed_low, dq_low, dkv_low, 0, gain_part, wg_near
    )

    ring_got = tie(rows_shift(total, 1), near_low)
    wg_got = tie(cols_swap(wg_far, 1), near_low, ring_got, pair_sent)
    by_core = jnp.where(core == 0, wg_near, wg_got), jnp.where(core == 0, wg_got, wg_near)

    def split(values):
        high = lax.reduce_precision(values, 8, 7)
        middle = lax.reduce_precision(values - high, 8, 7)
        parts = [high, middle, values - high - middle, jnp.zeros((values.shape[0], 58), F32)]
        return jnp.concatenate(parts, axis=1).astype(BF)

    def unsplit(columns):
        columns = columns[:, 576:582].astype(F32)
        return columns[:, :2] + columns[:, 2:4] + columns[:, 4:]

    gains = jnp.concatenate([gain_part / gain_one, gain_two_sum], axis=1).T
    gains = split((gains[:, :384] + cols_swap(gains[:, 384:], 1)).T)

    def slot_of(slot):
        part = by_core[slot // 2]
        which = slot % 2
        last = [part[2, :, n * 128 + which * HD : n * 128 + (which + 1) * HD] for n in range(3)]
        return jnp.concatenate([part[which]] + last + [gains], axis=1)

    slots = [slot_of(slot) for slot in range(4)]
    got_low = tie(cols_swap(far_low, 1), wg_near)
    sent_low = two(near_low[FB:], got_low[FB:])
    total = three(ring_got, g_near[0], g_got[0])

    def dp_sum(part, *deps):
        if lax.axis_size("dp") == 2:
            got = dp_swap(part)
            got = tie(got, *deps) if deps else got
            return part.astype(F32) + got.astype(F32)
        return lax.psum(part.astype(F32), "dp")

    pair_got = cols_swap(sent_low, 2)
    feed_sum = two(total[:FB], cols_swap(total[FB:], 2))
    parts = [slots[0]] + [rows_shift(slots[slot], -slot) for slot in (1, 2, 3)]
    parts[1] = tie(parts[1], pair_got, total)
    joined = sum(part[:, :576].astype(F32) for part in parts).astype(BF)
    shares = [unsplit(part) for part in parts]

    def share_of(row):
        slot = jnp.mod(r - row, 4)
        last = jnp.where(slot == 2, shares[2], shares[3])
        return jnp.where(slot == 0, shares[0], jnp.where(slot == 1, shares[1], last))

    shares = [share_of(row) for row in range(4)]
    gains = (shares[0] + shares[1]) + (shares[2] + shares[3])
    joined_sent = jnp.concatenate([joined[FB:], split(gains[FB:])], axis=1)
    joined_got = cols_swap(joined_sent, 2)
    joined_pair = jnp.concatenate(
        [two(joined[:FB], joined_got[:, :576]), split(gains[:FB] + unsplit(joined_got))], axis=1
    )

    where = jnp.stack([y, core]).astype(jnp.int32)
    low_sel = jnp.concatenate([where, jnp.array([0, 1, 1, 0, 0, 0, 1, 1], jnp.int32)])
    high_sel = jnp.concatenate([where, jnp.array([0, 0, 1, 1, 0, 1, 0, 1], jnp.int32)])
    gain_column = norm_gain_one.reshape(FB, 1)
    outputs = finish_half(
        high_sel, boths[0], crosses[0], *theres, near_high, got_high, pair_sent, block_input, scale_high,
        gain_column, 1, (), joined_sent,
    )
    output, grad_x = finish_half(
        low_sel, boths[0], crosses[0], *theres, near_low, got_low, pair_got, block_input, scale_low,
        gain_column, 0, tuple(outputs), joined_pair, feed_sum,
    )

    joined = dp_sum(joined_pair)
    gains = unsplit(joined)
    feed_total = dp_sum(feed_sum, grad_x)

    def joined_grad(n):
        return jnp.concatenate(
            [joined[:, n * 128 : (n + 1) * 128], joined[:, 384 + n * HD : 384 + (n + 1) * HD]], axis=1
        )

    return (
        output,
        grad_x,
        gains[:, 0],
        joined_grad(0),
        joined_grad(1),
        joined_grad(2),
        feed_total[:, D : D + FB].T,
        gains[:, 1],
        feed_total[:, :D],
        feed_total[:, D + 256 :],
    )


def solution(mesh):
    return jax.shard_map(
        per_device,
        mesh=mesh,
        in_specs=(
            P("cols", ("dp", "rows")),
            P("cols"),
            P("cols", "rows"),
            P("cols", "rows"),
            P("cols", "rows"),
            P("rows", "cols"),
            P("cols"),
            P("cols", "rows"),
            P("cols", "rows"),
            P(("dp", "cols"), None),
            P(("dp", "cols"), None),
            P("cols", ("dp", "rows")),
        ),
        out_specs=(
            P("cols", ("dp", "rows")),
            P("cols", ("dp", "rows")),
            P("cols"),
            P("cols", "rows"),
            P("cols", "rows"),
            P("cols", "rows"),
            P("rows", "cols"),
            P("cols"),
            P("cols", "rows"),
            P("cols", "rows"),
        ),
        check_vma=False,
    )
```
